32 devices in a mesh: group: 4 (over y, core), member: 8 (over z, x).
Axes of the slice: x: 2, y: 2, z: 4, core: 2. Of those that a mesh axis runs over, the one named last changes fastest.
Arguments:
- fine_blocks: float32 [512, 5, 128, 128], P(('group', 'member')), may hold values from -6 to 6
- neighbours: int32 [512, 5], P(('group', 'member')), may hold values from 0 to 511, as said below
- slot_one: int32 [512, 5], P(('group', 'member')), may hold values from 0 to 4
- pair_one: int32 [512], P(('group', 'member')), may hold values from 0 to 255, as said below
- prolong_one: float32 [128, 128], replicated, may hold values from -0.5 to 0.5
- slot_two: int32 [256, 5], P(('group', 'member')), may hold values from 0 to 4
- pair_two: int32 [256], P(('group', 'member')), may hold values from 0 to 127, as said below
- prolong_two: float32 [128, 128], replicated, may hold values from -0.5 to 0.5
- diag_inverse: float32 [512, 128, 128], P(('group', 'member')), may hold values from -0.01953125 to 0.01953125
- right_side: float32 [512, 128], P(('group', 'member')), may hold values from -96 to 96
- initial_guess: float32 [512, 128], P(('group', 'member')), may hold values from -6 to 6
Outputs:
- coarse_one: float32 [256, 5, 128, 128], P(('group', 'member'))
- coarse_two: float32 [128, 5, 128, 128], P(('group', 'member'))
- smoothed: float32 [512, 128], P(('group', 'member'))
The draws below stay inside these ranges and needn't reach their ends.
Inputs may be any that keep to these rules, and one draw needn't show every extreme that they name: Entry 0 of a row is the row's own element; the other four are its neighbours on a periodic grid and lie in the rows of the same device or of the devices just before and just after it in group-major order, cyclically. `pair_one`: every first-level coarse row is named by exactly two fine elements. A fine element names a coarse row held by a device of its own group; the rows of one device name at most 4 rows held by any one device, and some device names exactly 4 rows of some device. `pair_two`: every second-level coarse row is named by exactly two first-level rows. A first-level row names a row held by a device with the same member index; the rows of one device name at most 4 rows held by any one device, and some device names exactly 4 rows of some device.
All inputs are finite; a program needn't handle non-finite values.
Results may differ from the reference program's by a relative error of at most 0.0001.
Values sent between devices are 32-bit elements; how exact they have to be, the bound alone decides.
No kernel may reach another device: no remote copies, remote signals or barrier semaphores. Data moves between devices by JAX's collectives and lax.ppermute only.
A program may use at most 128 MiB of HBM per device.

```python
import jax
import jax.numpy as jnp
from jax import lax

BLOCK = 128
LINKS = 5
ROWS = 16
ELEMS = 512
CAP_ONE = 4
CAP_TWO = 4
N_GROUP = 4
N_MEMBER = 8


def route_table(base_key, cycle_count, peer_count, row_count, capacity):
    slot_total = peer_count * capacity

    def one_cycle(cycle_key):
        sub_keys = jax.random.split(cycle_key, 6)
        forced = jax.random.randint(sub_keys[0], (), 0, peer_count)
        slot_order = jax.random.permutation(sub_keys[1], slot_total).astype(jnp.int32)
        slot_ids = jnp.arange(slot_total, dtype=jnp.int32)
        slot_score = slot_order + jnp.where(slot_ids // capacity == forced, 0, slot_total).astype(jnp.int32)
        chosen = jnp.sort(jnp.argsort(slot_score)[:row_count].astype(jnp.int32))
        shifts = chosen // capacity
        sigma_map = jax.random.permutation(sub_keys[2], peer_count).astype(jnp.int32)
        rho_map = jax.random.permutation(sub_keys[3], peer_count).astype(jnp.int32)
        positions = jax.vmap(lambda sub_key: jax.random.permutation(sub_key, row_count))(jax.random.split(sub_keys[4], peer_count)).astype(jnp.int32)
        pairing = jax.vmap(lambda sub_key: jax.random.permutation(sub_key, row_count))(jax.random.split(sub_keys[5], peer_count)).astype(jnp.int32)
        target = sigma_map[(rho_map[:, None] + shifts[positions]) % peer_count]
        coarse_local = pairing[target, positions] // 2
        return (target, coarse_local)
    return jax.vmap(one_cycle)(jax.random.split(base_key, cycle_count))


def draw_pair_one(key, part):
    target, coarse_local = route_table(jax.random.fold_in(key, 11), N_GROUP, N_MEMBER, ROWS, CAP_ONE)
    group_ids = jnp.arange(N_GROUP, dtype=jnp.int32)[:, None, None]
    owner_dev = group_ids * N_MEMBER + target
    coarse_ids = owner_dev * (ROWS // 2) + coarse_local
    return coarse_ids.reshape(-1).astype(jnp.int32)


def draw_pair_two(key, part):
    target, coarse_local = route_table(jax.random.fold_in(key, 22), N_MEMBER, N_GROUP, ROWS // 2, CAP_TWO)
    member_ids = jnp.arange(N_MEMBER, dtype=jnp.int32)[:, None, None]
    owner_dev = target * N_MEMBER + member_ids
    coarse_ids = owner_dev * (ROWS // 4) + coarse_local
    return jnp.transpose(coarse_ids, (1, 0, 2)).reshape(-1).astype(jnp.int32)


def draw_neighbours(key, part):
    device_count = ELEMS // ROWS
    sub_keys = jax.random.split(jax.random.fold_in(key, 33), device_count)
    grid_place = jax.vmap(lambda sub_key: jax.random.permutation(sub_key, ROWS))(sub_keys).astype(jnp.int32)
    inverse = jnp.argsort(grid_place, axis=1).astype(jnp.int32)
    dev_row = jnp.arange(device_count, dtype=jnp.int32)[:, None]

    def element_id(dev_ids, grid_col):
        return dev_ids * ROWS + inverse[dev_ids, grid_col]
    own_ids = dev_row * ROWS + jnp.arange(ROWS, dtype=jnp.int32)[None, :]
    west_ids = element_id(dev_row, (grid_place - 1) % ROWS)
    east_ids = element_id(dev_row, (grid_place + 1) % ROWS)
    north_ids = element_id(jnp.broadcast_to((dev_row + 1) % device_count, grid_place.shape), grid_place)
    south_ids = element_id(jnp.broadcast_to((dev_row - 1) % device_count, grid_place.shape), grid_place)
    stacked = jnp.stack([own_ids, west_ids, east_ids, north_ids, south_ids], axis=-1)
    return stacked.reshape(ELEMS, 5).astype(jnp.int32)


def place_ends(values, key, least, largest):
    shape = values.shape
    spot = [jax.random.randint(jax.random.fold_in(key, axis), (), 0, shape[axis]) for axis in range(len(shape))]
    values = values.at[tuple(spot)].set(least)
    longest = shape.index(max(shape))
    spot[longest] = (spot[longest] + 1) % shape[longest]
    return values.at[tuple(spot)].set(largest)


def block_scale(own_key, shape, cuts, low, largest):
    level = 1.0
    for position, shards_of in cuts:
        heights = jax.random.uniform(jax.random.fold_in(jax.random.fold_in(own_key, 6), position), (shards_of,), jnp.float32, low / len(cuts), largest / len(cuts))
        level = level * jnp.repeat(jnp.exp(heights), shape[position] // shards_of).reshape((-1,) + (1,) * (len(shape) - 1 - position))
    return level


def scatter_about(own_key, shape, deviation, most, shards=(), kind=jnp.bfloat16):
    result = jax.random.normal(own_key, shape, jnp.float32) * deviation
    if len(shards) > 0:
        result = block_scale(own_key, shape, shards, -0.22, 0.18) * result
    return jnp.clip(result, min=-most, max=most).astype(kind)


def setup_inputs(seed: int = 0) -> dict:
    key_list = jax.random.split(jax.random.key(seed), 12)
    return {
        "fine_blocks": scatter_about(key_list[0], (ELEMS, LINKS, BLOCK, BLOCK), 1.0, 6.0, ((0, 32),), jnp.float32),
        "neighbours": draw_neighbours(jax.random.fold_in(key_list[11], 71), 0),
        "slot_one": place_ends(jax.random.randint(key_list[2], (ELEMS, LINKS), 0, LINKS), jax.random.fold_in(key_list[2], 1), 0, LINKS - 1).astype(jnp.int32),
        "pair_one": draw_pair_one(jax.random.fold_in(key_list[11], 71), 0),
        "prolong_one": scatter_about(key_list[4], (BLOCK, BLOCK), BLOCK ** -0.5, 0.5, (), jnp.float32),
        "slot_two": place_ends(jax.random.randint(key_list[5], (ELEMS // 2, LINKS), 0, LINKS), jax.random.fold_in(key_list[5], 1), 0, LINKS - 1).astype(jnp.int32),
        "pair_two": draw_pair_two(jax.random.fold_in(key_list[11], 71), 0),
        "prolong_two": scatter_about(key_list[7], (BLOCK, BLOCK), BLOCK ** -0.5, 0.5, (), jnp.float32),
        "diag_inverse": scatter_about(key_list[8], (ELEMS, BLOCK, BLOCK), (LINKS * BLOCK * BLOCK) ** -0.5, 0.01953125, ((0, 32),), jnp.float32),
        "right_side": scatter_about(key_list[9], (ELEMS, BLOCK), 16.0, 96.0, ((0, 32),), jnp.float32),
        "initial_guess": scatter_about(key_list[10], (ELEMS, BLOCK), 1.0, 6.0, ((0, 32),), jnp.float32),
    }


damping = 0.7


def triple(blocks, prolong):
    block_shape = blocks.shape
    flat_rows = blocks.reshape(-1, block_shape[-1])
    right_part = jnp.dot(flat_rows, prolong, precision=lax.Precision.HIGHEST)
    right_part = right_part.reshape(-1, block_shape[-2], block_shape[-1])
    left_side = jnp.einsum('ua,kub->kab', prolong, right_part, precision=lax.Precision.HIGHEST)
    return left_side.reshape(block_shape)


def galerkin(blocks, slot_map, pair_map, prolong, coarse_count):
    summed = jnp.zeros((coarse_count * LINKS, BLOCK, BLOCK), jnp.float32)
    for link_index in range(LINKS):
        seg_ids = (pair_map * LINKS + slot_map[:, link_index]).astype(jnp.int32)
        summed = summed + jax.ops.segment_sum(blocks[:, link_index], seg_ids, num_segments=coarse_count * LINKS)
    return triple(summed, prolong).reshape(coarse_count, LINKS, BLOCK, BLOCK)


def reference(fine_blocks, neighbours, slot_one, pair_one, prolong_one, slot_two, pair_two, prolong_two, diag_inverse, right_side, initial_guess):
    elem_count = fine_blocks.shape[0]
    coarse_one = galerkin(fine_blocks, slot_one, pair_one, prolong_one, elem_count // 2)
    coarse_two = galerkin(coarse_one, slot_two, pair_two, prolong_two, elem_count // 4)
    nearby = initial_guess[neighbours]
    product = jnp.einsum('ekuv,ekv->eu', fine_blocks, nearby, precision=lax.Precision.HIGHEST)
    defect = right_side - product
    smoothed = initial_guess + damping * jnp.einsum('euv,ev->eu', diag_inverse, defect, precision=lax.Precision.HIGHEST)
    return coarse_one, coarse_two, smoothed
```

```python
import functools

import jax
import jax.numpy as jnp
from jax import lax
from jax.experimental import pallas as pl
from jax.experimental.pallas import tpu as pltpu
from jax.sharding import PartitionSpec as P

damping = 0.7
chunk_goal = 4
vmem_limit = 48 * 1024 * 1024


def grid_of(member_count):
    x_count = max(d for d in range(1, member_count + 1) if member_count % d == 0 and d * d <= member_count)
    return member_count // x_count, x_count


def split(values):
    high = values.astype(jnp.bfloat16)
    low = (values - high.astype(jnp.float32)).astype(jnp.bfloat16)
    return high, low


def load_weights(prolong_ref, left_ref, right_ref):
    prolong = prolong_ref[...]
    size = prolong.shape[0]
    high, low = split(prolong)
    high_t, low_t = split(prolong.T)
    for half in range(2):
        at = pl.ds(half * size, size)
        left_ref[0:size, at] = high_t
        left_ref[size : 2 * size, at] = low_t
        right_ref[at, 0:size] = high
        right_ref[at, size : 2 * size] = low


def triple(blocks, left_ref, right_ref):
    size = blocks[0].shape[0]
    count = len(blocks)
    high, low = split(jnp.concatenate(blocks, axis=1))
    both = jnp.dot(
        left_ref[...], jnp.concatenate([high, low], axis=0), preferred_element_type=jnp.float32
    )
    left = both[:size] + both[size:]
    rows = jnp.concatenate([left[:, s * size : (s + 1) * size] for s in range(count)], axis=0)
    high, low = split(rows)
    both = jnp.dot(
        jnp.concatenate([high, low], axis=1), right_ref[...], preferred_element_type=jnp.float32
    )
    return (both[:, :size] + both[:, size:]).reshape(count, size, size)


def prepare_kernel(x_count, chunks, slot_ref, place_ref, prolong_ref, fine_ref, *rest):
    outs, (left_ref, right_ref, sums_ref, done_ref) = rest[:-4], rest[-4:]
    row = pl.program_id(0)
    links, size = fine_ref.shape[1], fine_ref.shape[2]
    part = size // x_count
    step = part // chunks

    @pl.when(row == 0)
    def _():
        load_weights(prolong_ref, left_ref, right_ref)

    sums_ref[...] = jnp.zeros_like(sums_ref)
    for link in range(links):
        slot = slot_ref[row, link]
        sums_ref[slot] += fine_ref[0, link]
    done_ref[...] = triple([sums_ref[s] for s in range(links)], left_ref, right_ref)
    for offset in range(x_count):
        start = lax.rem(place_ref[0] + offset, x_count) * part
        for chunk in range(chunks):
            at = pl.multiple_of(start + chunk * step, step)
            outs[offset * chunks + chunk][0] = done_ref[:, pl.ds(at, step), :]


def prepare(fine_blocks, slot_one, prolong_one, place, x_count, chunks):
    rows, links, size, _ = fine_blocks.shape
    step = size // x_count // chunks
    out = jax.ShapeDtypeStruct((rows, links, step, size), jnp.float32)
    outs = pl.pallas_call(
        functools.partial(prepare_kernel, x_count, chunks),
        out_shape=[out] * (x_count * chunks),
        grid_spec=pltpu.PrefetchScalarGridSpec(
            num_scalar_prefetch=2,
            grid=(rows,),
            in_specs=[
                pl.BlockSpec((size, size), lambda e, *_: (0, 0)),
                pl.BlockSpec((1, links, size, size), lambda e, *_: (e, 0, 0, 0)),
            ],
            out_specs=[pl.BlockSpec((1, links, step, size), lambda e, *_: (e, 0, 0, 0))]
            * (x_count * chunks),
            scratch_shapes=[
                pltpu.VMEM((2 * size, 2 * size), jnp.bfloat16),
                pltpu.VMEM((2 * size, 2 * size), jnp.bfloat16),
                pltpu.VMEM((links, size, size), jnp.float32),
                pltpu.VMEM((links, size, size), jnp.float32),
            ],
        ),
        compiler_params=pltpu.CompilerParams(vmem_limit_bytes=vmem_limit),
        cost_estimate=pl.CostEstimate(
            flops=16 * rows * links * size**3,
            bytes_accessed=8 * rows * links * size**2,
            transcendentals=0,
        ),
        name="prepare",
    )(slot_one, place, prolong_one, fine_blocks)
    return [outs[offset * chunks : (offset + 1) * chunks] for offset in range(x_count)]


def whole(kernel, scalars, arrays, out_shapes, name):
    held = sum(a.size for a in arrays) + sum(o.size for o in out_shapes)
    return pl.pallas_call(
        kernel,
        out_shape=out_shapes,
        in_specs=[pl.BlockSpec(memory_space=pltpu.SMEM)] * len(scalars)
        + [pl.BlockSpec(memory_space=pltpu.VMEM)] * len(arrays),
        out_specs=[pl.BlockSpec(memory_space=pltpu.VMEM)] * len(out_shapes),
        compiler_params=pltpu.CompilerParams(vmem_limit_bytes=vmem_limit),
        cost_estimate=pl.CostEstimate(flops=held, bytes_accessed=4 * held, transcendentals=0),
        name=name,
    )(*scalars, *arrays)


def combine_kernel(sources, target_ref, *refs):
    arrays, (far_ref, near_ref) = refs[:sources], refs[sources:]
    rows = arrays[0].shape[0]
    half = far_ref.shape[0]
    far_ref[...] = jnp.zeros_like(far_ref)
    near_ref[...] = jnp.zeros_like(near_ref)
    for source in range(sources):

        def one(row, carry, source=source):
            target = target_ref[source * rows + row]

            @pl.when(target < half)
            def _():
                far_ref[target] += arrays[source][row]

            @pl.when(target >= half)
            def _():
                near_ref[target - half] += arrays[source][row]

            return carry

        lax.fori_loop(0, rows, one, 0)


def finish_kernel(near_ref, got_ref, *outs):
    rows = outs[0].shape[0]
    for index, out in enumerate(outs):
        at = pl.ds(index * rows, rows)
        out[...] = near_ref[at] + got_ref[at]


def second_kernel(counts, slot_ref, target_ref, middle_ref, *refs):
    arrays, outs = refs[: sum(counts) + 1], refs[sum(counts) + 1 :]
    parts, buffer_ref = outs[:-1], outs[-1]
    rows, links, step, _ = parts[0].shape
    position = 1
    for offset, count in enumerate(counts):
        total = None
        for piece in arrays[position : position + count]:
            total = piece[...] if total is None else total + piece[...]
        position += count
        if offset == 0:
            own = jnp.where(middle_ref[0] > 0, arrays[0][...], 0.0)
            total = own if total is None else own + total
        parts[offset][...] = total
    buffer_ref[...] = jnp.zeros_like(buffer_ref)

    def one(row, carry):
        target = target_ref[row]
        for link in range(links):
            slot = slot_ref[row, link]
            for offset, part in enumerate(parts):
                buffer_ref[target, slot, offset * step : (offset + 1) * step, :] += part[row, link]
        return carry

    lax.fori_loop(0, rows, one, 0)


def place_kernel(x_count, chunks, place_ref, *refs):
    pieces, out = refs[:-1], refs[-1]
    part = out.shape[2] // x_count
    step = part // chunks
    for offset in range(x_count):
        start = lax.rem(place_ref[0] + x_count - offset, x_count) * part
        for chunk in range(chunks):
            at = pl.multiple_of(start + chunk * step, step)
            out[:, :, pl.ds(at, step), :] = pieces[offset * chunks + chunk][...]


def place_one(pieces, place, x_count, chunks):
    rows, links, step, size = pieces[0].shape
    return pl.pallas_call(
        functools.partial(place_kernel, x_count, chunks),
        out_shape=jax.ShapeDtypeStruct((rows, links, size, size), jnp.float32),
        grid_spec=pltpu.PrefetchScalarGridSpec(
            num_scalar_prefetch=1,
            grid=(rows,),
            in_specs=[pl.BlockSpec((1, links, step, size), lambda e, *_: (e, 0, 0, 0))] * len(pieces),
            out_specs=pl.BlockSpec((1, links, size, size), lambda e, *_: (e, 0, 0, 0)),
        ),
        compiler_params=pltpu.CompilerParams(vmem_limit_bytes=vmem_limit),
        cost_estimate=pl.CostEstimate(
            flops=0, bytes_accessed=8 * rows * links * size**2, transcendentals=0
        ),
        name="place_one",
    )(place, *pieces)


def last_kernel(x_count, chunks, place_ref, prolong_ref, *refs):
    pieces, (out, left_ref, right_ref, sums_ref) = refs[:-4], refs[-4:]
    links, size = out.shape[1], out.shape[2]
    part = size // x_count
    step = part // chunks

    @pl.when(pl.program_id(0) == 0)
    def _():
        load_weights(prolong_ref, left_ref, right_ref)

    for chunk, piece in enumerate(pieces):
        total = piece[0, 0]
        for peer in range(1, piece.shape[0]):
            total = total + piece[peer, 0]
        for offset in range(x_count):
            start = lax.rem(place_ref[0] + x_count - offset, x_count) * part
            at = pl.multiple_of(start + chunk * step, step)
            sums_ref[:, pl.ds(at, step), :] = total[:, offset * step : (offset + 1) * step, :]
    out[0] = triple([sums_ref[s] for s in range(links)], left_ref, right_ref)


def last(pieces, prolong_two, place, x_count, chunks):
    peers, rows, links, step, size = pieces[0].shape
    return pl.pallas_call(
        functools.partial(last_kernel, x_count, chunks),
        out_shape=jax.ShapeDtypeStruct((rows, links, size, size), jnp.float32),
        grid_spec=pltpu.PrefetchScalarGridSpec(
            num_scalar_prefetch=1,
            grid=(rows,),
            in_specs=[pl.BlockSpec((size, size), lambda e, *_: (0, 0))]
            + [pl.BlockSpec((peers, 1, links, step, size), lambda e, *_: (0, e, 0, 0, 0))]
            * len(pieces),
            out_specs=pl.BlockSpec((1, links, size, size), lambda e, *_: (e, 0, 0, 0)),
            scratch_shapes=[
                pltpu.VMEM((2 * size, 2 * size), jnp.bfloat16),
                pltpu.VMEM((2 * size, 2 * size), jnp.bfloat16),
                pltpu.VMEM((links, size, size), jnp.float32),
            ],
        ),
        compiler_params=pltpu.CompilerParams(vmem_limit_bytes=vmem_limit),
        cost_estimate=pl.CostEstimate(
            flops=16 * rows * links * size**3,
            bytes_accessed=4 * rows * links * size**2 * (peers + 1),
            transcendentals=0,
        ),
        name="last",
    )(place, prolong_two, *pieces)


def sweep(fine_blocks, neighbours, diag_inverse, right_side, initial_guess):
    rows = fine_blocks.shape[0]
    axes = ("group", "member")
    devices = lax.axis_size(axes)
    device = lax.axis_index(axes)
    before = lax.ppermute(initial_guess, axes, [(i, (i + 1) % devices) for i in range(devices)])
    after = lax.ppermute(initial_guess, axes, [(i, (i - 1) % devices) for i in range(devices)])
    window = jnp.concatenate([before, initial_guess, after], axis=0)
    position = (neighbours - device * rows + rows) % (rows * devices)
    nearby = window[position]
    product = jnp.sum(fine_blocks * nearby[:, :, None, :], axis=(1, 3))
    defect = right_side - product
    return initial_guess + damping * jnp.sum(diag_inverse * defect[:, None, :], axis=2)


def local(
    fine_blocks,
    neighbours,
    slot_one,
    pair_one,
    prolong_one,
    slot_two,
    pair_two,
    prolong_two,
    diag_inverse,
    right_side,
    initial_guess,
):
    rows, links, size, _ = fine_blocks.shape
    rows_one, rows_two = rows // 2, rows // 4
    members, groups = lax.axis_size("member"), lax.axis_size("group")
    z_count, x_count = grid_of(members)
    half = z_count // 2
    part = size // x_count
    chunks = max(c for c in range(1, chunk_goal + 1) if part % (8 * c) == 0)
    step = part // chunks

    member = lax.axis_index("member")
    z, x = member // x_count, member % x_count
    upper = (z >= half).astype(jnp.int32)
    place = jnp.stack([x]).astype(jnp.int32)

    def at(side, d, x_at):
        return (half + d if side else half - 1 - d) * x_count + x_at % x_count

    def hop(array, d_from, d_to, offset):
        pairs = [
            (at(side, d_from, x_at), at(side, d_to, x_at + offset))
            for side in range(2)
            for x_at in range(x_count)
        ]
        return lax.ppermute(array, "member", pairs)

    routes = [(d, o) for d in range(half) for o in range(x_count)]

    pairs_all = lax.all_gather(pair_one, "member", tiled=True).reshape(members, rows)
    owner = pairs_all // rows_one % members
    owner_z, owner_x = owner // x_count, owner % x_count
    owner_upper = (owner_z >= half).astype(jnp.int32)
    owner_d = jnp.where(owner_upper > 0, owner_z - half, half - 1 - owner_z)
    near = (owner_upper == upper).astype(jnp.int32)
    target_all = ((near * half + owner_d) * x_count + (owner_x - x) % x_count) * rows_one
    target_all = target_all + pairs_all % rows_one
    sources = jnp.stack(
        [jnp.where(upper > 0, half + d, half - 1 - d) * x_count + (x - o) % x_count for d, o in routes]
    )
    target_one = target_all[sources].reshape(-1).astype(jnp.int32)
    middle = jnp.stack([(z == half - 1) | (z == half)]).astype(jnp.int32)

    owner_two = pair_two // rows_two
    target_two = (owner_two // members * rows_two + pair_two % rows_two).astype(jnp.int32)

    outgoing = prepare(fine_blocks, slot_one, prolong_one, place, x_count, chunks)
    across = [(at(0, 0, x_at), at(1, 0, x_at)) for x_at in range(x_count)]
    across = across + [(b, a) for a, b in across]
    sums = jax.ShapeDtypeStruct((half * x_count * rows_one, links, step, size), jnp.float32)
    piece = jax.ShapeDtypeStruct((rows_one, links, step, size), jnp.float32)
    buffer = jax.ShapeDtypeStruct((groups * rows_two, links, x_count * step, size), jnp.float32)
    parts, received = [], []
    for chunk in range(chunks):
        held = [
            outgoing[0][chunk] if (d, o) == (0, 0) else hop(outgoing[o][chunk], d, 0, o)
            for d, o in routes
        ]
        far, kept = whole(
            functools.partial(combine_kernel, len(held)), [target_one], held, [sums, sums], "combine"
        )
        got = lax.ppermute(far, "member", across)
        finished = whole(finish_kernel, [], [kept, got], [piece] * len(routes), "finish")
        arrived = [[] for _ in range(x_count)]
        for (d, o), ready in zip(routes, finished):
            if (d, o) != (0, 0):
                arrived[o].append(hop(ready, 0, d, o))
        made = whole(
            functools.partial(second_kernel, [len(a) for a in arrived]),
            [slot_two, target_two, middle],
            [finished[0]] + [a for pieces in arrived for a in pieces],
            [piece] * x_count + [buffer],
            "second",
        )
        parts.append(made[:-1])
        sent = lax.all_to_all(made[-1], "group", split_axis=0, concat_axis=0, tiled=True)
        received.append(sent.reshape((groups, rows_two) + sent.shape[1:]))

    coarse_one = place_one(
        [parts[chunk][o] for o in range(x_count) for chunk in range(chunks)], place, x_count, chunks
    )
    coarse_two = last(received, prolong_two, place, x_count, chunks)
    smoothed = sweep(fine_blocks, neighbours, diag_inverse, right_side, initial_guess)
    return (coarse_one, coarse_two, smoothed)


def solution(mesh):
    rows = P(("group", "member"))
    return jax.shard_map(
        local,
        mesh=mesh,
        in_specs=(rows, rows, rows, rows, P(), rows, rows, P(), rows, rows, rows),
        out_specs=(rows, rows, rows),
        check_vma=False,
    )
```

```python
import functools

import jax
import jax.numpy as jnp
from jax import lax
from jax.experimental import pallas as pl
from jax.experimental.pallas import tpu as pltpu
from jax.sharding import PartitionSpec as P

damping = 0.7
chunk_goal = 4
vmem_limit = 48 * 1024 * 1024


def split(values):
    high = values.astype(jnp.bfloat16)
    low = (values - high.astype(jnp.float32)).astype(jnp.bfloat16)
    return high, low


def load_weights(prolong_ref, left_ref, right_ref):
    prolong = prolong_ref[...]
    size = prolong.shape[0]
    high, low = split(prolong)
    high_t, low_t = split(prolong.T)
    for half in range(2):
        at = pl.ds(half * size, size)
        left_ref[0:size, at] = high_t
        left_ref[size : 2 * size, at] = low_t
        right_ref[at, 0:size] = high
        right_ref[at, size : 2 * size] = low


def triple(blocks, left_ref, right_ref):
    size = blocks[0].shape[0]
    count = len(blocks)
    high, low = split(jnp.concatenate(blocks, axis=1))
    both = jnp.dot(
        left_ref[...], jnp.concatenate([high, low], axis=0), preferred_element_type=jnp.float32
    )
    left = both[:size] + both[size:]
    rows = jnp.concatenate([left[:, s * size : (s + 1) * size] for s in range(count)], axis=0)
    high, low = split(rows)
    both = jnp.dot(
        jnp.concatenate([high, low], axis=1), right_ref[...], preferred_element_type=jnp.float32
    )
    return (both[:, :size] + both[:, size:]).reshape(count, size, size)


def prepare_kernel(slot_ref, prolong_ref, fine_ref, *rest):
    outs, (left_ref, right_ref, sums_ref, done_ref) = rest[:-4], rest[-4:]
    row = pl.program_id(0)
    links, size = fine_ref.shape[1], fine_ref.shape[2]
    parts, step = outs[0].shape[0], outs[0].shape[3]

    @pl.when(row == 0)
    def _():
        load_weights(prolong_ref, left_ref, right_ref)

    sums_ref[...] = jnp.zeros_like(sums_ref)
    for link in range(links):
        slot = slot_ref[row, link]
        sums_ref[slot] += fine_ref[0, link]
    done_ref[...] = triple([sums_ref[s] for s in range(links)], left_ref, right_ref)
    for part in range(parts):
        for chunk, out in enumerate(outs):
            start = part * (size // parts) + chunk * step
            out[part, 0] = done_ref[:, start : start + step, :]


def prepare(fine_blocks, slot_one, prolong_one, parts, chunks):
    rows, links, size, _ = fine_blocks.shape
    step = size // parts // chunks
    return pl.pallas_call(
        prepare_kernel,
        out_shape=[jax.ShapeDtypeStruct((parts, rows, links, step, size), jnp.float32)] * chunks,
        grid_spec=pltpu.PrefetchScalarGridSpec(
            num_scalar_prefetch=1,
            grid=(rows,),
            in_specs=[
                pl.BlockSpec((size, size), lambda e, *_: (0, 0)),
                pl.BlockSpec((1, links, size, size), lambda e, *_: (e, 0, 0, 0)),
            ],
            out_specs=[
                pl.BlockSpec((parts, 1, links, step, size), lambda e, *_: (0, e, 0, 0, 0))
            ]
            * chunks,
            scratch_shapes=[
                pltpu.VMEM((2 * size, 2 * size), jnp.bfloat16),
                pltpu.VMEM((2 * size, 2 * size), jnp.bfloat16),
                pltpu.VMEM((links, size, size), jnp.float32),
                pltpu.VMEM((links, size, size), jnp.float32),
            ],
        ),
        compiler_params=pltpu.CompilerParams(vmem_limit_bytes=vmem_limit),
        cost_estimate=pl.CostEstimate(
            flops=16 * rows * links * size**3,
            bytes_accessed=8 * rows * links * size**2,
            transcendentals=0,
        ),
        name="prepare",
    )(slot_one, prolong_one, fine_blocks)


def whole(kernel, scalars, arrays, out_shapes, name):
    held = sum(a.size for a in arrays) + sum(o.size for o in out_shapes)
    return pl.pallas_call(
        kernel,
        out_shape=out_shapes,
        in_specs=[pl.BlockSpec(memory_space=pltpu.SMEM)] * len(scalars)
        + [pl.BlockSpec(memory_space=pltpu.VMEM)] * len(arrays),
        out_specs=[pl.BlockSpec(memory_space=pltpu.VMEM)] * len(out_shapes),
        compiler_params=pltpu.CompilerParams(vmem_limit_bytes=vmem_limit),
        cost_estimate=pl.CostEstimate(flops=held, bytes_accessed=4 * held, transcendentals=0),
        name=name,
    )(*scalars, *arrays)


def combine_kernel(target_ref, held_ref, out_ref):
    out_ref[...] = jnp.zeros_like(out_ref)
    for source in range(held_ref.shape[0]):

        def one(row, carry, source=source):
            out_ref[target_ref[source, row]] += held_ref[source, row]
            return carry

        lax.fori_loop(0, held_ref.shape[1], one, 0, unroll=4)


def second_kernel(slot_ref, target_ref, got_ref, *outs):
    pieces, buffer_ref = outs[:-1], outs[-1]
    parts = len(pieces)
    rows, links, step, _ = pieces[0].shape
    for part, piece in enumerate(pieces):
        total = got_ref[part]
        for index in range(part + parts, got_ref.shape[0], parts):
            total = total + got_ref[index]
        piece[...] = total
    buffer_ref[...] = jnp.zeros_like(buffer_ref)

    def one(row, carry):
        target = target_ref[row]
        for link in range(links):
            slot = slot_ref[row, link]
            for part, piece in enumerate(pieces):
                buffer_ref[target, slot, part * step : (part + 1) * step, :] += piece[row, link]
        return carry

    lax.fori_loop(0, rows, one, 0)


def place_kernel(parts, chunks, *refs):
    pieces, out = refs[:-1], refs[-1]
    step = pieces[0].shape[2]
    for part in range(parts):
        for chunk in range(chunks):
            start = (part * chunks + chunk) * step
            out[:, :, start : start + step, :] = pieces[part * chunks + chunk][...]


def place_one(pieces, parts, chunks):
    rows, links, step, size = pieces[0].shape
    return pl.pallas_call(
        functools.partial(place_kernel, parts, chunks),
        out_shape=jax.ShapeDtypeStruct((rows, links, size, size), jnp.float32),
        grid=(rows,),
        in_specs=[pl.BlockSpec((1, links, step, size), lambda e: (e, 0, 0, 0))] * len(pieces),
        out_specs=pl.BlockSpec((1, links, size, size), lambda e: (e, 0, 0, 0)),
        compiler_params=pltpu.CompilerParams(vmem_limit_bytes=vmem_limit),
        cost_estimate=pl.CostEstimate(
            flops=0, bytes_accessed=8 * rows * links * size**2, transcendentals=0
        ),
        name="place_one",
    )(*pieces)


def last_kernel(parts, prolong_ref, *refs):
    pieces, (out, left_ref, right_ref, sums_ref) = refs[:-4], refs[-4:]
    links, size = out.shape[1], out.shape[2]
    step = size // parts // len(pieces)

    @pl.when(pl.program_id(0) == 0)
    def _():
        load_weights(prolong_ref, left_ref, right_ref)

    for chunk, piece in enumerate(pieces):
        total = piece[0, 0]
        for peer in range(1, piece.shape[0]):
            total = total + piece[peer, 0]
        for part in range(parts):
            start = (part * len(pieces) + chunk) * step
            sums_ref[:, start : start + step, :] = total[:, part * step : (part + 1) * step, :]
    out[0] = triple([sums_ref[s] for s in range(links)], left_ref, right_ref)


def last(pieces, prolong_two, parts):
    peers, rows, links, step, size = pieces[0].shape
    return pl.pallas_call(
        functools.partial(last_kernel, parts),
        out_shape=jax.ShapeDtypeStruct((rows, links, size, size), jnp.float32),
        grid=(rows,),
        in_specs=[pl.BlockSpec((size, size), lambda e: (0, 0))]
        + [pl.BlockSpec((peers, 1, links, step, size), lambda e: (0, e, 0, 0, 0))] * len(pieces),
        out_specs=pl.BlockSpec((1, links, size, size), lambda e: (e, 0, 0, 0)),
        scratch_shapes=[
            pltpu.VMEM((2 * size, 2 * size), jnp.bfloat16),
            pltpu.VMEM((2 * size, 2 * size), jnp.bfloat16),
            pltpu.VMEM((links, size, size), jnp.float32),
        ],
        compiler_params=pltpu.CompilerParams(vmem_limit_bytes=vmem_limit),
        cost_estimate=pl.CostEstimate(
            flops=16 * rows * links * size**3,
            bytes_accessed=4 * rows * links * size**2 * (peers + 1),
            transcendentals=0,
        ),
        name="last",
    )(prolong_two, *pieces)


def sweep(fine_blocks, neighbours, diag_inverse, right_side, initial_guess):
    rows = fine_blocks.shape[0]
    axes = ("group", "member")
    devices = lax.axis_size(axes)
    device = lax.axis_index(axes)
    before = lax.ppermute(initial_guess, axes, [(i, (i + 1) % devices) for i in range(devices)])
    after = lax.ppermute(initial_guess, axes, [(i, (i - 1) % devices) for i in range(devices)])
    window = jnp.concatenate([before, initial_guess, after], axis=0)
    position = (neighbours - device * rows + rows) % (rows * devices)
    nearby = window[position]
    product = jnp.sum(fine_blocks * nearby[:, :, None, :], axis=(1, 3))
    defect = right_side - product
    return initial_guess + damping * jnp.sum(diag_inverse * defect[:, None, :], axis=2)


def local(
    fine_blocks,
    neighbours,
    slot_one,
    pair_one,
    prolong_one,
    slot_two,
    pair_two,
    prolong_two,
    diag_inverse,
    right_side,
    initial_guess,
):
    rows, links, size, _ = fine_blocks.shape
    rows_one, rows_two = rows // 2, rows // 4
    members, groups = lax.axis_size("member"), lax.axis_size("group")
    parts = max(members // 2, 1)
    chunks = max(c for c in range(1, chunk_goal + 1) if size // parts % (8 * c) == 0)
    step = size // parts // chunks
    halves = [list(range(first, first + parts)) for first in range(0, members, parts)]

    def within(array):
        return lax.all_to_all(array, "member", 0, 0, axis_index_groups=halves, tiled=True)

    target_own = (pair_one % (members * rows_one)).astype(jnp.int32)
    target_one = within(jnp.broadcast_to(target_own, (parts, rows)))
    target_two = pair_two // rows_two // members * rows_two + pair_two % rows_two
    target_two = target_two.astype(jnp.int32)

    outgoing = prepare(fine_blocks, slot_one, prolong_one, parts, chunks)
    sums = jax.ShapeDtypeStruct((members * rows_one, links, step, size), jnp.float32)
    piece = jax.ShapeDtypeStruct((rows_one, links, step, size), jnp.float32)
    buffer = jax.ShapeDtypeStruct((groups * rows_two, links, parts * step, size), jnp.float32)
    pieces, received = [], []
    for chunk in range(chunks):
        held = within(outgoing[chunk])
        (combined,) = whole(combine_kernel, [target_one], [held], [sums], "combine")
        got = lax.all_to_all(combined, "member", 0, 0, tiled=True)
        got = got.reshape((members, rows_one) + got.shape[1:])
        made = whole(second_kernel, [slot_two, target_two], [got], [piece] * parts + [buffer], "second")
        pieces.append(made[:-1])
        sent = lax.all_to_all(made[-1], "group", 0, 0, tiled=True)
        received.append(sent.reshape((groups, rows_two) + sent.shape[1:]))

    coarse_one = place_one(
        [pieces[chunk][part] for part in range(parts) for chunk in range(chunks)], parts, chunks
    )
    coarse_two = last(received, prolong_two, parts)
    smoothed = sweep(fine_blocks, neighbours, diag_inverse, right_side, initial_guess)
    return (coarse_one, coarse_two, smoothed)


def solution(mesh):
    rows = P(("group", "member"))
    return jax.shard_map(
        local,
        mesh=mesh,
        in_specs=(rows, rows, rows, rows, P(), rows, rows, P(), rows, rows, rows),
        out_specs=(rows, rows, rows),
        check_vma=False,
    )
```

```python
import functools

import jax
import jax.numpy as jnp
from jax import lax
from jax.experimental import pallas as pl
from jax.experimental.pallas import tpu as pltpu
from jax.sharding import PartitionSpec as P

damping = 0.7
chunk_goal = 4
vmem_limit = 48 * 1024 * 1024


def grid_of(member_count):
    x_count = max(d for d in range(1, member_count + 1) if member_count % d == 0 and d * d <= member_count)
    return member_count // x_count, x_count


def split(values):
    high = values.astype(jnp.bfloat16)
    low = (values - high.astype(jnp.float32)).astype(jnp.bfloat16)
    return high, low


def load_weights(prolong_ref, left_ref, right_ref):
    prolong = prolong_ref[...]
    size = prolong.shape[0]
    high, low = split(prolong)
    high_t, low_t = split(prolong.T)
    for half in range(2):
        at = pl.ds(half * size, size)
        left_ref[0:size, at] = high_t
        left_ref[size : 2 * size, at] = low_t
        right_ref[at, 0:size] = high
        right_ref[at, size : 2 * size] = low


def triple(blocks, left_ref, right_ref):
    size = blocks[0].shape[0]
    count = len(blocks)
    high, low = split(jnp.concatenate(blocks, axis=1))
    both = jnp.dot(
        left_ref[...], jnp.concatenate([high, low], axis=0), preferred_element_type=jnp.float32
    )
    left = both[:size] + both[size:]
    rows = jnp.concatenate([left[:, s * size : (s + 1) * size] for s in range(count)], axis=0)
    high, low = split(rows)
    both = jnp.dot(
        jnp.concatenate([high, low], axis=1), right_ref[...], preferred_element_type=jnp.float32
    )
    return (both[:, :size] + both[:, size:]).reshape(count, size, size)


def prepare_kernel(x_count, chunks, slot_ref, place_ref, prolong_ref, fine_ref, *rest):
    outs, (left_ref, right_ref, sums_ref, done_ref) = rest[:-4], rest[-4:]
    row = pl.program_id(0)
    links, size = fine_ref.shape[1], fine_ref.shape[2]
    part = size // x_count
    step = part // chunks

    @pl.when(row == 0)
    def _():
        load_weights(prolong_ref, left_ref, right_ref)

    sums_ref[...] = jnp.zeros_like(sums_ref)
    for link in range(links):
        slot = slot_ref[row, link]
        sums_ref[slot] += fine_ref[0, link]
    done_ref[...] = triple([sums_ref[s] for s in range(links)], left_ref, right_ref)
    for offset in range(x_count):
        start = lax.rem(place_ref[0] + offset, x_count) * part
        for chunk in range(chunks):
            at = pl.multiple_of(start + chunk * step, step)
            outs[offset * chunks + chunk][0] = done_ref[:, pl.ds(at, step), :]


def prepare(fine_blocks, slot_one, prolong_one, place, x_count, chunks):
    rows, links, size, _ = fine_blocks.shape
    step = size // x_count // chunks
    out = jax.ShapeDtypeStruct((rows, links, step, size), jnp.float32)
    outs = pl.pallas_call(
        functools.partial(prepare_kernel, x_count, chunks),
        out_shape=[out] * (x_count * chunks),
        grid_spec=pltpu.PrefetchScalarGridSpec(
            num_scalar_prefetch=2,
            grid=(rows,),
            in_specs=[
                pl.BlockSpec((size, size), lambda e, *_: (0, 0)),
                pl.BlockSpec((1, links, size, size), lambda e, *_: (e, 0, 0, 0)),
            ],
            out_specs=[pl.BlockSpec((1, links, step, size), lambda e, *_: (e, 0, 0, 0))]
            * (x_count * chunks),
            scratch_shapes=[
                pltpu.VMEM((2 * size, 2 * size), jnp.bfloat16),
                pltpu.VMEM((2 * size, 2 * size), jnp.bfloat16),
                pltpu.VMEM((links, size, size), jnp.float32),
                pltpu.VMEM((links, size, size), jnp.float32),
            ],
        ),
        compiler_params=pltpu.CompilerParams(vmem_limit_bytes=vmem_limit),
        cost_estimate=pl.CostEstimate(
            flops=16 * rows * links * size**3,
            bytes_accessed=8 * rows * links * size**2,
            transcendentals=0,
        ),
        name="prepare",
    )(slot_one, place, prolong_one, fine_blocks)
    return [outs[offset * chunks : (offset + 1) * chunks] for offset in range(x_count)]


def whole(kernel, scalars, arrays, out_shapes, name):
    return pl.pallas_call(
        kernel,
        out_shape=out_shapes,
        in_specs=[pl.BlockSpec(memory_space=pltpu.SMEM)] * len(scalars)
        + [pl.BlockSpec(memory_space=pltpu.VMEM)] * len(arrays),
        out_specs=[pl.BlockSpec(memory_space=pltpu.VMEM)] * len(out_shapes),
        compiler_params=pltpu.CompilerParams(vmem_limit_bytes=vmem_limit),
        cost_estimate=pl.CostEstimate(flops=0, bytes_accessed=0, transcendentals=0),
        name=name,
    )(*scalars, *arrays)


def combine_kernel(sources, target_ref, *refs):
    arrays, (far_ref, sums_ref) = refs[:sources], refs[sources:]
    rows = arrays[0].shape[0]
    sums_ref[...] = jnp.zeros_like(sums_ref)
    for source in range(sources):

        def one(row, carry, source=source):
            sums_ref[target_ref[source, row]] += arrays[source][row]
            return carry

        lax.fori_loop(0, rows, one, 0, unroll=4)
    far_ref[...] = sums_ref[0 : far_ref.shape[0]]


def finish_kernel(sums_ref, got_ref, *outs):
    rows, half = outs[0].shape[0], got_ref.shape[0]
    for index, out in enumerate(outs):
        at = index * rows
        out[...] = sums_ref[half + at : half + at + rows] + got_ref[at : at + rows]


def second_kernel(counts, slot_ref, target_ref, middle_ref, *refs):
    arrays, outs = refs[: sum(counts) + 1], refs[sum(counts) + 1 :]
    parts, buffer_ref = outs[:-1], outs[-1]
    rows, links, step, _ = parts[0].shape
    position = 1
    for offset, count in enumerate(counts):
        total = None
        for piece in arrays[position : position + count]:
            total = piece[...] if total is None else total + piece[...]
        position += count
        if offset == 0:
            own = jnp.where(middle_ref[0] > 0, arrays[0][...], 0.0)
            total = own if total is None else own + total
        parts[offset][...] = total
    buffer_ref[...] = jnp.zeros_like(buffer_ref)

    def one(row, carry):
        target = target_ref[row]
        for link in range(links):
            slot = slot_ref[row, link]
            for offset, part in enumerate(parts):
                buffer_ref[target, slot, offset * step : (offset + 1) * step, :] += part[row, link]
        return carry

    lax.fori_loop(0, rows, one, 0)


def place_kernel(x_count, chunks, place_ref, *refs):
    pieces, out = refs[:-1], refs[-1]
    part = out.shape[2] // x_count
    step = part // chunks
    for offset in range(x_count):
        start = lax.rem(place_ref[0] + x_count - offset, x_count) * part
        for chunk in range(chunks):
            at = pl.multiple_of(start + chunk * step, step)
            out[:, :, pl.ds(at, step), :] = pieces[offset * chunks + chunk][...]


def place_one(pieces, place, x_count, chunks):
    rows, links, step, size = pieces[0].shape
    return pl.pallas_call(
        functools.partial(place_kernel, x_count, chunks),
        out_shape=jax.ShapeDtypeStruct((rows, links, size, size), jnp.float32),
        grid_spec=pltpu.PrefetchScalarGridSpec(
            num_scalar_prefetch=1,
            grid=(rows,),
            in_specs=[pl.BlockSpec((1, links, step, size), lambda e, *_: (e, 0, 0, 0))] * len(pieces),
            out_specs=pl.BlockSpec((1, links, size, size), lambda e, *_: (e, 0, 0, 0)),
        ),
        compiler_params=pltpu.CompilerParams(vmem_limit_bytes=vmem_limit),
        cost_estimate=pl.CostEstimate(
            flops=0, bytes_accessed=8 * rows * links * size**2, transcendentals=0
        ),
        name="place_one",
    )(place, *pieces)


def last_kernel(x_count, chunks, place_ref, prolong_ref, *refs):
    pieces, (out, left_ref, right_ref, sums_ref) = refs[:-4], refs[-4:]
    links, size = out.shape[1], out.shape[2]
    part = size // x_count
    step = part // chunks

    @pl.when(pl.program_id(0) == 0)
    def _():
        load_weights(prolong_ref, left_ref, right_ref)

    for chunk, piece in enumerate(pieces):
        total = piece[0, 0]
        for peer in range(1, piece.shape[0]):
            total = total + piece[peer, 0]
        for offset in range(x_count):
            start = lax.rem(place_ref[0] + x_count - offset, x_count) * part
            at = pl.multiple_of(start + chunk * step, step)
            sums_ref[:, pl.ds(at, step), :] = total[:, offset * step : (offset + 1) * step, :]
    out[0] = triple([sums_ref[s] for s in range(links)], left_ref, right_ref)


def last(pieces, prolong_two, place, x_count, chunks):
    peers, rows, links, step, size = pieces[0].shape
    return pl.pallas_call(
        functools.partial(last_kernel, x_count, chunks),
        out_shape=jax.ShapeDtypeStruct((rows, links, size, size), jnp.float32),
        grid_spec=pltpu.PrefetchScalarGridSpec(
            num_scalar_prefetch=1,
            grid=(rows,),
            in_specs=[pl.BlockSpec((size, size), lambda e, *_: (0, 0))]
            + [pl.BlockSpec((peers, 1, links, step, size), lambda e, *_: (0, e, 0, 0, 0))]
            * len(pieces),
            out_specs=pl.BlockSpec((1, links, size, size), lambda e, *_: (e, 0, 0, 0)),
            scratch_shapes=[
                pltpu.VMEM((2 * size, 2 * size), jnp.bfloat16),
                pltpu.VMEM((2 * size, 2 * size), jnp.bfloat16),
                pltpu.VMEM((links, size, size), jnp.float32),
            ],
        ),
        compiler_params=pltpu.CompilerParams(vmem_limit_bytes=vmem_limit),
        cost_estimate=pl.CostEstimate(
            flops=16 * rows * links * size**3,
            bytes_accessed=4 * rows * links * size**2 * (peers + 1),
            transcendentals=0,
        ),
        name="last",
    )(place, prolong_two, *pieces)


def sweep(fine_blocks, neighbours, diag_inverse, right_side, initial_guess):
    rows = fine_blocks.shape[0]
    axes = ("group", "member")
    devices = lax.axis_size(axes)
    device = lax.axis_index(axes)
    before = lax.ppermute(initial_guess, axes, [(i, (i + 1) % devices) for i in range(devices)])
    after = lax.ppermute(initial_guess, axes, [(i, (i - 1) % devices) for i in range(devices)])
    window = jnp.concatenate([before, initial_guess, after], axis=0)
    position = (neighbours - device * rows + rows) % (rows * devices)
    nearby = window[position]
    product = jnp.sum(fine_blocks * nearby[:, :, None, :], axis=(1, 3))
    defect = right_side - product
    return initial_guess + damping * jnp.sum(diag_inverse * defect[:, None, :], axis=2)


def local(
    fine_blocks,
    neighbours,
    slot_one,
    pair_one,
    prolong_one,
    slot_two,
    pair_two,
    prolong_two,
    diag_inverse,
    right_side,
    initial_guess,
):
    rows, links, size, _ = fine_blocks.shape
    rows_one, rows_two = rows // 2, rows // 4
    members, groups = lax.axis_size("member"), lax.axis_size("group")
    z_count, x_count = grid_of(members)
    half = z_count // 2
    part = size // x_count
    chunks = max(c for c in range(1, chunk_goal + 1) if part % (8 * c) == 0)
    step = part // chunks

    member = lax.axis_index("member")
    z, x = member // x_count, member % x_count
    upper = (z >= half).astype(jnp.int32)
    place = jnp.stack([x]).astype(jnp.int32)

    def at(side, d, x_at):
        return (half + d if side else half - 1 - d) * x_count + x_at % x_count

    def hop(array, d_from, d_to, offset):
        pairs = [
            (at(side, d_from, x_at), at(side, d_to, x_at + offset))
            for side in range(2)
            for x_at in range(x_count)
        ]
        return lax.ppermute(array, "member", pairs)

    routes = [(d, o) for d in range(half) for o in range(x_count)]

    def gather_routes(arrays):
        return [
            arrays[o] if (d, o) == (0, 0) else hop(arrays[o], d, 0, o) for d, o in routes
        ]

    owner_rows = jnp.stack(gather_routes([pair_one] * x_count))
    owner = owner_rows // rows_one % members
    owner_z, owner_x = owner // x_count, owner % x_count
    owner_upper = (owner_z >= half).astype(jnp.int32)
    owner_d = jnp.where(owner_upper > 0, owner_z - half, half - 1 - owner_z)
    near = (owner_upper == upper).astype(jnp.int32)
    target_one = ((near * half + owner_d) * x_count + (owner_x - x + x_count) % x_count) * rows_one
    target_one = (target_one + owner_rows % rows_one).astype(jnp.int32)
    middle = jnp.stack([(z == half - 1) | (z == half)]).astype(jnp.int32)

    owner_two = pair_two // rows_two
    target_two = (owner_two // members * rows_two + pair_two % rows_two).astype(jnp.int32)

    outgoing = prepare(fine_blocks, slot_one, prolong_one, place, x_count, chunks)
    across = [(at(0, 0, x_at), at(1, 0, x_at)) for x_at in range(x_count)]
    across = across + [(b, a) for a, b in across]
    sums = jax.ShapeDtypeStruct((half * x_count * rows_one, links, step, size), jnp.float32)
    piece = jax.ShapeDtypeStruct((rows_one, links, step, size), jnp.float32)
    buffer = jax.ShapeDtypeStruct((groups * rows_two, links, x_count * step, size), jnp.float32)
    everything = jax.ShapeDtypeStruct((2 * sums.shape[0],) + sums.shape[1:], jnp.float32)
    parts, received, fars = [], [], []
    for chunk in range(chunks):
        sending = [outgoing[o][chunk] for o in range(x_count)]
        if chunk >= 2:
            sending, fars[chunk - 2] = lax.optimization_barrier((sending, fars[chunk - 2]))
        held = gather_routes(sending)
        far, kept = whole(
            functools.partial(combine_kernel, len(held)),
            [target_one],
            held,
            [sums, everything],
            "combine",
        )
        fars.append(far)
        parts.append((held, kept))
    crossing = [lax.ppermute(far, "member", across) for far in fars]
    made_parts = []
    for chunk in range(chunks):
        got, kept = crossing[chunk], parts[chunk][1]
        finished = whole(finish_kernel, [], [kept, got], [piece] * len(routes), "finish")
        arrived = [[] for _ in range(x_count)]
        for (d, o), ready in zip(routes, finished):
            if (d, o) != (0, 0):
                arrived[o].append(hop(ready, 0, d, o))
        made = whole(
            functools.partial(second_kernel, [len(a) for a in arrived]),
            [slot_two, target_two, middle],
            [finished[0]] + [a for pieces in arrived for a in pieces],
            [piece] * x_count + [buffer],
            "second",
        )
        made_parts.append(made[:-1])
        sent = lax.all_to_all(made[-1], "group", split_axis=0, concat_axis=0, tiled=True)
        received.append(sent.reshape((groups, rows_two) + sent.shape[1:]))
    parts = made_parts

    coarse_one = place_one(
        [parts[chunk][o] for o in range(x_count) for chunk in range(chunks)], place, x_count, chunks
    )
    coarse_two = last(received, prolong_two, place, x_count, chunks)
    smoothed = sweep(fine_blocks, neighbours, diag_inverse, right_side, initial_guess)
    return (coarse_one, coarse_two, smoothed)


def solution(mesh):
    rows = P(("group", "member"))
    return jax.shard_map(
        local,
        mesh=mesh,
        in_specs=(rows, rows, rows, rows, P(), rows, rows, P(), rows, rows, rows),
        out_specs=(rows, rows, rows),
        check_vma=False,
    )
```

```python
import functools

import jax
import jax.numpy as jnp
from jax import lax
from jax.experimental import pallas as pl
from jax.experimental.pallas import tpu as pltpu
from jax.sharding import PartitionSpec as P

damping = 0.7
chunk_goal = 4
vmem_limit = 48 * 1024 * 1024
beside = 64 * 1024 * 1024


def grid_of(member_count):
    x_count = max(d for d in range(1, member_count + 1) if member_count % d == 0 and d * d <= member_count)
    return member_count // x_count, x_count


def split(values):
    high = values.astype(jnp.bfloat16)
    low = (values - high.astype(jnp.float32)).astype(jnp.bfloat16)
    return high, low


def load_weights(prolong_ref, left_ref, right_ref):
    prolong = prolong_ref[...]
    size = prolong.shape[0]
    high, low = split(prolong)
    high_t, low_t = split(prolong.T)
    for half in range(2):
        at = pl.ds(half * size, size)
        left_ref[0:size, at] = high_t
        left_ref[size : 2 * size, at] = low_t
        right_ref[at, 0:size] = high
        right_ref[at, size : 2 * size] = low


def triple(blocks, left_ref, right_ref):
    size = blocks[0].shape[0]
    count = len(blocks)
    high, low = split(jnp.concatenate(blocks, axis=1))
    both = jnp.dot(
        left_ref[...], jnp.concatenate([high, low], axis=0), preferred_element_type=jnp.float32
    )
    left = both[:size] + both[size:]
    rows = jnp.concatenate([left[:, s * size : (s + 1) * size] for s in range(count)], axis=0)
    high, low = split(rows)
    both = jnp.dot(
        jnp.concatenate([high, low], axis=1), right_ref[...], preferred_element_type=jnp.float32
    )
    return (both[:, :size] + both[:, size:]).reshape(count, size, size)


def prepare_kernel(x_count, chunks, slot_ref, place_ref, prolong_ref, fine_ref, *rest):
    outs, (left_ref, right_ref, sums_ref, done_ref) = rest[:-4], rest[-4:]
    row = pl.program_id(0)
    links, size = fine_ref.shape[1], fine_ref.shape[2]
    part = size // x_count
    step = part // chunks

    @pl.when(row == 0)
    def _():
        load_weights(prolong_ref, left_ref, right_ref)

    sums_ref[...] = jnp.zeros_like(sums_ref)
    for link in range(links):
        slot = slot_ref[row, link]
        sums_ref[slot] += fine_ref[0, link]
    done_ref[...] = triple([sums_ref[s] for s in range(links)], left_ref, right_ref)
    for offset in range(x_count):
        start = lax.rem(place_ref[0] + offset, x_count) * part
        for chunk in range(chunks):
            at = pl.multiple_of(start + chunk * step, step)
            outs[offset * chunks + chunk][0] = done_ref[:, pl.ds(at, step), :]


def prepare(fine_blocks, slot_one, prolong_one, place, x_count, chunks):
    rows, links, size, _ = fine_blocks.shape
    step = size // x_count // chunks
    out = jax.ShapeDtypeStruct((rows, links, step, size), jnp.float32)
    outs = pl.pallas_call(
        functools.partial(prepare_kernel, x_count, chunks),
        out_shape=[out] * (x_count * chunks),
        grid_spec=pltpu.PrefetchScalarGridSpec(
            num_scalar_prefetch=2,
            grid=(rows,),
            in_specs=[
                pl.BlockSpec((size, size), lambda e, *_: (0, 0)),
                pl.BlockSpec((1, links, size, size), lambda e, *_: (e, 0, 0, 0)),
            ],
            out_specs=[pl.BlockSpec((1, links, step, size), lambda e, *_: (e, 0, 0, 0))]
            * (x_count * chunks),
            scratch_shapes=[
                pltpu.VMEM((2 * size, 2 * size), jnp.bfloat16),
                pltpu.VMEM((2 * size, 2 * size), jnp.bfloat16),
                pltpu.VMEM((links, size, size), jnp.float32),
                pltpu.VMEM((links, size, size), jnp.float32),
            ],
        ),
        compiler_params=pltpu.CompilerParams(vmem_limit_bytes=vmem_limit),
        cost_estimate=pl.CostEstimate(
            flops=16 * rows * links * size**3,
            bytes_accessed=8 * rows * links * size**2,
            transcendentals=0,
        ),
        name="prepare",
    )(slot_one, place, prolong_one, fine_blocks)
    return [outs[offset * chunks : (offset + 1) * chunks] for offset in range(x_count)]


def whole(kernel, scalars, arrays, out_shapes, name):
    return pl.pallas_call(
        kernel,
        out_shape=out_shapes,
        in_specs=[pl.BlockSpec(memory_space=pltpu.SMEM)] * len(scalars)
        + [pl.BlockSpec(memory_space=pltpu.VMEM)] * len(arrays),
        out_specs=[pl.BlockSpec(memory_space=pltpu.VMEM)] * len(out_shapes),
        compiler_params=pltpu.CompilerParams(vmem_limit_bytes=vmem_limit),
        cost_estimate=pl.CostEstimate(flops=0, bytes_accessed=beside, transcendentals=0),
        name=name,
    )(*scalars, *arrays)


def combine_kernel(sources, target_ref, *refs):
    arrays, (far_ref, sums_ref) = refs[:sources], refs[sources:]
    rows = arrays[0].shape[0]
    sums_ref[...] = jnp.zeros_like(sums_ref)
    for source in range(sources):

        def one(row, carry, source=source):
            sums_ref[target_ref[source, row]] += arrays[source][row]
            return carry

        lax.fori_loop(0, rows, one, 0, unroll=4)
    far_ref[...] = sums_ref[0 : far_ref.shape[0]]


def finish_kernel(middle_ref, sums_ref, got_ref, *outs):
    half, rows = got_ref.shape[0], outs[-1].shape[0]
    own = len([out for out in outs if out.shape[0] == rows])
    far, near = outs[:-own], outs[-own:]
    width = own * rows
    for d, out in enumerate(far):
        at = (d + 1) * width
        out[...] = sums_ref[half + at : half + at + width] + got_ref[at : at + width]
    for offset, out in enumerate(near):
        at = offset * rows
        total = sums_ref[half + at : half + at + rows] + got_ref[at : at + rows]
        out[...] = jnp.where(middle_ref[0] > 0, total, 0.0)


def settle_kernel(count, *refs):
    near, far, outs = refs[:count], refs[count:-count], refs[-count:]
    rows = outs[0].shape[0]
    for offset, out in enumerate(outs):
        total = near[offset][...]
        for piece in far:
            total = total + piece[offset * rows : (offset + 1) * rows]
        out[...] = total


def second_kernel(slot_ref, target_ref, *refs):
    parts, buffer_ref = refs[:-1], refs[-1]
    rows, links, step, _ = parts[0].shape
    buffer_ref[...] = jnp.zeros_like(buffer_ref)

    def one(row, carry):
        target = target_ref[row]
        for link in range(links):
            slot = slot_ref[row, link]
            for offset, part in enumerate(parts):
                buffer_ref[target, slot, offset * step : (offset + 1) * step, :] += part[row, link]
        return carry

    lax.fori_loop(0, rows, one, 0)


def place_kernel(x_count, chunks, place_ref, *refs):
    pieces, out = refs[:-1], refs[-1]
    part = out.shape[2] // x_count
    step = part // chunks
    for offset in range(x_count):
        start = lax.rem(place_ref[0] + x_count - offset, x_count) * part
        for chunk in range(chunks):
            at = pl.multiple_of(start + chunk * step, step)
            out[:, :, pl.ds(at, step), :] = pieces[offset * chunks + chunk][...]


def place_one(pieces, place, x_count, chunks):
    rows, links, step, size = pieces[0].shape
    return pl.pallas_call(
        functools.partial(place_kernel, x_count, chunks),
        out_shape=jax.ShapeDtypeStruct((rows, links, size, size), jnp.float32),
        grid_spec=pltpu.PrefetchScalarGridSpec(
            num_scalar_prefetch=1,
            grid=(rows,),
            in_specs=[pl.BlockSpec((1, links, step, size), lambda e, *_: (e, 0, 0, 0))] * len(pieces),
            out_specs=pl.BlockSpec((1, links, size, size), lambda e, *_: (e, 0, 0, 0)),
        ),
        compiler_params=pltpu.CompilerParams(vmem_limit_bytes=vmem_limit),
        cost_estimate=pl.CostEstimate(
            flops=0, bytes_accessed=8 * rows * links * size**2, transcendentals=0
        ),
        name="place_one",
    )(place, *pieces)


def last_kernel(x_count, chunks, place_ref, prolong_ref, *refs):
    pieces, (out, left_ref, right_ref, sums_ref) = refs[:-4], refs[-4:]
    links, size = out.shape[1], out.shape[2]
    part = size // x_count
    step = part // chunks

    @pl.when(pl.program_id(0) == 0)
    def _():
        load_weights(prolong_ref, left_ref, right_ref)

    for chunk, piece in enumerate(pieces):
        total = piece[0, 0]
        for peer in range(1, piece.shape[0]):
            total = total + piece[peer, 0]
        for offset in range(x_count):
            start = lax.rem(place_ref[0] + x_count - offset, x_count) * part
            at = pl.multiple_of(start + chunk * step, step)
            sums_ref[:, pl.ds(at, step), :] = total[:, offset * step : (offset + 1) * step, :]
    out[0] = triple([sums_ref[s] for s in range(links)], left_ref, right_ref)


def last(pieces, prolong_two, place, x_count, chunks):
    peers, rows, links, step, size = pieces[0].shape
    return pl.pallas_call(
        functools.partial(last_kernel, x_count, chunks),
        out_shape=jax.ShapeDtypeStruct((rows, links, size, size), jnp.float32),
        grid_spec=pltpu.PrefetchScalarGridSpec(
            num_scalar_prefetch=1,
            grid=(rows,),
            in_specs=[pl.BlockSpec((size, size), lambda e, *_: (0, 0))]
            + [pl.BlockSpec((peers, 1, links, step, size), lambda e, *_: (0, e, 0, 0, 0))]
            * len(pieces),
            out_specs=pl.BlockSpec((1, links, size, size), lambda e, *_: (e, 0, 0, 0)),
            scratch_shapes=[
                pltpu.VMEM((2 * size, 2 * size), jnp.bfloat16),
                pltpu.VMEM((2 * size, 2 * size), jnp.bfloat16),
                pltpu.VMEM((links, size, size), jnp.float32),
            ],
        ),
        compiler_params=pltpu.CompilerParams(vmem_limit_bytes=vmem_limit),
        cost_estimate=pl.CostEstimate(
            flops=16 * rows * links * size**3,
            bytes_accessed=4 * rows * links * size**2 * (peers + 1),
            transcendentals=0,
        ),
        name="last",
    )(place, prolong_two, *pieces)


def sweep(fine_blocks, neighbours, diag_inverse, right_side, initial_guess):
    rows = fine_blocks.shape[0]
    axes = ("group", "member")
    devices = lax.axis_size(axes)
    device = lax.axis_index(axes)
    before = lax.ppermute(initial_guess, axes, [(i, (i + 1) % devices) for i in range(devices)])
    after = lax.ppermute(initial_guess, axes, [(i, (i - 1) % devices) for i in range(devices)])
    window = jnp.concatenate([before, initial_guess, after], axis=0)
    position = (neighbours - device * rows + rows) % (rows * devices)
    nearby = window[position]
    product = jnp.sum(fine_blocks * nearby[:, :, None, :], axis=(1, 3))
    defect = right_side - product
    return initial_guess + damping * jnp.sum(diag_inverse * defect[:, None, :], axis=2)


def local(
    fine_blocks,
    neighbours,
    slot_one,
    pair_one,
    prolong_one,
    slot_two,
    pair_two,
    prolong_two,
    diag_inverse,
    right_side,
    initial_guess,
):
    rows, links, size, _ = fine_blocks.shape
    rows_one, rows_two = rows // 2, rows // 4
    members, groups = lax.axis_size("member"), lax.axis_size("group")
    z_count, x_count = grid_of(members)
    half = z_count // 2
    part = size // x_count
    chunks = max(c for c in range(1, chunk_goal + 1) if part % (8 * c) == 0)
    step = part // chunks

    member = lax.axis_index("member")
    z, x = member // x_count, member % x_count
    upper = (z >= half).astype(jnp.int32)
    place = jnp.stack([x]).astype(jnp.int32)

    def at(side, d, x_at):
        return (half + d if side else half - 1 - d) * x_count + x_at % x_count

    def hop(array, d_from, d_to, offset):
        pairs = [
            (at(side, d_from, x_at), at(side, d_to, x_at + offset))
            for side in range(2)
            for x_at in range(x_count)
        ]
        return lax.ppermute(array, "member", pairs)

    def hop_x(array, offset):
        pairs = [
            (z_at * x_count + x_at, z_at * x_count + (x_at + offset) % x_count)
            for z_at in range(z_count)
            for x_at in range(x_count)
        ]
        return lax.ppermute(array, "member", pairs)

    routes = [(d, o) for d in range(half) for o in range(x_count)]

    def along(arrays):
        return [array if o == 0 else hop_x(array, o) for o, array in enumerate(arrays)]

    def inward(arrays):
        return arrays + [hop(array, d, 0, 0) for d in range(1, half) for array in arrays]

    owner_rows = jnp.stack(
        [
            hop(pair_one, d, 0, o) if d > 0 else hop_x(pair_one, o) if o > 0 else pair_one
            for d, o in routes
        ]
    )
    owner = owner_rows // rows_one % members
    owner_z, owner_x = owner // x_count, owner % x_count
    owner_upper = (owner_z >= half).astype(jnp.int32)
    owner_d = jnp.where(owner_upper > 0, owner_z - half, half - 1 - owner_z)
    near = (owner_upper == upper).astype(jnp.int32)
    target_one = ((near * half + owner_d) * x_count + (owner_x - x + x_count) % x_count) * rows_one
    target_one = (target_one + owner_rows % rows_one).astype(jnp.int32)
    middle = jnp.stack([(z == half - 1) | (z == half)]).astype(jnp.int32)

    owner_two = pair_two // rows_two
    target_two = (owner_two // members * rows_two + pair_two % rows_two).astype(jnp.int32)

    slot_one, target_one = lax.optimization_barrier((slot_one, target_one))
    outgoing = prepare(fine_blocks, slot_one, prolong_one, place, x_count, chunks)
    across = [(at(0, 0, x_at), at(1, 0, x_at)) for x_at in range(x_count)]
    across = across + [(b, a) for a, b in across]
    sums = jax.ShapeDtypeStruct((half * x_count * rows_one, links, step, size), jnp.float32)
    piece = jax.ShapeDtypeStruct((rows_one, links, step, size), jnp.float32)
    buffer = jax.ShapeDtypeStruct((groups * rows_two, links, x_count * step, size), jnp.float32)
    everything = jax.ShapeDtypeStruct((2 * sums.shape[0],) + sums.shape[1:], jnp.float32)
    everything = jax.ShapeDtypeStruct((2 * sums.shape[0],) + sums.shape[1:], jnp.float32)
    wide = jax.ShapeDtypeStruct((x_count * rows_one,) + piece.shape[1:], jnp.float32)
    parts, received = [], []
    for chunk in range(chunks):
        held = inward(along([outgoing[o][chunk] for o in range(x_count)]))
        far, kept = whole(
            functools.partial(combine_kernel, len(held)),
            [target_one],
            held,
            [sums, everything],
            "combine",
        )
        got = lax.ppermute(far, "member", across)
        finished = whole(
            finish_kernel, [middle], [kept, got], [wide] * (half - 1) + [piece] * x_count, "finish"
        )
        near = list(finished[half - 1 :])
        spread = [hop(finished[d - 1], 0, d, 0) for d in range(1, half)]
        settled = whole(
            functools.partial(settle_kernel, x_count), [], near + spread, [piece] * x_count, "settle"
        )
        ours = along(settled)
        (ready,) = whole(second_kernel, [slot_two, target_two], ours, [buffer], "second")
        parts.append(ours)
        sent = lax.all_to_all(ready, "group", split_axis=0, concat_axis=0, tiled=True)
        received.append(sent.reshape((groups, rows_two) + sent.shape[1:]))

    coarse_one = place_one(
        [parts[chunk][o] for o in range(x_count) for chunk in range(chunks)], place, x_count, chunks
    )
    coarse_two = last(received, prolong_two, place, x_count, chunks)
    smoothed = sweep(fine_blocks, neighbours, diag_inverse, right_side, initial_guess)
    return (coarse_one, coarse_two, smoothed)


def solution(mesh):
    rows = P(("group", "member"))
    return jax.shard_map(
        local,
        mesh=mesh,
        in_specs=(rows, rows, rows, rows, P(), rows, rows, P(), rows, rows, rows),
        out_specs=(rows, rows, rows),
        check_vma=False,
    )
```

```python
import functools

import jax
import jax.numpy as jnp
from jax import lax
from jax.experimental import pallas as pl
from jax.experimental.pallas import tpu as pltpu
from jax.sharding import PartitionSpec as P

damping = 0.7
chunk_goal = 4
rows_a_step = 4
vmem_limit = 20 * 1024 * 1024
beside = 20 * 1000**3


def grid_of(member_count):
    x_count = max(d for d in range(1, member_count + 1) if member_count % d == 0 and d * d <= member_count)
    return member_count // x_count, x_count


def split(values):
    high = values.astype(jnp.bfloat16)
    low = (values - high.astype(jnp.float32)).astype(jnp.bfloat16)
    return high, low


def load_weights(prolong_ref, left_ref, right_ref):
    prolong = prolong_ref[...]
    size = prolong.shape[0]
    high, low = split(prolong)
    high_t, low_t = split(prolong.T)
    for half in range(2):
        at = pl.ds(half * size, size)
        left_ref[0:size, at] = high_t
        left_ref[size : 2 * size, at] = low_t
        right_ref[at, 0:size] = high
        right_ref[at, size : 2 * size] = low


def triple(blocks, left_ref, right_ref):
    size = blocks[0].shape[0]
    count = len(blocks)
    high, low = split(jnp.concatenate(blocks, axis=1))
    both = jnp.dot(
        left_ref[...], jnp.concatenate([high, low], axis=0), preferred_element_type=jnp.float32
    )
    left = both[:size] + both[size:]
    rows = jnp.concatenate([left[:, s * size : (s + 1) * size] for s in range(count)], axis=0)
    high, low = split(rows)
    both = jnp.dot(
        jnp.concatenate([high, low], axis=1), right_ref[...], preferred_element_type=jnp.float32
    )
    return (both[:, :size] + both[:, size:]).reshape(count, size, size)


def prepare_kernel(x_count, chunks, slot_ref, place_ref, prolong_ref, fine_ref, *rest):
    outs, (left_ref, right_ref, sums_ref, done_ref) = rest[:-4], rest[-4:]
    held, links, size, _ = fine_ref.shape
    part = size // x_count
    step = part // chunks

    @pl.when(pl.program_id(0) == 0)
    def _():
        load_weights(prolong_ref, left_ref, right_ref)

    sums_ref[...] = jnp.zeros_like(sums_ref)
    for row in range(held):
        for link in range(links):
            slot = slot_ref[pl.program_id(0) * held + row, link]
            sums_ref[row, slot] += fine_ref[row, link]
    sums = [sums_ref[row, slot] for row in range(held) for slot in range(links)]
    done_ref[...] = triple(sums, left_ref, right_ref).reshape(done_ref.shape)
    for offset in range(x_count):
        start = lax.rem(place_ref[0] + offset, x_count) * part
        for chunk in range(chunks):
            at = pl.multiple_of(start + chunk * step, step)
            outs[offset * chunks + chunk][...] = done_ref[:, :, pl.ds(at, step), :]


def prepare(fine_blocks, slot_one, prolong_one, place, x_count, chunks):
    rows, links, size, _ = fine_blocks.shape
    step = size // x_count // chunks
    held = max(h for h in range(1, rows_a_step + 1) if rows % h == 0)
    out = jax.ShapeDtypeStruct((rows, links, step, size), jnp.float32)
    outs = pl.pallas_call(
        functools.partial(prepare_kernel, x_count, chunks),
        out_shape=[out] * (x_count * chunks),
        grid_spec=pltpu.PrefetchScalarGridSpec(
            num_scalar_prefetch=2,
            grid=(rows // held,),
            in_specs=[
                pl.BlockSpec((size, size), lambda e, *_: (0, 0)),
                pl.BlockSpec((held, links, size, size), lambda e, *_: (e, 0, 0, 0)),
            ],
            out_specs=[pl.BlockSpec((held, links, step, size), lambda e, *_: (e, 0, 0, 0))]
            * (x_count * chunks),
            scratch_shapes=[
                pltpu.VMEM((2 * size, 2 * size), jnp.bfloat16),
                pltpu.VMEM((2 * size, 2 * size), jnp.bfloat16),
                pltpu.VMEM((held, links, size, size), jnp.float32),
                pltpu.VMEM((held, links, size, size), jnp.float32),
            ],
        ),
        compiler_params=pltpu.CompilerParams(vmem_limit_bytes=vmem_limit),
        cost_estimate=pl.CostEstimate(
            flops=16 * rows * links * size**3,
            bytes_accessed=8 * rows * links * size**2,
            transcendentals=0,
        ),
        name="prepare",
    )(slot_one, place, prolong_one, fine_blocks)
    return [outs[offset * chunks : (offset + 1) * chunks] for offset in range(x_count)]


def whole(kernel, scalars, arrays, out_shapes, name):
    return pl.pallas_call(
        kernel,
        out_shape=out_shapes,
        in_specs=[pl.BlockSpec(memory_space=pltpu.SMEM)] * len(scalars)
        + [pl.BlockSpec(memory_space=pltpu.VMEM)] * len(arrays),
        out_specs=[pl.BlockSpec(memory_space=pltpu.VMEM)] * len(out_shapes),
        compiler_params=pltpu.CompilerParams(vmem_limit_bytes=vmem_limit),
        cost_estimate=pl.CostEstimate(flops=beside, bytes_accessed=0, transcendentals=0),
        name=name,
    )(*scalars, *arrays)


def combine_kernel(sources, target_ref, *refs):
    arrays, (far_ref, sums_ref) = refs[:sources], refs[sources:]
    rows = arrays[0].shape[0]
    sums_ref[...] = jnp.zeros_like(sums_ref)
    for source in range(sources):

        def one(row, carry, source=source):
            sums_ref[target_ref[source, row]] += arrays[source][row]
            return carry

        lax.fori_loop(0, rows, one, 0, unroll=True)
    far_ref[...] = sums_ref[0 : far_ref.shape[0]]


def finish_kernel(middle_ref, sums_ref, got_ref, *outs):
    half, rows = got_ref.shape[0], outs[-1].shape[0]
    own = len([out for out in outs if out.shape[0] == rows])
    far, near = outs[:-own], outs[-own:]
    width = own * rows
    for d, out in enumerate(far):
        at = (d + 1) * width
        out[...] = sums_ref[half + at : half + at + width] + got_ref[at : at + width]
    for offset, out in enumerate(near):
        at = offset * rows
        total = sums_ref[half + at : half + at + rows] + got_ref[at : at + rows]
        out[...] = jnp.where(middle_ref[0] > 0, total, 0.0)


def settle_kernel(count, *refs):
    near, far, outs = refs[:count], refs[count:-count], refs[-count:]
    rows = outs[0].shape[0]
    for offset, out in enumerate(outs):
        total = near[offset][...]
        for piece in far:
            total = total + piece[offset * rows : (offset + 1) * rows]
        out[...] = total


def second_kernel(slot_ref, target_ref, *refs):
    parts, buffer_ref = refs[:-1], refs[-1]
    rows, links, step, _ = parts[0].shape
    buffer_ref[...] = jnp.zeros_like(buffer_ref)

    def one(row, carry):
        target = target_ref[row]
        for link in range(links):
            slot = slot_ref[row, link]
            for offset, part in enumerate(parts):
                buffer_ref[target, slot, offset * step : (offset + 1) * step, :] += part[row, link]
        return carry

    lax.fori_loop(0, rows, one, 0, unroll=True)


def place_kernel(x_count, chunks, place_ref, *refs):
    pieces, out = refs[:-1], refs[-1]
    part = out.shape[2] // x_count
    step = part // chunks
    for offset in range(x_count):
        start = lax.rem(place_ref[0] + x_count - offset, x_count) * part
        for chunk in range(chunks):
            at = pl.multiple_of(start + chunk * step, step)
            out[:, :, pl.ds(at, step), :] = pieces[offset * chunks + chunk][...]


def place_one(pieces, place, x_count, chunks):
    rows, links, step, size = pieces[0].shape
    return pl.pallas_call(
        functools.partial(place_kernel, x_count, chunks),
        out_shape=jax.ShapeDtypeStruct((rows, links, size, size), jnp.float32),
        grid_spec=pltpu.PrefetchScalarGridSpec(
            num_scalar_prefetch=1,
            grid=(rows,),
            in_specs=[pl.BlockSpec((1, links, step, size), lambda e, *_: (e, 0, 0, 0))] * len(pieces),
            out_specs=pl.BlockSpec((1, links, size, size), lambda e, *_: (e, 0, 0, 0)),
        ),
        compiler_params=pltpu.CompilerParams(vmem_limit_bytes=vmem_limit),
        cost_estimate=pl.CostEstimate(
            flops=0, bytes_accessed=8 * rows * links * size**2, transcendentals=0
        ),
        name="place_one",
    )(place, *pieces)


def last_kernel(x_count, chunks, place_ref, prolong_ref, *refs):
    pieces, (out, left_ref, right_ref, sums_ref) = refs[:-4], refs[-4:]
    links, size = out.shape[1], out.shape[2]
    part = size // x_count
    step = part // chunks

    @pl.when(pl.program_id(0) == 0)
    def _():
        load_weights(prolong_ref, left_ref, right_ref)

    for chunk, piece in enumerate(pieces):
        total = piece[0]
        for peer in range(1, piece.shape[0]):
            total = total + piece[peer]
        for offset in range(x_count):
            start = lax.rem(place_ref[0] + x_count - offset, x_count) * part
            at = pl.multiple_of(start + chunk * step, step)
            sums_ref[:, :, pl.ds(at, step), :] = total[:, :, offset * step : (offset + 1) * step, :]
    sums = [sums_ref[row, slot] for row in range(out.shape[0]) for slot in range(links)]
    out[...] = triple(sums, left_ref, right_ref).reshape(out.shape)


def last(pieces, prolong_two, place, x_count, chunks):
    peers, rows, links, step, size = pieces[0].shape
    held = max(h for h in range(1, rows_a_step // 2 + 1) if rows % h == 0)
    return pl.pallas_call(
        functools.partial(last_kernel, x_count, chunks),
        out_shape=jax.ShapeDtypeStruct((rows, links, size, size), jnp.float32),
        grid_spec=pltpu.PrefetchScalarGridSpec(
            num_scalar_prefetch=1,
            grid=(rows // held,),
            in_specs=[pl.BlockSpec((size, size), lambda e, *_: (0, 0))]
            + [pl.BlockSpec((peers, held, links, step, size), lambda e, *_: (0, e, 0, 0, 0))]
            * len(pieces),
            out_specs=pl.BlockSpec((held, links, size, size), lambda e, *_: (e, 0, 0, 0)),
            scratch_shapes=[
                pltpu.VMEM((2 * size, 2 * size), jnp.bfloat16),
                pltpu.VMEM((2 * size, 2 * size), jnp.bfloat16),
                pltpu.VMEM((held, links, size, size), jnp.float32),
            ],
        ),
        compiler_params=pltpu.CompilerParams(vmem_limit_bytes=vmem_limit),
        cost_estimate=pl.CostEstimate(
            flops=16 * rows * links * size**3,
            bytes_accessed=4 * rows * links * size**2 * (peers + 1),
            transcendentals=0,
        ),
        name="last",
    )(place, prolong_two, *pieces)


def sweep(fine_blocks, neighbours, diag_inverse, right_side, initial_guess):
    rows = fine_blocks.shape[0]
    axes = ("group", "member")
    devices = lax.axis_size(axes)
    device = lax.axis_index(axes)
    before = lax.ppermute(initial_guess, axes, [(i, (i + 1) % devices) for i in range(devices)])
    after = lax.ppermute(initial_guess, axes, [(i, (i - 1) % devices) for i in range(devices)])
    window = jnp.concatenate([before, initial_guess, after], axis=0)
    position = (neighbours - device * rows + rows) % (rows * devices)
    nearby = window[position]
    product = jnp.sum(fine_blocks * nearby[:, :, None, :], axis=(1, 3))
    defect = right_side - product
    return initial_guess + damping * jnp.sum(diag_inverse * defect[:, None, :], axis=2)


def local(
    fine_blocks,
    neighbours,
    slot_one,
    pair_one,
    prolong_one,
    slot_two,
    pair_two,
    prolong_two,
    diag_inverse,
    right_side,
    initial_guess,
):
    rows, links, size, _ = fine_blocks.shape
    rows_one, rows_two = rows // 2, rows // 4
    members, groups = lax.axis_size("member"), lax.axis_size("group")
    z_count, x_count = grid_of(members)
    half = z_count // 2
    part = size // x_count
    chunks = max(c for c in range(1, chunk_goal + 1) if part % (8 * c) == 0)
    step = part // chunks

    member = lax.axis_index("member")
    z, x = member // x_count, member % x_count
    upper = (z >= half).astype(jnp.int32)
    place = jnp.stack([x]).astype(jnp.int32)

    def at(side, d, x_at):
        return (half + d if side else half - 1 - d) * x_count + x_at % x_count

    def hop(array, d_from, d_to, offset):
        pairs = [
            (at(side, d_from, x_at), at(side, d_to, x_at + offset))
            for side in range(2)
            for x_at in range(x_count)
        ]
        return lax.ppermute(array, "member", pairs)

    def hop_x(array, offset):
        pairs = [
            (z_at * x_count + x_at, z_at * x_count + (x_at + offset) % x_count)
            for z_at in range(z_count)
            for x_at in range(x_count)
        ]
        return lax.ppermute(array, "member", pairs)

    routes = [(d, o) for d in range(half) for o in range(x_count)]

    def along(arrays):
        return [array if o == 0 else hop_x(array, o) for o, array in enumerate(arrays)]

    def inward(arrays):
        return arrays + [hop(array, d, 0, 0) for d in range(1, half) for array in arrays]

    owner_rows = jnp.stack(
        [
            hop(pair_one, d, 0, o) if d > 0 else hop_x(pair_one, o) if o > 0 else pair_one
            for d, o in routes
        ]
    )
    owner = owner_rows // rows_one % members
    owner_z, owner_x = owner // x_count, owner % x_count
    owner_upper = (owner_z >= half).astype(jnp.int32)
    owner_d = jnp.where(owner_upper > 0, owner_z - half, half - 1 - owner_z)
    near = (owner_upper == upper).astype(jnp.int32)
    target_one = ((near * half + owner_d) * x_count + (owner_x - x + x_count) % x_count) * rows_one
    target_one = (target_one + owner_rows % rows_one).astype(jnp.int32)
    middle = jnp.stack([(z == half - 1) | (z == half)]).astype(jnp.int32)

    owner_two = pair_two // rows_two
    target_two = (owner_two // members * rows_two + pair_two % rows_two).astype(jnp.int32)

    slot_one, target_one = lax.optimization_barrier((slot_one, target_one))
    outgoing = prepare(fine_blocks, slot_one, prolong_one, place, x_count, chunks)
    across = [(at(0, 0, x_at), at(1, 0, x_at)) for x_at in range(x_count)]
    across = across + [(b, a) for a, b in across]
    sums = jax.ShapeDtypeStruct((half * x_count * rows_one, links, step, size), jnp.float32)
    piece = jax.ShapeDtypeStruct((rows_one, links, step, size), jnp.float32)
    buffer = jax.ShapeDtypeStruct((groups * rows_two, links, x_count * step, size), jnp.float32)
    everything = jax.ShapeDtypeStruct((2 * sums.shape[0],) + sums.shape[1:], jnp.float32)
    everything = jax.ShapeDtypeStruct((2 * sums.shape[0],) + sums.shape[1:], jnp.float32)
    wide = jax.ShapeDtypeStruct((x_count * rows_one,) + piece.shape[1:], jnp.float32)
    parts, received = [], []
    for chunk in range(chunks):
        held = inward(along([outgoing[o][chunk] for o in range(x_count)]))
        far, kept = whole(
            functools.partial(combine_kernel, len(held)),
            [target_one],
            held,
            [sums, everything],
            "combine",
        )
        got = lax.ppermute(far, "member", across)
        finished = whole(
            finish_kernel, [middle], [kept, got], [wide] * (half - 1) + [piece] * x_count, "finish"
        )
        near = list(finished[half - 1 :])
        spread = [hop(finished[d - 1], 0, d, 0) for d in range(1, half)]
        settled = whole(
            functools.partial(settle_kernel, x_count), [], near + spread, [piece] * x_count, "settle"
        )
        ours = along(settled)
        (ready,) = whole(second_kernel, [slot_two, target_two], ours, [buffer], "second")
        parts.append(ours)
        sent = lax.all_to_all(ready, "group", split_axis=0, concat_axis=0, tiled=True)
        received.append(sent.reshape((groups, rows_two) + sent.shape[1:]))

    coarse_one = place_one(
        [parts[chunk][o] for o in range(x_count) for chunk in range(chunks)], place, x_count, chunks
    )
    coarse_two = last(received, prolong_two, place, x_count, chunks)
    smoothed = sweep(fine_blocks, neighbours, diag_inverse, right_side, initial_guess)
    return (coarse_one, coarse_two, smoothed)


def solution(mesh):
    rows = P(("group", "member"))
    return jax.shard_map(
        local,
        mesh=mesh,
        in_specs=(rows, rows, rows, rows, P(), rows, rows, P(), rows, rows, rows),
        out_specs=(rows, rows, rows),
        check_vma=False,
    )
```

```python
import functools

import jax
import jax.numpy as jnp
from jax import lax
from jax.experimental import pallas as pl
from jax.experimental.pallas import tpu as pltpu
from jax.sharding import PartitionSpec as P

damping = 0.7
rows_a_step = 4
vmem_limit = 20 * 1024 * 1024
beside = (6, 6, 6, 6, 6)


def grid_of(member_count):
    x_count = max(d for d in range(1, member_count + 1) if member_count % d == 0 and d * d <= member_count)
    return member_count // x_count, x_count


def chunk_steps(part):
    tiles = part // 8
    step = max(tiles // 4, 1)
    steps = [step] * (tiles // step)
    if step > 1:
        steps[-1:] = [step - step // 2, step // 2]
    if sum(steps) < tiles:
        steps.append(tiles - sum(steps))
    return [8 * step for step in steps]


def split(values):
    high = values.astype(jnp.bfloat16)
    low = (values - high.astype(jnp.float32)).astype(jnp.bfloat16)
    return high, low


def load_weights(prolong_ref, left_ref, right_ref):
    prolong = prolong_ref[...]
    size = prolong.shape[0]
    high, low = split(prolong)
    high_t, low_t = split(prolong.T)
    for half in range(2):
        at = pl.ds(half * size, size)
        left_ref[0:size, at] = high_t
        left_ref[size : 2 * size, at] = low_t
        right_ref[at, 0:size] = high
        right_ref[at, size : 2 * size] = low


def triple(blocks, left_ref, right_ref):
    size = blocks[0].shape[0]
    count = len(blocks)
    high, low = split(jnp.concatenate(blocks, axis=1))
    both = jnp.dot(
        left_ref[...], jnp.concatenate([high, low], axis=0), preferred_element_type=jnp.float32
    )
    left = both[:size] + both[size:]
    rows = jnp.concatenate([left[:, s * size : (s + 1) * size] for s in range(count)], axis=0)
    high, low = split(rows)
    both = jnp.dot(
        jnp.concatenate([high, low], axis=1), right_ref[...], preferred_element_type=jnp.float32
    )
    return (both[:, :size] + both[:, size:]).reshape(count, size, size)


def prepare_kernel(x_count, slot_ref, place_ref, prolong_ref, fine_ref, *rest):
    outs, (left_ref, right_ref, sums_ref, done_ref) = rest[:-4], rest[-4:]
    held, links, size, _ = fine_ref.shape
    chunks = len(outs) // x_count
    part = size // x_count

    @pl.when(pl.program_id(0) == 0)
    def _():
        load_weights(prolong_ref, left_ref, right_ref)

    sums_ref[...] = jnp.zeros_like(sums_ref)
    for row in range(held):
        for link in range(links):
            slot = slot_ref[pl.program_id(0) * held + row, link]
            sums_ref[row, slot] += fine_ref[row, link]
    sums = [sums_ref[row, slot] for row in range(held) for slot in range(links)]
    done_ref[...] = triple(sums, left_ref, right_ref).reshape(done_ref.shape)
    for offset in range(x_count):
        start = lax.rem(place_ref[0] + offset, x_count) * part
        for out in outs[offset * chunks : (offset + 1) * chunks]:
            step = out.shape[2]
            out[...] = done_ref[:, :, pl.ds(pl.multiple_of(start, 8), step), :]
            start = start + step


def prepare(fine_blocks, slot_one, prolong_one, place, x_count, steps):
    rows, links, size, _ = fine_blocks.shape
    chunks = len(steps)
    held = max(h for h in range(1, rows_a_step + 1) if rows % h == 0)
    outs = pl.pallas_call(
        functools.partial(prepare_kernel, x_count),
        out_shape=[jax.ShapeDtypeStruct((rows, links, step, size), jnp.float32) for step in steps]
        * x_count,
        grid_spec=pltpu.PrefetchScalarGridSpec(
            num_scalar_prefetch=2,
            grid=(rows // held,),
            in_specs=[
                pl.BlockSpec((size, size), lambda e, *_: (0, 0)),
                pl.BlockSpec((held, links, size, size), lambda e, *_: (e, 0, 0, 0)),
            ],
            out_specs=[
                pl.BlockSpec((held, links, step, size), lambda e, *_: (e, 0, 0, 0)) for step in steps
            ]
            * x_count,
            scratch_shapes=[
                pltpu.VMEM((2 * size, 2 * size), jnp.bfloat16),
                pltpu.VMEM((2 * size, 2 * size), jnp.bfloat16),
                pltpu.VMEM((held, links, size, size), jnp.float32),
                pltpu.VMEM((held, links, size, size), jnp.float32),
            ],
        ),
        compiler_params=pltpu.CompilerParams(vmem_limit_bytes=vmem_limit),
        cost_estimate=pl.CostEstimate(
            flops=16 * rows * links * size**3,
            bytes_accessed=8 * rows * links * size**2,
            transcendentals=0,
        ),
        name="prepare",
    )(slot_one, place, prolong_one, fine_blocks)
    return [outs[offset * chunks : (offset + 1) * chunks] for offset in range(x_count)]


def whole(kernel, scalars, arrays, out_shapes, name, work=0, scratch=()):
    return pl.pallas_call(
        kernel,
        out_shape=out_shapes,
        in_specs=[pl.BlockSpec(memory_space=pltpu.SMEM)] * len(scalars)
        + [pl.BlockSpec(memory_space=pltpu.VMEM)] * len(arrays),
        out_specs=[pl.BlockSpec(memory_space=pltpu.VMEM)] * len(out_shapes),
        scratch_shapes=scratch,
        compiler_params=pltpu.CompilerParams(vmem_limit_bytes=vmem_limit),
        cost_estimate=pl.CostEstimate(flops=work * 10**9, bytes_accessed=0, transcendentals=0),
        name=name,
    )(*scalars, *arrays)


def combine_kernel(sources, target_ref, *refs):
    arrays, (far_ref, sums_ref) = refs[:sources], refs[sources:]
    rows = arrays[0].shape[0]
    sums_ref[...] = jnp.zeros_like(sums_ref)
    for source in range(sources):

        def one(row, carry, source=source):
            sums_ref[target_ref[source, row]] += arrays[source][row]
            return carry

        lax.fori_loop(0, rows, one, 0, unroll=True)
    far_ref[...] = sums_ref[0 : far_ref.shape[0]]


def finish_kernel(middle_ref, sums_ref, got_ref, *outs):
    half, rows = got_ref.shape[0], outs[-1].shape[0]
    own = len([out for out in outs if out.shape[0] == rows])
    far, near = outs[:-own], outs[-own:]
    width = own * rows
    for d, out in enumerate(far):
        at = (d + 1) * width
        out[...] = sums_ref[half + at : half + at + width] + got_ref[at : at + width]
    for offset, out in enumerate(near):
        at = offset * rows
        total = sums_ref[half + at : half + at + rows] + got_ref[at : at + rows]
        out[...] = jnp.where(middle_ref[0] > 0, total, 0.0)


def settle_kernel(count, *refs):
    near, far, outs = refs[:count], refs[count:-count], refs[-count:]
    rows = outs[0].shape[0]
    for offset, out in enumerate(outs):
        total = near[offset][...]
        for piece in far:
            total = total + piece[offset * rows : (offset + 1) * rows]
        out[...] = total


def second_kernel(x_count, slot_ref, target_ref, *refs):
    parts, outs, sums_ref = refs[:x_count], refs[x_count:-1], refs[-1]
    rows, links, step, _ = parts[0].shape
    share = outs[0].shape[0]
    sums_ref[...] = jnp.zeros_like(sums_ref)

    def one(row, carry):
        target = target_ref[row]
        for link in range(links):
            slot = slot_ref[row, link]
            for offset, part in enumerate(parts):
                sums_ref[target, slot, offset * step : (offset + 1) * step, :] += part[row, link]
        return carry

    lax.fori_loop(0, rows, one, 0, unroll=True)
    for way, out in enumerate(outs):
        out[...] = sums_ref[way * share : (way + 1) * share]


def place_kernel(x_count, place_ref, *refs):
    pieces, out = refs[:-1], refs[-1]
    part = out.shape[2] // x_count
    chunks = len(pieces) // x_count
    for offset in range(x_count):
        start = lax.rem(place_ref[0] + x_count - offset, x_count) * part
        for piece in pieces[offset * chunks : (offset + 1) * chunks]:
            step = piece.shape[2]
            out[:, :, pl.ds(pl.multiple_of(start, 8), step), :] = piece[...]
            start = start + step


def place_one(pieces, place, x_count):
    rows, links, _, size = pieces[0].shape
    return pl.pallas_call(
        functools.partial(place_kernel, x_count),
        out_shape=jax.ShapeDtypeStruct((rows, links, size, size), jnp.float32),
        grid_spec=pltpu.PrefetchScalarGridSpec(
            num_scalar_prefetch=1,
            grid=(rows,),
            in_specs=[
                pl.BlockSpec((1, links, piece.shape[2], size), lambda e, *_: (e, 0, 0, 0))
                for piece in pieces
            ],
            out_specs=pl.BlockSpec((1, links, size, size), lambda e, *_: (e, 0, 0, 0)),
        ),
        compiler_params=pltpu.CompilerParams(vmem_limit_bytes=vmem_limit),
        cost_estimate=pl.CostEstimate(
            flops=0, bytes_accessed=8 * rows * links * size**2, transcendentals=0
        ),
        name="place_one",
    )(place, *pieces)


def last_kernel(x_count, peers, place_ref, prolong_ref, *refs):
    pieces, (out, left_ref, right_ref, sums_ref) = refs[:-4], refs[-4:]
    links, size = out.shape[1], out.shape[2]
    part = size // x_count

    @pl.when(pl.program_id(0) == 0)
    def _():
        load_weights(prolong_ref, left_ref, right_ref)

    done = 0
    for first in range(0, len(pieces), peers):
        total = pieces[first][...]
        for piece in pieces[first + 1 : first + peers]:
            total = total + piece[...]
        step = total.shape[2] // x_count
        for offset in range(x_count):
            start = lax.rem(place_ref[0] + x_count - offset, x_count) * part
            at = pl.multiple_of(start + done, 8)
            sums_ref[:, :, pl.ds(at, step), :] = total[:, :, offset * step : (offset + 1) * step, :]
        done += step
    sums = [sums_ref[row, slot] for row in range(out.shape[0]) for slot in range(links)]
    out[...] = triple(sums, left_ref, right_ref).reshape(out.shape)


def last(pieces, prolong_two, place, x_count, peers):
    rows, links, _, size = pieces[0].shape
    held = max(h for h in range(1, rows_a_step // 2 + 1) if rows % h == 0)
    return pl.pallas_call(
        functools.partial(last_kernel, x_count, peers),
        out_shape=jax.ShapeDtypeStruct((rows, links, size, size), jnp.float32),
        grid_spec=pltpu.PrefetchScalarGridSpec(
            num_scalar_prefetch=1,
            grid=(rows // held,),
            in_specs=[pl.BlockSpec((size, size), lambda e, *_: (0, 0))]
            + [
                pl.BlockSpec((held, links, piece.shape[2], size), lambda e, *_: (e, 0, 0, 0))
                for piece in pieces
            ],
            out_specs=pl.BlockSpec((held, links, size, size), lambda e, *_: (e, 0, 0, 0)),
            scratch_shapes=[
                pltpu.VMEM((2 * size, 2 * size), jnp.bfloat16),
                pltpu.VMEM((2 * size, 2 * size), jnp.bfloat16),
                pltpu.VMEM((held, links, size, size), jnp.float32),
            ],
        ),
        compiler_params=pltpu.CompilerParams(vmem_limit_bytes=vmem_limit),
        cost_estimate=pl.CostEstimate(
            flops=16 * rows * links * size**3,
            bytes_accessed=4 * rows * links * size**2 * (peers + 1),
            transcendentals=0,
        ),
        name="last",
    )(place, prolong_two, *pieces)


def sweep(fine_blocks, neighbours, diag_inverse, right_side, initial_guess):
    rows = fine_blocks.shape[0]
    axes = ("group", "member")
    devices = lax.axis_size(axes)
    device = lax.axis_index(axes)
    before = lax.ppermute(initial_guess, axes, [(i, (i + 1) % devices) for i in range(devices)])
    after = lax.ppermute(initial_guess, axes, [(i, (i - 1) % devices) for i in range(devices)])
    window = jnp.concatenate([before, initial_guess, after], axis=0)
    position = (neighbours - device * rows + rows) % (rows * devices)
    nearby = window[position]
    product = jnp.sum(fine_blocks * nearby[:, :, None, :], axis=(1, 3))
    defect = right_side - product
    return initial_guess + damping * jnp.sum(diag_inverse * defect[:, None, :], axis=2)


def local(
    fine_blocks,
    neighbours,
    slot_one,
    pair_one,
    prolong_one,
    slot_two,
    pair_two,
    prolong_two,
    diag_inverse,
    right_side,
    initial_guess,
):
    rows, links, size, _ = fine_blocks.shape
    rows_one, rows_two = rows // 2, rows // 4
    members, groups = lax.axis_size("member"), lax.axis_size("group")
    z_count, x_count = grid_of(members)
    half = z_count // 2
    part = size // x_count
    steps = chunk_steps(part)

    member = lax.axis_index("member")
    z, x = member // x_count, member % x_count
    upper = (z >= half).astype(jnp.int32)
    place = jnp.stack([x]).astype(jnp.int32)

    def at(side, d, x_at):
        return (half + d if side else half - 1 - d) * x_count + x_at % x_count

    def hop(array, d_from, d_to, offset):
        pairs = [
            (at(side, d_from, x_at), at(side, d_to, x_at + offset))
            for side in range(2)
            for x_at in range(x_count)
        ]
        return lax.ppermute(array, "member", pairs)

    def hop_x(array, offset):
        pairs = [
            (z_at * x_count + x_at, z_at * x_count + (x_at + offset) % x_count)
            for z_at in range(z_count)
            for x_at in range(x_count)
        ]
        return lax.ppermute(array, "member", pairs)

    routes = [(d, o) for d in range(half) for o in range(x_count)]

    def along(arrays):
        return [array if o == 0 else hop_x(array, o) for o, array in enumerate(arrays)]

    def inward(arrays):
        return arrays + [hop(array, d, 0, 0) for d in range(1, half) for array in arrays]

    owner_rows = jnp.stack(
        [
            hop(pair_one, d, 0, o) if d > 0 else hop_x(pair_one, o) if o > 0 else pair_one
            for d, o in routes
        ]
    )
    owner = owner_rows // rows_one % members
    owner_z, owner_x = owner // x_count, owner % x_count
    owner_upper = (owner_z >= half).astype(jnp.int32)
    owner_d = jnp.where(owner_upper > 0, owner_z - half, half - 1 - owner_z)
    near = (owner_upper == upper).astype(jnp.int32)
    target_one = ((near * half + owner_d) * x_count + (owner_x - x + x_count) % x_count) * rows_one
    target_one = (target_one + owner_rows % rows_one).astype(jnp.int32)
    middle = jnp.stack([(z == half - 1) | (z == half)]).astype(jnp.int32)

    way = (pair_two // rows_two // members - lax.axis_index("group") + groups) % groups
    target_two = (way * rows_two + pair_two % rows_two).astype(jnp.int32)

    slot_one, target_one = lax.optimization_barrier((slot_one, target_one))
    outgoing = prepare(fine_blocks, slot_one, prolong_one, place, x_count, steps)
    across = [(at(0, 0, x_at), at(1, 0, x_at)) for x_at in range(x_count)]
    across = across + [(b, a) for a, b in across]
    smoothed = sweep(fine_blocks, neighbours, diag_inverse, right_side, initial_guess)
    before = [smoothed]

    def in_turn(kernel, scalars, arrays, out_shapes, name, **more):
        arrays, before[0] = lax.optimization_barrier((list(arrays), before[0]))
        outs = whole(kernel, scalars, arrays, out_shapes, name, **more)
        before[0] = outs[0]
        return outs

    def rows_of(count, height):
        return jax.ShapeDtypeStruct((count, links, height, size), jnp.float32)

    coming = [inward(along([ways[chunk] for ways in outgoing])) for chunk in range(len(steps))]
    received = []

    def combine(chunk):
        held = coming[chunk]
        total = half * x_count * rows_one
        far, kept = in_turn(
            functools.partial(combine_kernel, len(held)),
            [target_one],
            held,
            [rows_of(total, steps[chunk]), rows_of(2 * total, steps[chunk])],
            "combine",
            work=beside[min(chunk, len(beside) - 1)],
        )
        return kept, lax.ppermute(far, "member", across)

    def finish(chunk, sums):
        if chunk + 2 < len(steps):
            ahead = coming[chunk + 2]
            ahead[x_count], sums = lax.optimization_barrier((ahead[x_count], sums))
        finished = in_turn(
            finish_kernel,
            [middle],
            sums,
            [rows_of(x_count * rows_one, steps[chunk])] * (half - 1)
            + [rows_of(rows_one, steps[chunk])] * x_count,
            "finish",
        )
        return list(finished[half - 1 :]) + [hop(finished[d - 1], 0, d, 0) for d in range(1, half)]

    def settle(chunk, finished):
        return along(
            in_turn(
                functools.partial(settle_kernel, x_count),
                [],
                finished,
                [rows_of(rows_one, steps[chunk])] * x_count,
                "settle",
            )
        )

    def second(chunk, ours):
        received[-groups:], ours = lax.optimization_barrier((received[-groups:], ours))
        height = x_count * steps[chunk]
        shares = in_turn(
            functools.partial(second_kernel, x_count),
            [slot_two, target_two],
            ours,
            [rows_of(rows_two, height)] * groups,
            "second",
            scratch=[pltpu.VMEM((groups * rows_two, links, height, size), jnp.float32)],
        )
        for way, share in enumerate(shares):
            around = [(g, (g + way) % groups) for g in range(groups)]
            received.append(lax.ppermute(share, "group", around) if way > 0 else share)
        return ours

    stages, delays = (combine, finish, settle, second), (0, 1, 2, 2)
    held = [[None] * len(steps) for _ in range(len(stages) + 1)]
    for turn in range(len(steps) + delays[-1]):
        for stage, delay in sorted(enumerate(delays), key=lambda item: (0, 2, 1, 3)[item[0]]):
            chunk = turn - delay
            if 0 <= chunk < len(steps):
                given = [held[stage][chunk]] if stage > 0 else []
                held[stage + 1][chunk] = stages[stage](chunk, *given)
    parts = held[4]

    coarse_one = place_one(
        [parts[chunk][o] for o in range(x_count) for chunk in range(len(steps))], place, x_count
    )
    coarse_two = last(received, prolong_two, place, x_count, groups)
    return (coarse_one, coarse_two, smoothed)


def solution(mesh):
    rows = P(("group", "member"))
    return jax.shard_map(
        local,
        mesh=mesh,
        in_specs=(rows, rows, rows, rows, P(), rows, rows, P(), rows, rows, rows),
        out_specs=(rows, rows, rows),
        check_vma=False,
    )
```

```python
import functools

import jax
import jax.numpy as jnp
from jax import lax
from jax.experimental import pallas as pl
from jax.experimental.pallas import tpu as pltpu
from jax.sharding import PartitionSpec as P

damping = 0.7
rows_a_step = 4
prepare_limit = 48 * 1024 * 1024
vmem_limit = 20 * 1024 * 1024
beside = 6


def grid_of(member_count):
    x_count = max(d for d in range(1, member_count + 1) if member_count % d == 0 and d * d <= member_count)
    return member_count // x_count, x_count


def chunk_steps(part):
    tiles = part // 8
    step = max(tiles // 4, 1)
    ends = [max(step // 2, 1)] * min(2, tiles)
    inner = tiles - sum(ends)
    steps = ends[:1] + [step] * (inner // step) + [inner % step] * (inner % step > 0) + ends[1:]
    return [8 * step for step in steps]


def split(values):
    high = values.astype(jnp.bfloat16)
    low = (values - high.astype(jnp.float32)).astype(jnp.bfloat16)
    return high, low


def load_weights(prolong_ref, left_ref, right_ref):
    prolong = prolong_ref[...]
    size = prolong.shape[0]
    high, low = split(prolong)
    high_t, low_t = split(prolong.T)
    for half in range(2):
        at = pl.ds(half * size, size)
        left_ref[0:size, at] = high_t
        left_ref[size : 2 * size, at] = low_t
        right_ref[at, 0:size] = high
        right_ref[at, size : 2 * size] = low


def triple(blocks, left_ref, right_ref):
    size = blocks[0].shape[0]
    count = len(blocks)
    high, low = split(jnp.concatenate(blocks, axis=1))
    both = jnp.dot(
        left_ref[...], jnp.concatenate([high, low], axis=0), preferred_element_type=jnp.float32
    )
    left = both[:size] + both[size:]
    rows = jnp.concatenate([left[:, s * size : (s + 1) * size] for s in range(count)], axis=0)
    high, low = split(rows)
    both = jnp.dot(
        jnp.concatenate([high, low], axis=1), right_ref[...], preferred_element_type=jnp.float32
    )
    return (both[:, :size] + both[:, size:]).reshape(count, size, size)


def prepare_kernel(x_count, slot_ref, place_ref, prolong_ref, fine_ref, *rest):
    outs, (left_ref, right_ref, sums_ref, done_ref) = rest[:-4], rest[-4:]
    held, links, size, _ = fine_ref.shape
    chunks = len(outs) // x_count
    part = size // x_count

    @pl.when(pl.program_id(0) == 0)
    def _():
        load_weights(prolong_ref, left_ref, right_ref)

    sums_ref[...] = jnp.zeros_like(sums_ref)
    for row in range(held):
        for link in range(links):
            slot = slot_ref[pl.program_id(0) * held + row, link]
            sums_ref[row, slot] += fine_ref[row, link]
    sums = [sums_ref[row, slot] for row in range(held) for slot in range(links)]
    done_ref[...] = triple(sums, left_ref, right_ref).reshape(done_ref.shape)
    for offset in range(x_count):
        start = lax.rem(place_ref[0] + offset, x_count) * part
        for out in outs[offset * chunks : (offset + 1) * chunks]:
            step = out.shape[2]
            out[...] = done_ref[:, :, pl.ds(pl.multiple_of(start, 8), step), :]
            start = start + step


def prepare(fine_blocks, slot_one, prolong_one, place, x_count, steps):
    rows, links, size, _ = fine_blocks.shape
    chunks = len(steps)
    held = max(h for h in range(1, rows_a_step + 1) if rows % h == 0)
    outs = pl.pallas_call(
        functools.partial(prepare_kernel, x_count),
        out_shape=[jax.ShapeDtypeStruct((rows, links, step, size), jnp.float32) for step in steps]
        * x_count,
        grid_spec=pltpu.PrefetchScalarGridSpec(
            num_scalar_prefetch=2,
            grid=(rows // held,),
            in_specs=[
                pl.BlockSpec((size, size), lambda e, *_: (0, 0)),
                pl.BlockSpec((held, links, size, size), lambda e, *_: (e, 0, 0, 0)),
            ],
            out_specs=[
                pl.BlockSpec((held, links, step, size), lambda e, *_: (e, 0, 0, 0)) for step in steps
            ]
            * x_count,
            scratch_shapes=[
                pltpu.VMEM((2 * size, 2 * size), jnp.bfloat16),
                pltpu.VMEM((2 * size, 2 * size), jnp.bfloat16),
                pltpu.VMEM((held, links, size, size), jnp.float32),
                pltpu.VMEM((held, links, size, size), jnp.float32),
            ],
        ),
        compiler_params=pltpu.CompilerParams(vmem_limit_bytes=prepare_limit),
        cost_estimate=pl.CostEstimate(
            flops=16 * rows * links * size**3,
            bytes_accessed=8 * rows * links * size**2,
            transcendentals=0,
        ),
        name="prepare",
    )(slot_one, place, prolong_one, fine_blocks)
    return [list(outs[offset * chunks : (offset + 1) * chunks]) for offset in range(x_count)]


def whole(kernel, scalars, arrays, out_shapes, name, work=0, scratch=()):
    return pl.pallas_call(
        kernel,
        out_shape=out_shapes,
        in_specs=[pl.BlockSpec(memory_space=pltpu.SMEM)] * len(scalars)
        + [pl.BlockSpec(memory_space=pltpu.VMEM)] * len(arrays),
        out_specs=[pl.BlockSpec(memory_space=pltpu.VMEM)] * len(out_shapes),
        scratch_shapes=scratch,
        compiler_params=pltpu.CompilerParams(vmem_limit_bytes=vmem_limit),
        cost_estimate=pl.CostEstimate(flops=work * 10**9, bytes_accessed=0, transcendentals=0),
        name=name,
    )(*scalars, *arrays)


def combine_kernel(sources, target_ref, *refs):
    arrays, (far_ref, sums_ref) = refs[:sources], refs[sources:]
    rows = arrays[0].shape[0]
    sums_ref[...] = jnp.zeros_like(sums_ref)
    for source in range(sources):

        def one(row, carry, source=source):
            sums_ref[target_ref[source, row]] += arrays[source][row]
            return carry

        lax.fori_loop(0, rows, one, 0, unroll=True)
    far_ref[...] = sums_ref[0 : far_ref.shape[0]]


def finish_kernel(middle_ref, sums_ref, got_ref, *outs):
    half, rows = got_ref.shape[0], outs[-1].shape[0]
    own = len([out for out in outs if out.shape[0] == rows])
    far, near = outs[:-own], outs[-own:]
    width = own * rows
    for d, out in enumerate(far):
        at = (d + 1) * width
        out[...] = sums_ref[half + at : half + at + width] + got_ref[at : at + width]
    for offset, out in enumerate(near):
        at = offset * rows
        total = sums_ref[half + at : half + at + rows] + got_ref[at : at + rows]
        out[...] = jnp.where(middle_ref[0] > 0, total, 0.0)


def settle_kernel(count, *refs):
    near, far, outs = refs[:count], refs[count:-count], refs[-count:]
    rows = outs[0].shape[0]
    for offset, out in enumerate(outs):
        total = near[offset][...]
        for piece in far:
            total = total + piece[offset * rows : (offset + 1) * rows]
        out[...] = total


def second_kernel(x_count, slot_ref, target_ref, *refs):
    parts, outs, sums_ref = refs[:x_count], refs[x_count:-1], refs[-1]
    rows, links, step, _ = parts[0].shape
    share = outs[0].shape[0]
    sums_ref[...] = jnp.zeros_like(sums_ref)

    def one(row, carry):
        target = target_ref[row]
        for link in range(links):
            slot = slot_ref[row, link]
            for offset, part in enumerate(parts):
                sums_ref[target, slot, offset * step : (offset + 1) * step, :] += part[row, link]
        return carry

    lax.fori_loop(0, rows, one, 0, unroll=True)
    for way, out in enumerate(outs):
        out[...] = sums_ref[way * share : (way + 1) * share]


def place_kernel(x_count, place_ref, *refs):
    pieces, out = refs[:-1], refs[-1]
    part = out.shape[2] // x_count
    chunks = len(pieces) // x_count
    for offset in range(x_count):
        start = lax.rem(place_ref[0] + x_count - offset, x_count) * part
        for piece in pieces[offset * chunks : (offset + 1) * chunks]:
            step = piece.shape[2]
            out[:, :, pl.ds(pl.multiple_of(start, 8), step), :] = piece[...]
            start = start + step


def place_one(pieces, place, x_count):
    rows, links, _, size = pieces[0].shape
    return pl.pallas_call(
        functools.partial(place_kernel, x_count),
        out_shape=jax.ShapeDtypeStruct((rows, links, size, size), jnp.float32),
        grid_spec=pltpu.PrefetchScalarGridSpec(
            num_scalar_prefetch=1,
            grid=(rows,),
            in_specs=[
                pl.BlockSpec((1, links, piece.shape[2], size), lambda e, *_: (e, 0, 0, 0))
                for piece in pieces
            ],
            out_specs=pl.BlockSpec((1, links, size, size), lambda e, *_: (e, 0, 0, 0)),
        ),
        compiler_params=pltpu.CompilerParams(vmem_limit_bytes=vmem_limit),
        cost_estimate=pl.CostEstimate(
            flops=0, bytes_accessed=8 * rows * links * size**2, transcendentals=0
        ),
        name="place_one",
    )(place, *pieces)


def last_kernel(x_count, peers, place_ref, prolong_ref, *refs):
    pieces, (out, left_ref, right_ref, sums_ref) = refs[:-4], refs[-4:]
    links, size = out.shape[1], out.shape[2]
    part = size // x_count

    @pl.when(pl.program_id(0) == 0)
    def _():
        load_weights(prolong_ref, left_ref, right_ref)

    done = 0
    for first in range(0, len(pieces), peers):
        total = pieces[first][...]
        for piece in pieces[first + 1 : first + peers]:
            total = total + piece[...]
        step = total.shape[2] // x_count
        for offset in range(x_count):
            start = lax.rem(place_ref[0] + x_count - offset, x_count) * part
            at = pl.multiple_of(start + done, 8)
            sums_ref[:, :, pl.ds(at, step), :] = total[:, :, offset * step : (offset + 1) * step, :]
        done += step
    sums = [sums_ref[row, slot] for row in range(out.shape[0]) for slot in range(links)]
    out[...] = triple(sums, left_ref, right_ref).reshape(out.shape)


def last(pieces, prolong_two, place, x_count, peers):
    rows, links, _, size = pieces[0].shape
    held = max(h for h in range(1, rows_a_step // 2 + 1) if rows % h == 0)
    return pl.pallas_call(
        functools.partial(last_kernel, x_count, peers),
        out_shape=jax.ShapeDtypeStruct((rows, links, size, size), jnp.float32),
        grid_spec=pltpu.PrefetchScalarGridSpec(
            num_scalar_prefetch=1,
            grid=(rows // held,),
            in_specs=[pl.BlockSpec((size, size), lambda e, *_: (0, 0))]
            + [
                pl.BlockSpec((held, links, piece.shape[2], size), lambda e, *_: (e, 0, 0, 0))
                for piece in pieces
            ],
            out_specs=pl.BlockSpec((held, links, size, size), lambda e, *_: (e, 0, 0, 0)),
            scratch_shapes=[
                pltpu.VMEM((2 * size, 2 * size), jnp.bfloat16),
                pltpu.VMEM((2 * size, 2 * size), jnp.bfloat16),
                pltpu.VMEM((held, links, size, size), jnp.float32),
            ],
        ),
        compiler_params=pltpu.CompilerParams(vmem_limit_bytes=vmem_limit),
        cost_estimate=pl.CostEstimate(
            flops=16 * rows * links * size**3,
            bytes_accessed=4 * rows * links * size**2 * (peers + 1),
            transcendentals=0,
        ),
        name="last",
    )(place, prolong_two, *pieces)


def sweep(fine_blocks, neighbours, diag_inverse, right_side, initial_guess):
    rows = fine_blocks.shape[0]
    axes = ("group", "member")
    devices = lax.axis_size(axes)
    device = lax.axis_index(axes)
    before = lax.ppermute(initial_guess, axes, [(i, (i + 1) % devices) for i in range(devices)])
    after = lax.ppermute(initial_guess, axes, [(i, (i - 1) % devices) for i in range(devices)])
    window = jnp.concatenate([before, initial_guess, after], axis=0)
    position = (neighbours - device * rows + rows) % (rows * devices)
    nearby = window[position]
    product = jnp.sum(fine_blocks * nearby[:, :, None, :], axis=(1, 3))
    defect = right_side - product
    return initial_guess + damping * jnp.sum(diag_inverse * defect[:, None, :], axis=2)


def local(
    fine_blocks,
    neighbours,
    slot_one,
    pair_one,
    prolong_one,
    slot_two,
    pair_two,
    prolong_two,
    diag_inverse,
    right_side,
    initial_guess,
):
    rows, links, size, _ = fine_blocks.shape
    rows_one, rows_two = rows // 2, rows // 4
    members, groups = lax.axis_size("member"), lax.axis_size("group")
    z_count, x_count = grid_of(members)
    half = z_count // 2
    part = size // x_count
    steps = chunk_steps(part)

    member = lax.axis_index("member")
    z, x = member // x_count, member % x_count
    upper = (z >= half).astype(jnp.int32)
    place = jnp.stack([x]).astype(jnp.int32)

    def at(side, d, x_at):
        return (half + d if side else half - 1 - d) * x_count + x_at % x_count

    def hop(array, d_from, d_to, offset):
        pairs = [
            (at(side, d_from, x_at), at(side, d_to, x_at + offset))
            for side in range(2)
            for x_at in range(x_count)
        ]
        return lax.ppermute(array, "member", pairs)

    def hop_x(array, offset):
        pairs = [
            (z_at * x_count + x_at, z_at * x_count + (x_at + offset) % x_count)
            for z_at in range(z_count)
            for x_at in range(x_count)
        ]
        return lax.ppermute(array, "member", pairs)

    routes = [(d, o) for d in range(half) for o in range(x_count)]

    def along(arrays):
        return [array if o == 0 else hop_x(array, o) for o, array in enumerate(arrays)]

    def inward(arrays):
        return arrays + [hop(array, d, 0, 0) for d in range(1, half) for array in arrays]

    tags = jnp.stack(along([pair_one] * x_count))
    slot_one, tags = lax.optimization_barrier((slot_one, tags))
    owner_rows = jnp.concatenate([tags] + [hop(tags, d, 0, 0) for d in range(1, half)])
    owner = owner_rows // rows_one % members
    owner_z, owner_x = owner // x_count, owner % x_count
    owner_upper = (owner_z >= half).astype(jnp.int32)
    owner_d = jnp.where(owner_upper > 0, owner_z - half, half - 1 - owner_z)
    near = (owner_upper == upper).astype(jnp.int32)
    target_one = ((near * half + owner_d) * x_count + (owner_x - x + x_count) % x_count) * rows_one
    target_one = (target_one + owner_rows % rows_one).astype(jnp.int32)
    middle = jnp.stack([(z == half - 1) | (z == half)]).astype(jnp.int32)

    way = (pair_two // rows_two // members - lax.axis_index("group") + groups) % groups
    target_two = (way * rows_two + pair_two % rows_two).astype(jnp.int32)

    outgoing = prepare(fine_blocks, slot_one, prolong_one, place, x_count, steps)
    across = [(at(0, 0, x_at), at(1, 0, x_at)) for x_at in range(x_count)]
    across = across + [(b, a) for a, b in across]
    smoothed = sweep(fine_blocks, neighbours, diag_inverse, right_side, initial_guess)
    before = [smoothed]

    def in_turn(kernel, scalars, arrays, out_shapes, name, **more):
        arrays, before[0] = lax.optimization_barrier((list(arrays), before[0]))
        outs = whole(kernel, scalars, arrays, out_shapes, name, **more)
        before[0] = outs[0]
        return outs

    def rows_of(count, height):
        return jax.ShapeDtypeStruct((count, links, height, size), jnp.float32)

    coming, targets = [], [target_one]
    for chunk in range(len(steps)):
        own = outgoing[0][chunk]
        if chunk > 0:
            ahead = coming[-1]
            tied = (own, ahead[x_count], targets[0]) if chunk == 1 else (own, ahead[x_count])
            own, ahead[x_count], *seen = lax.optimization_barrier(tied)
            targets += seen
        coming.append(inward(along([own] + [ways[chunk] for ways in outgoing[1:]])))
    received = []

    def combine(chunk):
        held = coming[chunk]
        total = half * x_count * rows_one
        far, kept = in_turn(
            functools.partial(combine_kernel, len(held)),
            [targets[min(chunk, 1)]],
            held,
            [rows_of(total, steps[chunk]), rows_of(2 * total, steps[chunk])],
            "combine",
            work=beside,
        )
        return kept, lax.ppermute(far, "member", across)

    def finish(chunk, sums):
        if chunk + 2 < len(steps):
            ahead = coming[chunk + 2]
            ahead[x_count], sums = lax.optimization_barrier((ahead[x_count], sums))
        finished = in_turn(
            finish_kernel,
            [middle],
            sums,
            [rows_of(x_count * rows_one, steps[chunk])] * (half - 1)
            + [rows_of(rows_one, steps[chunk])] * x_count,
            "finish",
        )
        return list(finished[half - 1 :]) + [hop(finished[d - 1], 0, d, 0) for d in range(1, half)]

    def settle(chunk, finished):
        return along(
            in_turn(
                functools.partial(settle_kernel, x_count),
                [],
                finished,
                [rows_of(rows_one, steps[chunk])] * x_count,
                "settle",
            )
        )

    def second(chunk, ours):
        received[-groups:], ours = lax.optimization_barrier((received[-groups:], ours))
        height = x_count * steps[chunk]
        shares = in_turn(
            functools.partial(second_kernel, x_count),
            [slot_two, target_two],
            ours,
            [rows_of(rows_two, height)] * groups,
            "second",
            scratch=[pltpu.VMEM((groups * rows_two, links, height, size), jnp.float32)],
        )
        for way, share in enumerate(shares):
            around = [(g, (g + way) % groups) for g in range(groups)]
            received.append(lax.ppermute(share, "group", around) if way > 0 else share)
        return ours

    stages, delays = (combine, finish, settle, second), (0, 1, 2, 2)
    order = [(stage, delays[stage]) for stage in (0, 2, 1, 3)]
    held = [[None] * len(steps) for _ in range(len(stages) + 1)]
    for turn in range(len(steps) + delays[-1]):
        for stage, delay in order:
            chunk = turn - delay
            if 0 <= chunk < len(steps):
                given = [held[stage][chunk]] if stage > 0 else []
                held[stage + 1][chunk] = stages[stage](chunk, *given)
    parts = held[4]

    coarse_one = place_one(
        [parts[chunk][o] for o in range(x_count) for chunk in range(len(steps))], place, x_count
    )
    coarse_two = last(received, prolong_two, place, x_count, groups)
    return (coarse_one, coarse_two, smoothed)


def solution(mesh):
    rows = P(("group", "member"))
    return jax.shard_map(
        local,
        mesh=mesh,
        in_specs=(rows, rows, rows, rows, P(), rows, rows, P(), rows, rows, rows),
        out_specs=(rows, rows, rows),
        check_vma=False,
    )
```

```python
import functools

import jax
import jax.numpy as jnp
from jax import lax
from jax.experimental import pallas as pl
from jax.experimental.pallas import tpu as pltpu
from jax.sharding import PartitionSpec as P

damping = 0.7
rows_a_step = 4
prepare_limit = 48 * 1024 * 1024
vmem_limit = 20 * 1024 * 1024
pause = 5
beside = 6


def grid_of(member_count):
    x_count = max(d for d in range(1, member_count + 1) if member_count % d == 0 and d * d <= member_count)
    return member_count // x_count, x_count


def chunk_steps(part):
    tiles = part // 8
    step = max(tiles // 4, 1)
    ends = [max(step // 2, 1)] * min(2, tiles)
    inner = tiles - sum(ends)
    steps = ends[:1] + [step] * (inner // step) + [inner % step] * (inner % step > 0) + ends[1:]
    return [8 * step for step in steps]


def split(values):
    high = values.astype(jnp.bfloat16)
    low = (values - high.astype(jnp.float32)).astype(jnp.bfloat16)
    return high, low


def load_weights(prolong_ref, left_ref, right_ref):
    prolong = prolong_ref[...]
    size = prolong.shape[0]
    high, low = split(prolong)
    high_t, low_t = split(prolong.T)
    for half in range(2):
        at = pl.ds(half * size, size)
        left_ref[0:size, at] = high_t
        left_ref[size : 2 * size, at] = low_t
        right_ref[at, 0:size] = high
        right_ref[at, size : 2 * size] = low


def triple(blocks, left_ref, right_ref):
    size = blocks[0].shape[0]
    count = len(blocks)
    high, low = split(jnp.concatenate(blocks, axis=1))
    both = jnp.dot(
        left_ref[...], jnp.concatenate([high, low], axis=0), preferred_element_type=jnp.float32
    )
    left = both[:size] + both[size:]
    rows = jnp.concatenate([left[:, s * size : (s + 1) * size] for s in range(count)], axis=0)
    high, low = split(rows)
    both = jnp.dot(
        jnp.concatenate([high, low], axis=1), right_ref[...], preferred_element_type=jnp.float32
    )
    return (both[:, :size] + both[:, size:]).reshape(count, size, size)


def prepare_kernel(x_count, slot_ref, place_ref, prolong_ref, fine_ref, *rest):
    outs, (left_ref, right_ref, sums_ref, done_ref) = rest[:-4], rest[-4:]
    held, links, size, _ = fine_ref.shape
    chunks = len(outs) // x_count
    part = size // x_count

    @pl.when(pl.program_id(0) == 0)
    def _():
        load_weights(prolong_ref, left_ref, right_ref)

    sums_ref[...] = jnp.zeros_like(sums_ref)
    for row in range(held):
        for link in range(links):
            slot = slot_ref[pl.program_id(0) * held + row, link]
            sums_ref[row, slot] += fine_ref[row, link]
    sums = [sums_ref[row, slot] for row in range(held) for slot in range(links)]
    done_ref[...] = triple(sums, left_ref, right_ref).reshape(done_ref.shape)
    for offset in range(x_count):
        start = lax.rem(place_ref[0] + offset, x_count) * part
        for out in outs[offset * chunks : (offset + 1) * chunks]:
            step = out.shape[2]
            out[...] = done_ref[:, :, pl.ds(pl.multiple_of(start, 8), step), :]
            start = start + step


def prepare(fine_blocks, slot_one, prolong_one, place, x_count, steps):
    rows, links, size, _ = fine_blocks.shape
    chunks = len(steps)
    held = max(h for h in range(1, rows_a_step + 1) if rows % h == 0)
    outs = pl.pallas_call(
        functools.partial(prepare_kernel, x_count),
        out_shape=[jax.ShapeDtypeStruct((rows, links, step, size), jnp.float32) for step in steps]
        * x_count,
        grid_spec=pltpu.PrefetchScalarGridSpec(
            num_scalar_prefetch=2,
            grid=(rows // held,),
            in_specs=[
                pl.BlockSpec((size, size), lambda e, *_: (0, 0)),
                pl.BlockSpec((held, links, size, size), lambda e, *_: (e, 0, 0, 0)),
            ],
            out_specs=[
                pl.BlockSpec((held, links, step, size), lambda e, *_: (e, 0, 0, 0)) for step in steps
            ]
            * x_count,
            scratch_shapes=[
                pltpu.VMEM((2 * size, 2 * size), jnp.bfloat16),
                pltpu.VMEM((2 * size, 2 * size), jnp.bfloat16),
                pltpu.VMEM((held, links, size, size), jnp.float32),
                pltpu.VMEM((held, links, size, size), jnp.float32),
            ],
        ),
        compiler_params=pltpu.CompilerParams(vmem_limit_bytes=prepare_limit),
        cost_estimate=pl.CostEstimate(
            flops=16 * rows * links * size**3,
            bytes_accessed=8 * rows * links * size**2,
            transcendentals=0,
        ),
        name="prepare",
    )(slot_one, place, prolong_one, fine_blocks)
    return [list(outs[offset * chunks : (offset + 1) * chunks]) for offset in range(x_count)]


def whole(kernel, scalars, arrays, out_shapes, name, work=0, scratch=()):
    return pl.pallas_call(
        kernel,
        out_shape=out_shapes,
        in_specs=[pl.BlockSpec(memory_space=pltpu.SMEM)] * len(scalars)
        + [pl.BlockSpec(memory_space=pltpu.VMEM)] * len(arrays),
        out_specs=[pl.BlockSpec(memory_space=pltpu.VMEM)] * len(out_shapes),
        scratch_shapes=scratch,
        compiler_params=pltpu.CompilerParams(vmem_limit_bytes=vmem_limit),
        cost_estimate=pl.CostEstimate(flops=work * 10**9, bytes_accessed=0, transcendentals=0),
        name=name,
    )(*scalars, *arrays)


def combine_kernel(sources, target_ref, *refs):
    arrays, (far_ref, sums_ref) = refs[:sources], refs[sources:]
    rows = arrays[0].shape[0]
    sums_ref[...] = jnp.zeros_like(sums_ref)
    for source in range(sources):

        def one(row, carry, source=source):
            sums_ref[target_ref[source, row]] += arrays[source][row]
            return carry

        lax.fori_loop(0, rows, one, 0, unroll=True)
    far_ref[...] = sums_ref[0 : far_ref.shape[0]]


def finish_kernel(middle_ref, sums_ref, got_ref, *outs):
    half, rows = got_ref.shape[0], outs[-1].shape[0]
    own = len([out for out in outs if out.shape[0] == rows])
    far, near = outs[:-own], outs[-own:]
    width = own * rows
    for d, out in enumerate(far):
        at = (d + 1) * width
        out[...] = sums_ref[half + at : half + at + width] + got_ref[at : at + width]
    for offset, out in enumerate(near):
        at = offset * rows
        total = sums_ref[half + at : half + at + rows] + got_ref[at : at + rows]
        out[...] = jnp.where(middle_ref[0] > 0, total, 0.0)


def settle_kernel(count, *refs):
    near, far, outs = refs[:count], refs[count:-count], refs[-count:]
    rows = outs[0].shape[0]
    for offset, out in enumerate(outs):
        total = near[offset][...]
        for piece in far:
            total = total + piece[offset * rows : (offset + 1) * rows]
        out[...] = total


def second_kernel(x_count, slot_ref, target_ref, *refs):
    parts, outs, sums_ref = refs[:x_count], refs[x_count:-1], refs[-1]
    rows, links, step, _ = parts[0].shape
    share = outs[0].shape[0]
    sums_ref[...] = jnp.zeros_like(sums_ref)

    def one(row, carry):
        target = target_ref[row]
        for link in range(links):
            slot = slot_ref[row, link]
            for offset, part in enumerate(parts):
                sums_ref[target, slot, offset * step : (offset + 1) * step, :] += part[row, link]
        return carry

    lax.fori_loop(0, rows, one, 0, unroll=True)
    for way, out in enumerate(outs):
        out[...] = sums_ref[way * share : (way + 1) * share]


def place_kernel(x_count, place_ref, *refs):
    pieces, out = refs[:-1], refs[-1]
    part = out.shape[2] // x_count
    chunks = len(pieces) // x_count
    for offset in range(x_count):
        start = lax.rem(place_ref[0] + x_count - offset, x_count) * part
        for piece in pieces[offset * chunks : (offset + 1) * chunks]:
            step = piece.shape[2]
            out[:, :, pl.ds(pl.multiple_of(start, 8), step), :] = piece[...]
            start = start + step


def place_one(pieces, place, x_count):
    rows, links, _, size = pieces[0].shape
    return pl.pallas_call(
        functools.partial(place_kernel, x_count),
        out_shape=jax.ShapeDtypeStruct((rows, links, size, size), jnp.float32),
        grid_spec=pltpu.PrefetchScalarGridSpec(
            num_scalar_prefetch=1,
            grid=(rows,),
            in_specs=[
                pl.BlockSpec((1, links, piece.shape[2], size), lambda e, *_: (e, 0, 0, 0))
                for piece in pieces
            ],
            out_specs=pl.BlockSpec((1, links, size, size), lambda e, *_: (e, 0, 0, 0)),
        ),
        compiler_params=pltpu.CompilerParams(vmem_limit_bytes=vmem_limit),
        cost_estimate=pl.CostEstimate(
            flops=0, bytes_accessed=8 * rows * links * size**2, transcendentals=0
        ),
        name="place_one",
    )(place, *pieces)


def last_kernel(x_count, peers, place_ref, prolong_ref, *refs):
    pieces, (out, left_ref, right_ref, sums_ref) = refs[:-4], refs[-4:]
    links, size = out.shape[1], out.shape[2]
    part = size // x_count

    @pl.when(pl.program_id(0) == 0)
    def _():
        load_weights(prolong_ref, left_ref, right_ref)

    done = 0
    for first in range(0, len(pieces), peers):
        total = pieces[first][...]
        for piece in pieces[first + 1 : first + peers]:
            total = total + piece[...]
        step = total.shape[2] // x_count
        for offset in range(x_count):
            start = lax.rem(place_ref[0] + x_count - offset, x_count) * part
            at = pl.multiple_of(start + done, 8)
            sums_ref[:, :, pl.ds(at, step), :] = total[:, :, offset * step : (offset + 1) * step, :]
        done += step
    sums = [sums_ref[row, slot] for row in range(out.shape[0]) for slot in range(links)]
    out[...] = triple(sums, left_ref, right_ref).reshape(out.shape)


def last(pieces, prolong_two, place, x_count, peers):
    rows = pieces[-1][0].shape[0]
    links, size = pieces[0][0].shape[1], pieces[0][0].shape[3]
    held = max(h for h in range(1, rows_a_step // 2 + 1) if rows % h == 0)

    def block(piece, first):
        return pl.BlockSpec(
            (held, links, piece.shape[2], size), lambda e, *_: (first // held + e, 0, 0, 0)
        )

    return pl.pallas_call(
        functools.partial(last_kernel, x_count, peers),
        out_shape=jax.ShapeDtypeStruct((rows, links, size, size), jnp.float32),
        grid_spec=pltpu.PrefetchScalarGridSpec(
            num_scalar_prefetch=1,
            grid=(rows // held,),
            in_specs=[pl.BlockSpec((size, size), lambda e, *_: (0, 0))]
            + [block(*piece) for piece in pieces],
            out_specs=pl.BlockSpec((held, links, size, size), lambda e, *_: (e, 0, 0, 0)),
            scratch_shapes=[
                pltpu.VMEM((2 * size, 2 * size), jnp.bfloat16),
                pltpu.VMEM((2 * size, 2 * size), jnp.bfloat16),
                pltpu.VMEM((held, links, size, size), jnp.float32),
            ],
        ),
        compiler_params=pltpu.CompilerParams(vmem_limit_bytes=vmem_limit),
        cost_estimate=pl.CostEstimate(
            flops=16 * rows * links * size**3,
            bytes_accessed=4 * rows * links * size**2 * (peers + 1),
            transcendentals=0,
        ),
        name="last",
    )(place, prolong_two, *[piece for piece, _ in pieces])


def sweep(fine_blocks, neighbours, diag_inverse, right_side, initial_guess):
    rows = fine_blocks.shape[0]
    axes = ("group", "member")
    devices = lax.axis_size(axes)
    device = lax.axis_index(axes)
    before = lax.ppermute(initial_guess, axes, [(i, (i + 1) % devices) for i in range(devices)])
    after = lax.ppermute(initial_guess, axes, [(i, (i - 1) % devices) for i in range(devices)])
    window = jnp.concatenate([before, initial_guess, after], axis=0)
    position = (neighbours - device * rows + rows) % (rows * devices)
    nearby = window[position]
    product = jnp.sum(fine_blocks * nearby[:, :, None, :], axis=(1, 3))
    defect = right_side - product
    return initial_guess + damping * jnp.sum(diag_inverse * defect[:, None, :], axis=2)


def local(
    fine_blocks,
    neighbours,
    slot_one,
    pair_one,
    prolong_one,
    slot_two,
    pair_two,
    prolong_two,
    diag_inverse,
    right_side,
    initial_guess,
):
    rows, links, size, _ = fine_blocks.shape
    rows_one, rows_two = rows // 2, rows // 4
    members, groups = lax.axis_size("member"), lax.axis_size("group")
    z_count, x_count = grid_of(members)
    half = z_count // 2
    part = size // x_count
    steps = chunk_steps(part)

    member = lax.axis_index("member")
    z, x = member // x_count, member % x_count
    upper = (z >= half).astype(jnp.int32)
    place = jnp.stack([x]).astype(jnp.int32)

    def at(side, d, x_at):
        return (half + d if side else half - 1 - d) * x_count + x_at % x_count

    def hop(array, d_from, d_to, offset):
        pairs = [
            (at(side, d_from, x_at), at(side, d_to, x_at + offset))
            for side in range(2)
            for x_at in range(x_count)
        ]
        return lax.ppermute(array, "member", pairs)

    def hop_x(array, offset):
        pairs = [
            (z_at * x_count + x_at, z_at * x_count + (x_at + offset) % x_count)
            for z_at in range(z_count)
            for x_at in range(x_count)
        ]
        return lax.ppermute(array, "member", pairs)

    routes = [(d, o) for d in range(half) for o in range(x_count)]

    def along(arrays):
        return [array if o == 0 else hop_x(array, o) for o, array in enumerate(arrays)]

    def inward(arrays):
        return arrays + [hop(array, d, 0, 0) for d in range(1, half) for array in arrays]

    tags = jnp.stack(along([pair_one] * x_count))
    slot_one, tags = lax.optimization_barrier((slot_one, tags))
    owner_rows = jnp.concatenate([tags] + [hop(tags, d, 0, 0) for d in range(1, half)])
    owner = owner_rows // rows_one % members
    owner_z, owner_x = owner // x_count, owner % x_count
    owner_upper = (owner_z >= half).astype(jnp.int32)
    owner_d = jnp.where(owner_upper > 0, owner_z - half, half - 1 - owner_z)
    near = (owner_upper == upper).astype(jnp.int32)
    target_one = ((near * half + owner_d) * x_count + (owner_x - x + x_count) % x_count) * rows_one
    target_one = (target_one + owner_rows % rows_one).astype(jnp.int32)
    middle = jnp.stack([(z == half - 1) | (z == half)]).astype(jnp.int32)

    to_group = pair_two // rows_two // members
    target_two = (to_group * rows_two + pair_two % rows_two).astype(jnp.int32)
    way = (to_group - lax.axis_index("group") + groups) % groups
    target_way = (way * rows_two + pair_two % rows_two).astype(jnp.int32)

    outgoing = prepare(fine_blocks, slot_one, prolong_one, place, x_count, steps)
    across = [(at(0, 0, x_at), at(1, 0, x_at)) for x_at in range(x_count)]
    across = across + [(b, a) for a, b in across]
    before = [target_one]

    def in_turn(kernel, scalars, arrays, out_shapes, name, **more):
        arrays, before[0] = lax.optimization_barrier((list(arrays), before[0]))
        outs = whole(kernel, scalars, arrays, out_shapes, name, **more)
        before[0] = outs[0]
        return outs

    def rows_of(count, height):
        return jax.ShapeDtypeStruct((count, links, height, size), jnp.float32)

    coming, targets = [], [target_one]
    for chunk in range(len(steps)):
        own = outgoing[0][chunk]
        if chunk > 0:
            ahead = coming[-1]
            tied = (own, ahead[x_count], targets[0]) if chunk == 1 else (own, ahead[x_count])
            own, ahead[x_count], *seen = lax.optimization_barrier(tied)
            targets += seen
        coming.append(inward(along([own] + [ways[chunk] for ways in outgoing[1:]])))
    received = []

    smoothed = []

    def combine(chunk):
        held = coming[chunk]
        if chunk == min(1, len(steps) - 1):
            later, before[0] = lax.optimization_barrier((neighbours, before[0]))
            swept = sweep(fine_blocks, later, diag_inverse, right_side, initial_guess)
            held, swept = lax.optimization_barrier((held, swept))
            smoothed.append(swept)
        total = half * x_count * rows_one
        far, kept = in_turn(
            functools.partial(combine_kernel, len(held)),
            [targets[min(chunk, 1)]],
            held,
            [rows_of(total, steps[chunk]), rows_of(2 * total, steps[chunk])],
            "combine",
            work=beside,
        )
        return kept, lax.ppermute(far, "member", across)

    def finish(chunk, sums):
        finished = in_turn(
            finish_kernel,
            [middle],
            sums,
            [rows_of(x_count * rows_one, steps[chunk])] * (half - 1)
            + [rows_of(rows_one, steps[chunk])] * x_count,
            "finish",
        )
        return list(finished[half - 1 :]) + [hop(finished[d - 1], 0, d, 0) for d in range(1, half)]

    def settle(chunk, finished):
        return along(
            in_turn(
                functools.partial(settle_kernel, x_count),
                [],
                finished,
                [rows_of(rows_one, steps[chunk])] * x_count,
                "settle",
            )
        )

    def second(chunk, ours):
        height = x_count * steps[chunk]
        final = chunk == len(steps) - 1
        shares = in_turn(
            functools.partial(second_kernel, x_count),
            [slot_two, target_way if final else target_two],
            ours,
            [rows_of(rows_two, height)] * groups if final else [rows_of(groups * rows_two, height)],
            "second",
            scratch=[pltpu.VMEM((groups * rows_two, links, height, size), jnp.float32)],
        )
        if final:
            for way, share in enumerate(shares):
                around = [(g, (g + way) % groups) for g in range(groups)]
                received.append((lax.ppermute(share, "group", around) if way > 0 else share, 0))
        else:
            sent = lax.all_to_all(shares[0], "group", 0, 0, tiled=True)
            received.extend((sent, g * rows_two) for g in range(groups))
        return ours

    stages, shares = (combine, finish, settle, second), (1.0, 0.5, 0.25)
    turns, rows_in, swapped = [], 0.0, 0.0
    for chunk, step in enumerate(steps):
        rows_in += step
        time = swapped = max(rows_in, swapped) + step + pause
        turns += [(rows_in, 0, chunk), (time, 1, chunk)]
        for stage, share in enumerate(shares[1:], 2):
            time += share * step + pause
            turns.append((time, stage, chunk))
    held = [[None] * len(steps) for _ in range(len(stages) + 1)]
    for _, stage, chunk in sorted(turns):
        given = [held[stage][chunk]] if stage > 0 else []
        held[stage + 1][chunk] = stages[stage](chunk, *given)
    parts = held[4]

    coarse_one = place_one(
        [parts[chunk][o] for o in range(x_count) for chunk in range(len(steps))], place, x_count
    )
    coarse_two = last(received, prolong_two, place, x_count, groups)
    return (coarse_one, coarse_two, smoothed[0])


def solution(mesh):
    rows = P(("group", "member"))
    return jax.shard_map(
        local,
        mesh=mesh,
        in_specs=(rows, rows, rows, rows, P(), rows, rows, P(), rows, rows, rows),
        out_specs=(rows, rows, rows),
        check_vma=False,
    )
```

```python
import functools

import jax
import jax.numpy as jnp
from jax import lax
from jax.experimental import pallas as pl
from jax.experimental.pallas import tpu as pltpu
from jax.sharding import PartitionSpec as P

damping = 0.7
rows_a_step = 4
prepare_limit = 20 * 1024 * 1024
vmem_limit = 20 * 1024 * 1024
pause = 3
beside = 6


def grid_of(member_count):
    x_count = max(d for d in range(1, member_count + 1) if member_count % d == 0 and d * d <= member_count)
    return member_count // x_count, x_count


def chunk_steps(part):
    tiles = part // 8
    step = max(tiles // 4, 1)
    ends = [max(step // 2, 1)] * min(2, tiles)
    inner = tiles - sum(ends)
    steps = ends[:1] + [step] * (inner // step) + [inner % step] * (inner % step > 0) + ends[1:]
    return [8 * step for step in steps]


def split(values):
    high = values.astype(jnp.bfloat16)
    low = (values - high.astype(jnp.float32)).astype(jnp.bfloat16)
    return high, low


def load_weights(prolong_ref, left_ref, right_ref):
    prolong = prolong_ref[...]
    size = prolong.shape[0]
    high, low = split(prolong)
    high_t, low_t = split(prolong.T)
    for half in range(2):
        at = pl.ds(half * size, size)
        left_ref[0:size, at] = high_t
        left_ref[size : 2 * size, at] = low_t
        right_ref[at, 0:size] = high
        right_ref[at, size : 2 * size] = low


def triple(blocks, left_ref, right_ref):
    size = blocks[0].shape[0]
    count = len(blocks)
    high, low = split(jnp.concatenate(blocks, axis=1))
    both = jnp.dot(
        left_ref[...], jnp.concatenate([high, low], axis=0), preferred_element_type=jnp.float32
    )
    left = both[:size] + both[size:]
    rows = jnp.concatenate([left[:, s * size : (s + 1) * size] for s in range(count)], axis=0)
    high, low = split(rows)
    both = jnp.dot(
        jnp.concatenate([high, low], axis=1), right_ref[...], preferred_element_type=jnp.float32
    )
    return (both[:, :size] + both[:, size:]).reshape(count, size, size)


def prepare_kernel(x_count, slot_ref, place_ref, prolong_ref, fine_ref, *rest):
    outs, (left_ref, right_ref, sums_ref, done_ref) = rest[:-4], rest[-4:]
    held, links, size, _ = fine_ref.shape
    chunks = len(outs) // x_count
    part = size // x_count

    @pl.when(pl.program_id(0) == 0)
    def _():
        load_weights(prolong_ref, left_ref, right_ref)

    sums_ref[...] = jnp.zeros_like(sums_ref)
    for row in range(held):
        for link in range(links):
            slot = slot_ref[pl.program_id(0) * held + row, link]
            sums_ref[row, slot] += fine_ref[row, link]
    sums = [sums_ref[row, slot] for row in range(held) for slot in range(links)]
    done_ref[...] = triple(sums, left_ref, right_ref).reshape(done_ref.shape)
    for offset in range(x_count):
        start = lax.rem(place_ref[0] + offset, x_count) * part
        for out in outs[offset * chunks : (offset + 1) * chunks]:
            step = out.shape[2]
            out[...] = done_ref[:, :, pl.ds(pl.multiple_of(start, 8), step), :]
            start = start + step


def prepare(fine_blocks, slot_one, prolong_one, place, x_count, steps):
    rows, links, size, _ = fine_blocks.shape
    chunks = len(steps)
    held = max(h for h in range(1, rows_a_step + 1) if rows % h == 0)
    outs = pl.pallas_call(
        functools.partial(prepare_kernel, x_count),
        out_shape=[jax.ShapeDtypeStruct((rows, links, step, size), jnp.float32) for step in steps]
        * x_count,
        grid_spec=pltpu.PrefetchScalarGridSpec(
            num_scalar_prefetch=2,
            grid=(rows // held,),
            in_specs=[
                pl.BlockSpec((size, size), lambda e, *_: (0, 0)),
                pl.BlockSpec((held, links, size, size), lambda e, *_: (e, 0, 0, 0)),
            ],
            out_specs=[
                pl.BlockSpec((held, links, step, size), lambda e, *_: (e, 0, 0, 0)) for step in steps
            ]
            * x_count,
            scratch_shapes=[
                pltpu.VMEM((2 * size, 2 * size), jnp.bfloat16),
                pltpu.VMEM((2 * size, 2 * size), jnp.bfloat16),
                pltpu.VMEM((held, links, size, size), jnp.float32),
                pltpu.VMEM((held, links, size, size), jnp.float32),
            ],
        ),
        compiler_params=pltpu.CompilerParams(vmem_limit_bytes=prepare_limit),
        cost_estimate=pl.CostEstimate(
            flops=16 * rows * links * size**3,
            bytes_accessed=8 * rows * links * size**2,
            transcendentals=0,
        ),
        name="prepare",
    )(slot_one, place, prolong_one, fine_blocks)
    return [list(outs[offset * chunks : (offset + 1) * chunks]) for offset in range(x_count)]


def whole(kernel, scalars, arrays, out_shapes, name, work=0, scratch=()):
    return pl.pallas_call(
        kernel,
        out_shape=out_shapes,
        in_specs=[pl.BlockSpec(memory_space=pltpu.SMEM)] * len(scalars)
        + [pl.BlockSpec(memory_space=pltpu.VMEM)] * len(arrays),
        out_specs=[pl.BlockSpec(memory_space=pltpu.VMEM)] * len(out_shapes),
        scratch_shapes=scratch,
        compiler_params=pltpu.CompilerParams(vmem_limit_bytes=vmem_limit),
        cost_estimate=pl.CostEstimate(flops=work * 10**9, bytes_accessed=0, transcendentals=0),
        name=name,
    )(*scalars, *arrays)


def combine_kernel(sources, target_ref, *refs):
    arrays, (far_ref, sums_ref) = refs[:sources], refs[sources:]
    rows = arrays[0].shape[0]
    sums_ref[...] = jnp.zeros_like(sums_ref)
    for source in range(sources):

        def one(row, carry, source=source):
            sums_ref[target_ref[source, row]] += arrays[source][row]
            return carry

        lax.fori_loop(0, rows, one, 0, unroll=True)
    far_ref[...] = sums_ref[0 : far_ref.shape[0]]


def finish_kernel(middle_ref, sums_ref, got_ref, *outs):
    half, rows = got_ref.shape[0], outs[-1].shape[0]
    own = len([out for out in outs if out.shape[0] == rows])
    far, near = outs[:-own], outs[-own:]
    width = own * rows
    for d, out in enumerate(far):
        at = (d + 1) * width
        out[...] = sums_ref[half + at : half + at + width] + got_ref[at : at + width]
    for offset, out in enumerate(near):
        at = offset * rows
        total = sums_ref[half + at : half + at + rows] + got_ref[at : at + rows]
        out[...] = jnp.where(middle_ref[0] > 0, total, 0.0)


def settle_kernel(count, *refs):
    near, far, outs = refs[:count], refs[count:-count], refs[-count:]
    rows = outs[0].shape[0]
    for offset, out in enumerate(outs):
        total = near[offset][...]
        for piece in far:
            total = total + piece[offset * rows : (offset + 1) * rows]
        out[...] = total


def second_kernel(x_count, slot_ref, target_ref, *refs):
    parts, outs, sums_ref = refs[:x_count], refs[x_count:-1], refs[-1]
    rows, links, step, _ = parts[0].shape
    share = outs[0].shape[0]
    sums_ref[...] = jnp.zeros_like(sums_ref)

    def one(row, carry):
        target = target_ref[row]
        for link in range(links):
            slot = slot_ref[row, link]
            for offset, part in enumerate(parts):
                sums_ref[target, slot, offset * step : (offset + 1) * step, :] += part[row, link]
        return carry

    lax.fori_loop(0, rows, one, 0, unroll=True)
    for way, out in enumerate(outs):
        out[...] = sums_ref[way * share : (way + 1) * share]


def place_kernel(x_count, place_ref, *refs):
    pieces, out = refs[:-1], refs[-1]
    part = out.shape[2] // x_count
    chunks = len(pieces) // x_count
    for offset in range(x_count):
        start = lax.rem(place_ref[0] + x_count - offset, x_count) * part
        for piece in pieces[offset * chunks : (offset + 1) * chunks]:
            step = piece.shape[2]
            out[:, :, pl.ds(pl.multiple_of(start, 8), step), :] = piece[...]
            start = start + step


def place_one(pieces, place, x_count):
    rows, links, _, size = pieces[0].shape
    return pl.pallas_call(
        functools.partial(place_kernel, x_count),
        out_shape=jax.ShapeDtypeStruct((rows, links, size, size), jnp.float32),
        grid_spec=pltpu.PrefetchScalarGridSpec(
            num_scalar_prefetch=1,
            grid=(rows,),
            in_specs=[
                pl.BlockSpec((1, links, piece.shape[2], size), lambda e, *_: (e, 0, 0, 0))
                for piece in pieces
            ],
            out_specs=pl.BlockSpec((1, links, size, size), lambda e, *_: (e, 0, 0, 0)),
        ),
        compiler_params=pltpu.CompilerParams(vmem_limit_bytes=vmem_limit),
        cost_estimate=pl.CostEstimate(
            flops=0, bytes_accessed=8 * rows * links * size**2, transcendentals=0
        ),
        name="place_one",
    )(place, *pieces)


def last_kernel(x_count, peers, place_ref, prolong_ref, *refs):
    pieces, (out, left_ref, right_ref, sums_ref) = refs[:-4], refs[-4:]
    links, size = out.shape[1], out.shape[2]
    part = size // x_count

    @pl.when(pl.program_id(0) == 0)
    def _():
        load_weights(prolong_ref, left_ref, right_ref)

    done = 0
    for first in range(0, len(pieces), peers):
        total = pieces[first][...]
        for piece in pieces[first + 1 : first + peers]:
            total = total + piece[...]
        step = total.shape[2] // x_count
        for offset in range(x_count):
            start = lax.rem(place_ref[0] + x_count - offset, x_count) * part
            at = pl.multiple_of(start + done, 8)
            sums_ref[:, :, pl.ds(at, step), :] = total[:, :, offset * step : (offset + 1) * step, :]
        done += step
    sums = [sums_ref[row, slot] for row in range(out.shape[0]) for slot in range(links)]
    out[...] = triple(sums, left_ref, right_ref).reshape(out.shape)


def last(pieces, prolong_two, place, x_count, peers):
    rows, links, _, size = pieces[0].shape
    held = max(h for h in range(1, rows_a_step // 2 + 1) if rows % h == 0)
    return pl.pallas_call(
        functools.partial(last_kernel, x_count, peers),
        out_shape=jax.ShapeDtypeStruct((rows, links, size, size), jnp.float32),
        grid_spec=pltpu.PrefetchScalarGridSpec(
            num_scalar_prefetch=1,
            grid=(rows // held,),
            in_specs=[pl.BlockSpec((size, size), lambda e, *_: (0, 0))]
            + [
                pl.BlockSpec((held, links, piece.shape[2], size), lambda e, *_: (e, 0, 0, 0))
                for piece in pieces
            ],
            out_specs=pl.BlockSpec((held, links, size, size), lambda e, *_: (e, 0, 0, 0)),
            scratch_shapes=[
                pltpu.VMEM((2 * size, 2 * size), jnp.bfloat16),
                pltpu.VMEM((2 * size, 2 * size), jnp.bfloat16),
                pltpu.VMEM((held, links, size, size), jnp.float32),
            ],
        ),
        compiler_params=pltpu.CompilerParams(vmem_limit_bytes=vmem_limit),
        cost_estimate=pl.CostEstimate(
            flops=16 * rows * links * size**3,
            bytes_accessed=4 * rows * links * size**2 * (peers + 1),
            transcendentals=0,
        ),
        name="last",
    )(place, prolong_two, *pieces)


def sweep(fine_blocks, neighbours, diag_inverse, right_side, initial_guess):
    rows = fine_blocks.shape[0]
    axes = ("group", "member")
    devices = lax.axis_size(axes)
    device = lax.axis_index(axes)
    before = lax.ppermute(initial_guess, axes, [(i, (i + 1) % devices) for i in range(devices)])
    after = lax.ppermute(initial_guess, axes, [(i, (i - 1) % devices) for i in range(devices)])
    window = jnp.concatenate([before, initial_guess, after], axis=0)
    position = (neighbours - device * rows + rows) % (rows * devices)
    nearby = window[position]
    product = jnp.sum(fine_blocks * nearby[:, :, None, :], axis=(1, 3))
    defect = right_side - product
    return initial_guess + damping * jnp.sum(diag_inverse * defect[:, None, :], axis=2)


def local(
    fine_blocks,
    neighbours,
    slot_one,
    pair_one,
    prolong_one,
    slot_two,
    pair_two,
    prolong_two,
    diag_inverse,
    right_side,
    initial_guess,
):
    rows, links, size, _ = fine_blocks.shape
    rows_one, rows_two = rows // 2, rows // 4
    members, groups = lax.axis_size("member"), lax.axis_size("group")
    z_count, x_count = grid_of(members)
    half = z_count // 2
    part = size // x_count
    steps = chunk_steps(part)

    member = lax.axis_index("member")
    z, x = member // x_count, member % x_count
    upper = (z >= half).astype(jnp.int32)
    place = jnp.stack([x]).astype(jnp.int32)

    def at(side, d, x_at):
        return (half + d if side else half - 1 - d) * x_count + x_at % x_count

    def hop(array, d_from, d_to, offset):
        pairs = [
            (at(side, d_from, x_at), at(side, d_to, x_at + offset))
            for side in range(2)
            for x_at in range(x_count)
        ]
        return lax.ppermute(array, "member", pairs)

    def hop_x(array, offset):
        pairs = [
            (z_at * x_count + x_at, z_at * x_count + (x_at + offset) % x_count)
            for z_at in range(z_count)
            for x_at in range(x_count)
        ]
        return lax.ppermute(array, "member", pairs)

    routes = [(d, o) for d in range(half) for o in range(x_count)]

    def along(arrays):
        return [array if o == 0 else hop_x(array, o) for o, array in enumerate(arrays)]

    def inward(arrays):
        return arrays + [hop(array, d, 0, 0) for d in range(1, half) for array in arrays]

    tags = jnp.stack(along([pair_one] * x_count))
    slot_one, tags = lax.optimization_barrier((slot_one, tags))
    owner_rows = jnp.concatenate([tags] + [hop(tags, d, 0, 0) for d in range(1, half)])
    owner = owner_rows // rows_one % members
    owner_z, owner_x = owner // x_count, owner % x_count
    owner_upper = (owner_z >= half).astype(jnp.int32)
    owner_d = jnp.where(owner_upper > 0, owner_z - half, half - 1 - owner_z)
    near = (owner_upper == upper).astype(jnp.int32)
    target_one = ((near * half + owner_d) * x_count + (owner_x - x + x_count) % x_count) * rows_one
    target_one = (target_one + owner_rows % rows_one).astype(jnp.int32)
    middle = jnp.stack([(z == half - 1) | (z == half)]).astype(jnp.int32)

    way = (pair_two // rows_two // members - lax.axis_index("group") + groups) % groups
    target_two = (way * rows_two + pair_two % rows_two).astype(jnp.int32)

    outgoing = prepare(fine_blocks, slot_one, prolong_one, place, x_count, steps)
    across = [(at(0, 0, x_at), at(1, 0, x_at)) for x_at in range(x_count)]
    across = across + [(b, a) for a, b in across]
    before = [target_one]

    def in_turn(kernel, scalars, arrays, out_shapes, name, **more):
        arrays, before[0] = lax.optimization_barrier((list(arrays), before[0]))
        outs = whole(kernel, scalars, arrays, out_shapes, name, **more)
        before[0] = outs[0]
        return outs

    def rows_of(count, height):
        return jax.ShapeDtypeStruct((count, links, height, size), jnp.float32)

    coming, targets = [], [target_one]
    for chunk in range(len(steps)):
        own = outgoing[0][chunk]
        if chunk > 0:
            ahead = coming[-1]
            tied = (own, ahead[x_count], targets[0]) if chunk == 1 else (own, ahead[x_count])
            own, ahead[x_count], *seen = lax.optimization_barrier(tied)
            targets += seen
        coming.append(inward(along([own] + [ways[chunk] for ways in outgoing[1:]])))
    received = []

    smoothed = []

    def combine(chunk):
        held = coming[chunk]
        if chunk == min(1, len(steps) - 1):
            later, before[0] = lax.optimization_barrier((neighbours, before[0]))
            swept = sweep(fine_blocks, later, diag_inverse, right_side, initial_guess)
            held, swept = lax.optimization_barrier((held, swept))
            smoothed.append(swept)
        total = half * x_count * rows_one
        far, kept = in_turn(
            functools.partial(combine_kernel, len(held)),
            [targets[min(chunk, 1)]],
            held,
            [rows_of(total, steps[chunk]), rows_of(2 * total, steps[chunk])],
            "combine",
            work=beside,
        )
        return kept, lax.ppermute(far, "member", across)

    def finish(chunk, sums):
        finished = in_turn(
            finish_kernel,
            [middle],
            sums,
            [rows_of(x_count * rows_one, steps[chunk])] * (half - 1)
            + [rows_of(rows_one, steps[chunk])] * x_count,
            "finish",
        )
        return list(finished[half - 1 :]) + [hop(finished[d - 1], 0, d, 0) for d in range(1, half)]

    def settle(chunk, finished):
        return along(
            in_turn(
                functools.partial(settle_kernel, x_count),
                [],
                finished,
                [rows_of(rows_one, steps[chunk])] * x_count,
                "settle",
            )
        )

    def second(chunk, ours):
        received[-groups:], ours = lax.optimization_barrier((received[-groups:], ours))
        height = x_count * steps[chunk]
        shares = in_turn(
            functools.partial(second_kernel, x_count),
            [slot_two, target_two],
            ours,
            [rows_of(rows_two, height)] * groups,
            "second",
            scratch=[pltpu.VMEM((groups * rows_two, links, height, size), jnp.float32)],
        )
        for way, share in enumerate(shares):
            around = [(g, (g + way) % groups) for g in range(groups)]
            received.append(lax.ppermute(share, "group", around) if way > 0 else share)
        return ours

    stages, shares = (combine, finish, settle, second), (1.0, 0.5, 0.25)
    turns, rows_in, swapped = [], 0.0, 0.0
    for chunk, step in enumerate(steps):
        rows_in += step
        time = swapped = max(rows_in, swapped) + step + pause
        turns += [(rows_in, 0, chunk), (time, 1, chunk)]
        for stage, share in enumerate(shares[1:], 2):
            time += share * step + pause
            turns.append((time, stage, chunk))
    held = [[None] * len(steps) for _ in range(len(stages) + 1)]
    for _, stage, chunk in sorted(turns):
        given = [held[stage][chunk]] if stage > 0 else []
        held[stage + 1][chunk] = stages[stage](chunk, *given)
    parts = held[4]

    coarse_one = place_one(
        [parts[chunk][o] for o in range(x_count) for chunk in range(len(steps))], place, x_count
    )
    coarse_two = last(received, prolong_two, place, x_count, groups)
    return (coarse_one, coarse_two, smoothed[0])


def solution(mesh):
    rows = P(("group", "member"))
    return jax.shard_map(
        local,
        mesh=mesh,
        in_specs=(rows, rows, rows, rows, P(), rows, rows, P(), rows, rows, rows),
        out_specs=(rows, rows, rows),
        check_vma=False,
    )
```

```python
import functools

import jax
import jax.numpy as jnp
from jax import lax
from jax.experimental import pallas as pl
from jax.experimental.pallas import tpu as pltpu
from jax.sharding import PartitionSpec as P

damping = 0.7
rows_a_step = 4
prepare_limit = 20 * 1024 * 1024
vmem_limit = 20 * 1024 * 1024
pause = 3
beside = 6


def grid_of(member_count):
    x_count = max(d for d in range(1, member_count + 1) if member_count % d == 0 and d * d <= member_count)
    return member_count // x_count, x_count


def chunk_steps(part):
    tiles = part // 8
    step = max(tiles // 4, 1)
    ends = [max(step // 2, 1)] * min(2, tiles)
    inner = tiles - sum(ends)
    steps = ends[:1] + [step] * (inner // step) + [inner % step] * (inner % step > 0) + ends[1:]
    return [8 * step for step in steps]


def split(values):
    high = values.astype(jnp.bfloat16)
    low = (values - high.astype(jnp.float32)).astype(jnp.bfloat16)
    return high, low


def load_weights(prolong_ref, left_ref, right_ref):
    prolong = prolong_ref[...]
    size = prolong.shape[0]
    high, low = split(prolong)
    high_t, low_t = split(prolong.T)
    for half in range(2):
        at = pl.ds(half * size, size)
        left_ref[0:size, at] = high_t
        left_ref[size : 2 * size, at] = low_t
        right_ref[at, 0:size] = high
        right_ref[at, size : 2 * size] = low


def triple(blocks, left_ref, right_ref):
    size = blocks[0].shape[0]
    count = len(blocks)
    high, low = split(jnp.concatenate(blocks, axis=1))
    both = jnp.dot(
        left_ref[...], jnp.concatenate([high, low], axis=0), preferred_element_type=jnp.float32
    )
    left = both[:size] + both[size:]
    rows = jnp.concatenate([left[:, s * size : (s + 1) * size] for s in range(count)], axis=0)
    high, low = split(rows)
    both = jnp.dot(
        jnp.concatenate([high, low], axis=1), right_ref[...], preferred_element_type=jnp.float32
    )
    return (both[:, :size] + both[:, size:]).reshape(count, size, size)


def prepare_kernel(x_count, slot_ref, place_ref, prolong_ref, fine_ref, *rest):
    outs, (left_ref, right_ref, sums_ref, done_ref) = rest[:-4], rest[-4:]
    held, links, size, _ = fine_ref.shape
    chunks = len(outs) // x_count
    part = size // x_count

    @pl.when(pl.program_id(0) == 0)
    def _():
        load_weights(prolong_ref, left_ref, right_ref)

    sums_ref[...] = jnp.zeros_like(sums_ref)
    for row in range(held):
        for link in range(links):
            slot = slot_ref[pl.program_id(0) * held + row, link]
            sums_ref[row, slot] += fine_ref[row, link]
    sums = [sums_ref[row, slot] for row in range(held) for slot in range(links)]
    done_ref[...] = triple(sums, left_ref, right_ref).reshape(done_ref.shape)
    for offset in range(x_count):
        start = lax.rem(place_ref[0] + offset, x_count) * part
        for out in outs[offset * chunks : (offset + 1) * chunks]:
            step = out.shape[2]
            out[...] = done_ref[:, :, pl.ds(pl.multiple_of(start, 8), step), :]
            start = start + step


def prepare(fine_blocks, slot_one, prolong_one, place, x_count, steps):
    rows, links, size, _ = fine_blocks.shape
    chunks = len(steps)
    held = max(h for h in range(1, rows_a_step + 1) if rows % h == 0)
    outs = pl.pallas_call(
        functools.partial(prepare_kernel, x_count),
        out_shape=[jax.ShapeDtypeStruct((rows, links, step, size), jnp.float32) for step in steps]
        * x_count,
        grid_spec=pltpu.PrefetchScalarGridSpec(
            num_scalar_prefetch=2,
            grid=(rows // held,),
            in_specs=[
                pl.BlockSpec((size, size), lambda e, *_: (0, 0)),
                pl.BlockSpec((held, links, size, size), lambda e, *_: (e, 0, 0, 0)),
            ],
            out_specs=[
                pl.BlockSpec((held, links, step, size), lambda e, *_: (e, 0, 0, 0)) for step in steps
            ]
            * x_count,
            scratch_shapes=[
                pltpu.VMEM((2 * size, 2 * size), jnp.bfloat16),
                pltpu.VMEM((2 * size, 2 * size), jnp.bfloat16),
                pltpu.VMEM((held, links, size, size), jnp.float32),
                pltpu.VMEM((held, links, size, size), jnp.float32),
            ],
        ),
        compiler_params=pltpu.CompilerParams(vmem_limit_bytes=prepare_limit),
        cost_estimate=pl.CostEstimate(
            flops=16 * rows * links * size**3,
            bytes_accessed=8 * rows * links * size**2,
            transcendentals=0,
        ),
        name="prepare",
    )(slot_one, place, prolong_one, fine_blocks)
    return [list(outs[offset * chunks : (offset + 1) * chunks]) for offset in range(x_count)]


def whole(kernel, scalars, arrays, out_shapes, name, work=0, scratch=()):
    return pl.pallas_call(
        kernel,
        out_shape=out_shapes,
        in_specs=[pl.BlockSpec(memory_space=pltpu.SMEM)] * len(scalars)
        + [pl.BlockSpec(memory_space=pltpu.VMEM)] * len(arrays),
        out_specs=[pl.BlockSpec(memory_space=pltpu.VMEM)] * len(out_shapes),
        scratch_shapes=scratch,
        compiler_params=pltpu.CompilerParams(vmem_limit_bytes=vmem_limit),
        cost_estimate=pl.CostEstimate(flops=work * 10**9, bytes_accessed=0, transcendentals=0),
        name=name,
    )(*scalars, *arrays)


def combine_kernel(sources, target_ref, *refs):
    arrays, (far_ref, sums_ref) = refs[:sources], refs[sources:]
    rows = arrays[0].shape[0]
    sums_ref[...] = jnp.zeros_like(sums_ref)
    for source in range(sources):

        def one(row, carry, source=source):
            sums_ref[target_ref[source, row]] += arrays[source][row]
            return carry

        lax.fori_loop(0, rows, one, 0, unroll=True)
    far_ref[...] = sums_ref[0 : far_ref.shape[0]]


def finish_kernel(middle_ref, sums_ref, got_ref, *outs):
    half, rows = got_ref.shape[0], outs[-1].shape[0]
    own = len([out for out in outs if out.shape[0] == rows])
    far, near = outs[:-own], outs[-own:]
    width = own * rows
    for d, out in enumerate(far):
        at = (d + 1) * width
        out[...] = sums_ref[half + at : half + at + width] + got_ref[at : at + width]
    for offset, out in enumerate(near):
        at = offset * rows
        total = sums_ref[half + at : half + at + rows] + got_ref[at : at + rows]
        out[...] = jnp.where(middle_ref[0] > 0, total, 0.0)


def settle_kernel(count, *refs):
    near, far, outs = refs[:count], refs[count:-count], refs[-count:]
    rows = outs[0].shape[0]
    for offset, out in enumerate(outs):
        total = near[offset][...]
        for piece in far:
            total = total + piece[offset * rows : (offset + 1) * rows]
        out[...] = total


def second_kernel(x_count, slot_ref, target_ref, *refs):
    parts, outs, sums_ref = refs[:x_count], refs[x_count:-1], refs[-1]
    rows, links, step, _ = parts[0].shape
    share = outs[0].shape[0]
    sums_ref[...] = jnp.zeros_like(sums_ref)

    def one(row, carry):
        target = target_ref[row]
        for link in range(links):
            slot = slot_ref[row, link]
            for offset, part in enumerate(parts):
                sums_ref[target, slot, offset * step : (offset + 1) * step, :] += part[row, link]
        return carry

    lax.fori_loop(0, rows, one, 0, unroll=True)
    for way, out in enumerate(outs):
        out[...] = sums_ref[way * share : (way + 1) * share]


def place_kernel(x_count, place_ref, *refs):
    pieces, out = refs[:-1], refs[-1]
    part = out.shape[2] // x_count
    chunks = len(pieces) // x_count
    for offset in range(x_count):
        start = lax.rem(place_ref[0] + x_count - offset, x_count) * part
        for piece in pieces[offset * chunks : (offset + 1) * chunks]:
            step = piece.shape[2]
            out[:, :, pl.ds(pl.multiple_of(start, 8), step), :] = piece[...]
            start = start + step


def place_one(pieces, place, x_count):
    rows, links, _, size = pieces[0].shape
    return pl.pallas_call(
        functools.partial(place_kernel, x_count),
        out_shape=jax.ShapeDtypeStruct((rows, links, size, size), jnp.float32),
        grid_spec=pltpu.PrefetchScalarGridSpec(
            num_scalar_prefetch=1,
            grid=(rows,),
            in_specs=[
                pl.BlockSpec((1, links, piece.shape[2], size), lambda e, *_: (e, 0, 0, 0))
                for piece in pieces
            ],
            out_specs=pl.BlockSpec((1, links, size, size), lambda e, *_: (e, 0, 0, 0)),
        ),
        compiler_params=pltpu.CompilerParams(vmem_limit_bytes=vmem_limit),
        cost_estimate=pl.CostEstimate(
            flops=0, bytes_accessed=8 * rows * links * size**2, transcendentals=0
        ),
        name="place_one",
    )(place, *pieces)


def last_kernel(x_count, peers, place_ref, prolong_ref, *refs):
    pieces, (out, left_ref, right_ref, sums_ref) = refs[:-4], refs[-4:]
    links, size = out.shape[1], out.shape[2]
    part = size // x_count

    @pl.when(pl.program_id(0) == 0)
    def _():
        load_weights(prolong_ref, left_ref, right_ref)

    done = 0
    for first in range(0, len(pieces), peers):
        total = pieces[first][...]
        for piece in pieces[first + 1 : first + peers]:
            total = total + piece[...]
        step = total.shape[2] // x_count
        for offset in range(x_count):
            start = lax.rem(place_ref[0] + x_count - offset, x_count) * part
            at = pl.multiple_of(start + done, 8)
            sums_ref[:, :, pl.ds(at, step), :] = total[:, :, offset * step : (offset + 1) * step, :]
        done += step
    sums = [sums_ref[row, slot] for row in range(out.shape[0]) for slot in range(links)]
    out[...] = triple(sums, left_ref, right_ref).reshape(out.shape)


def last(pieces, prolong_two, place, x_count, peers):
    rows, links, _, size = pieces[0].shape
    held = max(h for h in range(1, rows_a_step // 2 + 1) if rows % h == 0)
    return pl.pallas_call(
        functools.partial(last_kernel, x_count, peers),
        out_shape=jax.ShapeDtypeStruct((rows, links, size, size), jnp.float32),
        grid_spec=pltpu.PrefetchScalarGridSpec(
            num_scalar_prefetch=1,
            grid=(rows // held,),
            in_specs=[pl.BlockSpec((size, size), lambda e, *_: (0, 0))]
            + [
                pl.BlockSpec((held, links, piece.shape[2], size), lambda e, *_: (e, 0, 0, 0))
                for piece in pieces
            ],
            out_specs=pl.BlockSpec((held, links, size, size), lambda e, *_: (e, 0, 0, 0)),
            scratch_shapes=[
                pltpu.VMEM((2 * size, 2 * size), jnp.bfloat16),
                pltpu.VMEM((2 * size, 2 * size), jnp.bfloat16),
                pltpu.VMEM((held, links, size, size), jnp.float32),
            ],
        ),
        compiler_params=pltpu.CompilerParams(vmem_limit_bytes=vmem_limit),
        cost_estimate=pl.CostEstimate(
            flops=16 * rows * links * size**3,
            bytes_accessed=4 * rows * links * size**2 * (peers + 1),
            transcendentals=0,
        ),
        name="last",
    )(place, prolong_two, *pieces)


def around(initial_guess):
    axes = ("group", "member")
    devices = lax.axis_size(axes)
    before = lax.ppermute(initial_guess, axes, [(i, (i + 1) % devices) for i in range(devices)])
    after = lax.ppermute(initial_guess, axes, [(i, (i - 1) % devices) for i in range(devices)])
    return [before, initial_guess, after]


def sweep(fine_blocks, neighbours, diag_inverse, right_side, initial_guess, window):
    rows = fine_blocks.shape[0]
    axes = ("group", "member")
    devices = lax.axis_size(axes)
    device = lax.axis_index(axes)
    window = jnp.concatenate(window, axis=0)
    position = (neighbours - device * rows + rows) % (rows * devices)
    nearby = window[position]
    product = jnp.sum(fine_blocks * nearby[:, :, None, :], axis=(1, 3))
    defect = right_side - product
    return initial_guess + damping * jnp.sum(diag_inverse * defect[:, None, :], axis=2)


def local(
    fine_blocks,
    neighbours,
    slot_one,
    pair_one,
    prolong_one,
    slot_two,
    pair_two,
    prolong_two,
    diag_inverse,
    right_side,
    initial_guess,
):
    rows, links, size, _ = fine_blocks.shape
    rows_one, rows_two = rows // 2, rows // 4
    members, groups = lax.axis_size("member"), lax.axis_size("group")
    z_count, x_count = grid_of(members)
    half = z_count // 2
    part = size // x_count
    steps = chunk_steps(part)

    member = lax.axis_index("member")
    z, x = member // x_count, member % x_count
    upper = (z >= half).astype(jnp.int32)
    place = jnp.stack([x]).astype(jnp.int32)

    def at(side, d, x_at):
        return (half + d if side else half - 1 - d) * x_count + x_at % x_count

    def hop(array, d_from, d_to, offset):
        pairs = [
            (at(side, d_from, x_at), at(side, d_to, x_at + offset))
            for side in range(2)
            for x_at in range(x_count)
        ]
        return lax.ppermute(array, "member", pairs)

    def hop_x(array, offset):
        pairs = [
            (z_at * x_count + x_at, z_at * x_count + (x_at + offset) % x_count)
            for z_at in range(z_count)
            for x_at in range(x_count)
        ]
        return lax.ppermute(array, "member", pairs)

    routes = [(d, o) for d in range(half) for o in range(x_count)]

    def along(arrays):
        return [array if o == 0 else hop_x(array, o) for o, array in enumerate(arrays)]

    def inward(arrays):
        return arrays + [hop(array, d, 0, 0) for d in range(1, half) for array in arrays]

    tags = jnp.stack(along([pair_one] * x_count))
    slot_one, tags, window = lax.optimization_barrier((slot_one, tags, around(initial_guess)))
    owner_rows = jnp.concatenate([tags] + [hop(tags, d, 0, 0) for d in range(1, half)])
    owner = owner_rows // rows_one % members
    owner_z, owner_x = owner // x_count, owner % x_count
    owner_upper = (owner_z >= half).astype(jnp.int32)
    owner_d = jnp.where(owner_upper > 0, owner_z - half, half - 1 - owner_z)
    near = (owner_upper == upper).astype(jnp.int32)
    target_one = ((near * half + owner_d) * x_count + (owner_x - x + x_count) % x_count) * rows_one
    target_one = (target_one + owner_rows % rows_one).astype(jnp.int32)
    middle = jnp.stack([(z == half - 1) | (z == half)]).astype(jnp.int32)

    way = (pair_two // rows_two // members - lax.axis_index("group") + groups) % groups
    target_two = (way * rows_two + pair_two % rows_two).astype(jnp.int32)

    outgoing = prepare(fine_blocks, slot_one, prolong_one, place, x_count, steps)
    across = [(at(0, 0, x_at), at(1, 0, x_at)) for x_at in range(x_count)]
    across = across + [(b, a) for a, b in across]
    before = [target_one]

    def in_turn(kernel, scalars, arrays, out_shapes, name, **more):
        arrays, before[0] = lax.optimization_barrier((list(arrays), before[0]))
        outs = whole(kernel, scalars, arrays, out_shapes, name, **more)
        before[0] = outs[0]
        return outs

    def rows_of(count, height):
        return jax.ShapeDtypeStruct((count, links, height, size), jnp.float32)

    coming, targets = [], [target_one]
    for chunk in range(len(steps)):
        own = outgoing[0][chunk]
        if chunk > 0:
            ahead = coming[-1]
            tied = (own, ahead[x_count], targets[0]) if chunk == 1 else (own, ahead[x_count])
            own, ahead[x_count], *seen = lax.optimization_barrier(tied)
            targets += seen
        coming.append(inward(along([own] + [ways[chunk] for ways in outgoing[1:]])))
    received = []

    smoothed = []

    def combine(chunk):
        held = coming[chunk]
        if chunk == min(1, len(steps) - 1):
            later, before[0] = lax.optimization_barrier((neighbours, before[0]))
            swept = sweep(fine_blocks, later, diag_inverse, right_side, initial_guess, window)
            held, swept = lax.optimization_barrier((held, swept))
            smoothed.append(swept)
        total = half * x_count * rows_one
        far, kept = in_turn(
            functools.partial(combine_kernel, len(held)),
            [targets[min(chunk, 1)]],
            held,
            [rows_of(total, steps[chunk]), rows_of(2 * total, steps[chunk])],
            "combine",
            work=beside,
        )
        return kept, lax.ppermute(far, "member", across)

    def finish(chunk, sums):
        finished = in_turn(
            finish_kernel,
            [middle],
            sums,
            [rows_of(x_count * rows_one, steps[chunk])] * (half - 1)
            + [rows_of(rows_one, steps[chunk])] * x_count,
            "finish",
        )
        return list(finished[half - 1 :]) + [hop(finished[d - 1], 0, d, 0) for d in range(1, half)]

    def settle(chunk, finished):
        return along(
            in_turn(
                functools.partial(settle_kernel, x_count),
                [],
                finished,
                [rows_of(rows_one, steps[chunk])] * x_count,
                "settle",
            )
        )

    def second(chunk, ours):
        if chunk + 1 < len(steps):
            received[-groups:], ours = lax.optimization_barrier((received[-groups:], ours))
        height = x_count * steps[chunk]
        shares = in_turn(
            functools.partial(second_kernel, x_count),
            [slot_two, target_two],
            ours,
            [rows_of(rows_two, height)] * groups,
            "second",
            scratch=[pltpu.VMEM((groups * rows_two, links, height, size), jnp.float32)],
        )
        for way, share in enumerate(shares):
            circle = [(g, (g + way) % groups) for g in range(groups)]
            received.append(lax.ppermute(share, "group", circle) if way > 0 else share)
        return ours

    stages, shares = (combine, finish, settle, second), (1.0, 0.5, 0.25)
    turns, rows_in, swapped = [], 0.0, 0.0
    for chunk, step in enumerate(steps):
        rows_in += step
        time = swapped = max(rows_in, swapped) + step + pause
        turns += [(rows_in, 0, chunk), (time, 1, chunk)]
        for stage, share in enumerate(shares[1:], 2):
            time += share * step + pause
            turns.append((time, stage, chunk))
    held = [[None] * len(steps) for _ in range(len(stages) + 1)]
    for _, stage, chunk in sorted(turns):
        given = [held[stage][chunk]] if stage > 0 else []
        held[stage + 1][chunk] = stages[stage](chunk, *given)
    parts = held[4]

    coarse_one = place_one(
        [parts[chunk][o] for o in range(x_count) for chunk in range(len(steps))], place, x_count
    )
    coarse_two = last(received, prolong_two, place, x_count, groups)
    return (coarse_one, coarse_two, smoothed[0])


def solution(mesh):
    rows = P(("group", "member"))
    return jax.shard_map(
        local,
        mesh=mesh,
        in_specs=(rows, rows, rows, rows, P(), rows, rows, P(), rows, rows, rows),
        out_specs=(rows, rows, rows),
        check_vma=False,
    )
```

```python
import functools

import jax
import jax.numpy as jnp
from jax import lax
from jax.experimental import pallas as pl
from jax.experimental.pallas import tpu as pltpu
from jax.sharding import PartitionSpec as P

damping = 0.7
rows_a_step = 4
prepare_limit = 20 * 1024 * 1024
vmem_limit = 20 * 1024 * 1024
pause = 3
beside = 6


def grid_of(member_count):
    x_count = max(d for d in range(1, member_count + 1) if member_count % d == 0 and d * d <= member_count)
    return member_count // x_count, x_count


def chunk_steps(part):
    tiles = part // 8
    step = max(tiles // 4, 1)
    ends = [max(step // 2, 1)] * min(2, tiles)
    inner = tiles - sum(ends)
    steps = ends[:1] + [step] * (inner // step) + [inner % step] * (inner % step > 0) + ends[1:]
    return [8 * step for step in steps]


def split(values):
    high = values.astype(jnp.bfloat16)
    low = (values - high.astype(jnp.float32)).astype(jnp.bfloat16)
    return high, low


def load_weights(prolong_ref, left_ref, right_ref):
    prolong = prolong_ref[...]
    size = prolong.shape[0]
    high, low = split(prolong)
    high_t, low_t = split(prolong.T)
    for half in range(2):
        at = pl.ds(half * size, size)
        left_ref[0:size, at] = high_t
        left_ref[size : 2 * size, at] = low_t
        right_ref[at, 0:size] = high
        right_ref[at, size : 2 * size] = low


def triple(blocks, left_ref, right_ref):
    size = blocks[0].shape[0]
    count = len(blocks)
    high, low = split(jnp.concatenate(blocks, axis=1))
    both = jnp.dot(
        left_ref[...], jnp.concatenate([high, low], axis=0), preferred_element_type=jnp.float32
    )
    left = both[:size] + both[size:]
    rows = jnp.concatenate([left[:, s * size : (s + 1) * size] for s in range(count)], axis=0)
    high, low = split(rows)
    both = jnp.dot(
        jnp.concatenate([high, low], axis=1), right_ref[...], preferred_element_type=jnp.float32
    )
    return (both[:, :size] + both[:, size:]).reshape(count, size, size)


def prepare_kernel(x_count, slot_ref, place_ref, prolong_ref, fine_ref, *rest):
    outs, (left_ref, right_ref, sums_ref, done_ref) = rest[:-4], rest[-4:]
    held, links, size, _ = fine_ref.shape
    chunks = len(outs) // x_count
    part = size // x_count

    @pl.when(pl.program_id(0) == 0)
    def _():
        load_weights(prolong_ref, left_ref, right_ref)

    sums_ref[...] = jnp.zeros_like(sums_ref)
    for row in range(held):
        for link in range(links):
            slot = slot_ref[pl.program_id(0) * held + row, link]
            sums_ref[row, slot] += fine_ref[row, link]
    sums = [sums_ref[row, slot] for row in range(held) for slot in range(links)]
    done_ref[...] = triple(sums, left_ref, right_ref).reshape(done_ref.shape)
    for offset in range(x_count):
        start = lax.rem(place_ref[0] + offset, x_count) * part
        for out in outs[offset * chunks : (offset + 1) * chunks]:
            step = out.shape[2]
            out[...] = done_ref[:, :, pl.ds(pl.multiple_of(start, 8), step), :]
            start = start + step


def prepare(fine_blocks, slot_one, prolong_one, place, x_count, steps):
    rows, links, size, _ = fine_blocks.shape
    chunks = len(steps)
    held = max(h for h in range(1, rows_a_step + 1) if rows % h == 0)
    outs = pl.pallas_call(
        functools.partial(prepare_kernel, x_count),
        out_shape=[
            jax.ShapeDtypeStruct((rows, links, step, size), jnp.float32)
            if chunk < 2
            else pltpu.HBM((rows, links, step, size), jnp.float32)
            for chunk, step in enumerate(steps)
        ]
        * x_count,
        grid_spec=pltpu.PrefetchScalarGridSpec(
            num_scalar_prefetch=2,
            grid=(rows // held,),
            in_specs=[
                pl.BlockSpec((size, size), lambda e, *_: (0, 0)),
                pl.BlockSpec((held, links, size, size), lambda e, *_: (e, 0, 0, 0)),
            ],
            out_specs=[
                pl.BlockSpec((held, links, step, size), lambda e, *_: (e, 0, 0, 0)) for step in steps
            ]
            * x_count,
            scratch_shapes=[
                pltpu.VMEM((2 * size, 2 * size), jnp.bfloat16),
                pltpu.VMEM((2 * size, 2 * size), jnp.bfloat16),
                pltpu.VMEM((held, links, size, size), jnp.float32),
                pltpu.VMEM((held, links, size, size), jnp.float32),
            ],
        ),
        compiler_params=pltpu.CompilerParams(vmem_limit_bytes=prepare_limit),
        cost_estimate=pl.CostEstimate(
            flops=16 * rows * links * size**3,
            bytes_accessed=8 * rows * links * size**2,
            transcendentals=0,
        ),
        name="prepare",
    )(slot_one, place, prolong_one, fine_blocks)
    return [list(outs[offset * chunks : (offset + 1) * chunks]) for offset in range(x_count)]


def whole(kernel, scalars, arrays, out_shapes, name, work=0, scratch=()):
    return pl.pallas_call(
        kernel,
        out_shape=out_shapes,
        in_specs=[pl.BlockSpec(memory_space=pltpu.SMEM)] * len(scalars)
        + [pl.BlockSpec(memory_space=pltpu.VMEM)] * len(arrays),
        out_specs=[pl.BlockSpec(memory_space=pltpu.VMEM)] * len(out_shapes),
        scratch_shapes=scratch,
        compiler_params=pltpu.CompilerParams(vmem_limit_bytes=vmem_limit),
        cost_estimate=pl.CostEstimate(flops=work * 10**9, bytes_accessed=0, transcendentals=0),
        name=name,
    )(*scalars, *arrays)


def combine_kernel(sources, target_ref, *refs):
    arrays, (far_ref, sums_ref) = refs[:sources], refs[sources:]
    rows = arrays[0].shape[0]
    sums_ref[...] = jnp.zeros_like(sums_ref)
    for source in range(sources):

        def one(row, carry, source=source):
            sums_ref[target_ref[source, row]] += arrays[source][row]
            return carry

        lax.fori_loop(0, rows, one, 0, unroll=True)
    far_ref[...] = sums_ref[0 : far_ref.shape[0]]


def finish_kernel(middle_ref, sums_ref, got_ref, *outs):
    half, rows = got_ref.shape[0], outs[-1].shape[0]
    own = len([out for out in outs if out.shape[0] == rows])
    far, near = outs[:-own], outs[-own:]
    width = own * rows
    for d, out in enumerate(far):
        at = (d + 1) * width
        out[...] = sums_ref[half + at : half + at + width] + got_ref[at : at + width]
    for offset, out in enumerate(near):
        at = offset * rows
        total = sums_ref[half + at : half + at + rows] + got_ref[at : at + rows]
        out[...] = jnp.where(middle_ref[0] > 0, total, 0.0)


def settle_kernel(count, *refs):
    near, far, outs = refs[:count], refs[count:-count], refs[-count:]
    rows = outs[0].shape[0]
    for offset, out in enumerate(outs):
        total = near[offset][...]
        for piece in far:
            total = total + piece[offset * rows : (offset + 1) * rows]
        out[...] = total


def second_kernel(x_count, slot_ref, target_ref, *refs):
    parts, outs, sums_ref = refs[:x_count], refs[x_count:-1], refs[-1]
    rows, links, step, _ = parts[0].shape
    share = outs[0].shape[0]
    sums_ref[...] = jnp.zeros_like(sums_ref)

    def one(row, carry):
        target = target_ref[row]
        for link in range(links):
            slot = slot_ref[row, link]
            for offset, part in enumerate(parts):
                sums_ref[target, slot, offset * step : (offset + 1) * step, :] += part[row, link]
        return carry

    lax.fori_loop(0, rows, one, 0, unroll=True)
    for way, out in enumerate(outs):
        out[...] = sums_ref[way * share : (way + 1) * share]


def place_kernel(x_count, place_ref, *refs):
    pieces, out = refs[:-1], refs[-1]
    part = out.shape[2] // x_count
    chunks = len(pieces) // x_count
    for offset in range(x_count):
        start = lax.rem(place_ref[0] + x_count - offset, x_count) * part
        for piece in pieces[offset * chunks : (offset + 1) * chunks]:
            step = piece.shape[2]
            out[:, :, pl.ds(pl.multiple_of(start, 8), step), :] = piece[...]
            start = start + step


def place_one(pieces, place, x_count):
    rows, links, _, size = pieces[0].shape
    return pl.pallas_call(
        functools.partial(place_kernel, x_count),
        out_shape=jax.ShapeDtypeStruct((rows, links, size, size), jnp.float32),
        grid_spec=pltpu.PrefetchScalarGridSpec(
            num_scalar_prefetch=1,
            grid=(rows,),
            in_specs=[
                pl.BlockSpec((1, links, piece.shape[2], size), lambda e, *_: (e, 0, 0, 0))
                for piece in pieces
            ],
            out_specs=pl.BlockSpec((1, links, size, size), lambda e, *_: (e, 0, 0, 0)),
        ),
        compiler_params=pltpu.CompilerParams(vmem_limit_bytes=vmem_limit),
        cost_estimate=pl.CostEstimate(
            flops=0, bytes_accessed=8 * rows * links * size**2, transcendentals=0
        ),
        name="place_one",
    )(place, *pieces)


def last_kernel(x_count, peers, place_ref, prolong_ref, *refs):
    pieces, (out, left_ref, right_ref, sums_ref) = refs[:-4], refs[-4:]
    links, size = out.shape[1], out.shape[2]
    part = size // x_count

    @pl.when(pl.program_id(0) == 0)
    def _():
        load_weights(prolong_ref, left_ref, right_ref)

    done = 0
    for first in range(0, len(pieces), peers):
        total = pieces[first][...]
        for piece in pieces[first + 1 : first + peers]:
            total = total + piece[...]
        step = total.shape[2] // x_count
        for offset in range(x_count):
            start = lax.rem(place_ref[0] + x_count - offset, x_count) * part
            at = pl.multiple_of(start + done, 8)
            sums_ref[:, :, pl.ds(at, step), :] = total[:, :, offset * step : (offset + 1) * step, :]
        done += step
    sums = [sums_ref[row, slot] for row in range(out.shape[0]) for slot in range(links)]
    out[...] = triple(sums, left_ref, right_ref).reshape(out.shape)


def last(pieces, prolong_two, place, x_count, peers):
    rows, links, _, size = pieces[0].shape
    held = max(h for h in range(1, rows_a_step // 2 + 1) if rows % h == 0)
    return pl.pallas_call(
        functools.partial(last_kernel, x_count, peers),
        out_shape=jax.ShapeDtypeStruct((rows, links, size, size), jnp.float32),
        grid_spec=pltpu.PrefetchScalarGridSpec(
            num_scalar_prefetch=1,
            grid=(rows // held,),
            in_specs=[pl.BlockSpec((size, size), lambda e, *_: (0, 0))]
            + [
                pl.BlockSpec((held, links, piece.shape[2], size), lambda e, *_: (e, 0, 0, 0))
                for piece in pieces
            ],
            out_specs=pl.BlockSpec((held, links, size, size), lambda e, *_: (e, 0, 0, 0)),
            scratch_shapes=[
                pltpu.VMEM((2 * size, 2 * size), jnp.bfloat16),
                pltpu.VMEM((2 * size, 2 * size), jnp.bfloat16),
                pltpu.VMEM((held, links, size, size), jnp.float32),
            ],
        ),
        compiler_params=pltpu.CompilerParams(vmem_limit_bytes=vmem_limit),
        cost_estimate=pl.CostEstimate(
            flops=16 * rows * links * size**3,
            bytes_accessed=4 * rows * links * size**2 * (peers + 1),
            transcendentals=0,
        ),
        name="last",
    )(place, prolong_two, *pieces)


def around(initial_guess):
    axes = ("group", "member")
    devices = lax.axis_size(axes)
    before = lax.ppermute(initial_guess, axes, [(i, (i + 1) % devices) for i in range(devices)])
    after = lax.ppermute(initial_guess, axes, [(i, (i - 1) % devices) for i in range(devices)])
    return [before, initial_guess, after]


def sweep(fine_blocks, neighbours, diag_inverse, right_side, initial_guess, window):
    rows = fine_blocks.shape[0]
    axes = ("group", "member")
    devices = lax.axis_size(axes)
    device = lax.axis_index(axes)
    window = jnp.concatenate(window, axis=0)
    position = (neighbours - device * rows + rows) % (rows * devices)
    nearby = window[position]
    product = jnp.sum(fine_blocks * nearby[:, :, None, :], axis=(1, 3))
    defect = right_side - product
    return initial_guess + damping * jnp.sum(diag_inverse * defect[:, None, :], axis=2)


def local(
    fine_blocks,
    neighbours,
    slot_one,
    pair_one,
    prolong_one,
    slot_two,
    pair_two,
    prolong_two,
    diag_inverse,
    right_side,
    initial_guess,
):
    rows, links, size, _ = fine_blocks.shape
    rows_one, rows_two = rows // 2, rows // 4
    members, groups = lax.axis_size("member"), lax.axis_size("group")
    z_count, x_count = grid_of(members)
    half = z_count // 2
    part = size // x_count
    steps = chunk_steps(part)

    member = lax.axis_index("member")
    z, x = member // x_count, member % x_count
    upper = (z >= half).astype(jnp.int32)
    place = jnp.stack([x]).astype(jnp.int32)

    def at(side, d, x_at):
        return (half + d if side else half - 1 - d) * x_count + x_at % x_count

    def hop(array, d_from, d_to, offset):
        pairs = [
            (at(side, d_from, x_at), at(side, d_to, x_at + offset))
            for side in range(2)
            for x_at in range(x_count)
        ]
        return lax.ppermute(array, "member", pairs)

    def hop_x(array, offset):
        pairs = [
            (z_at * x_count + x_at, z_at * x_count + (x_at + offset) % x_count)
            for z_at in range(z_count)
            for x_at in range(x_count)
        ]
        return lax.ppermute(array, "member", pairs)

    routes = [(d, o) for d in range(half) for o in range(x_count)]

    def along(arrays):
        return [array if o == 0 else hop_x(array, o) for o, array in enumerate(arrays)]

    def inward(arrays):
        return arrays + [hop(array, d, 0, 0) for d in range(1, half) for array in arrays]

    tags = jnp.stack(along([pair_one] * x_count))
    slot_one, tags, window = lax.optimization_barrier((slot_one, tags, around(initial_guess)))
    owner_rows = jnp.concatenate([tags] + [hop(tags, d, 0, 0) for d in range(1, half)])
    owner = owner_rows // rows_one % members
    owner_z, owner_x = owner // x_count, owner % x_count
    owner_upper = (owner_z >= half).astype(jnp.int32)
    owner_d = jnp.where(owner_upper > 0, owner_z - half, half - 1 - owner_z)
    near = (owner_upper == upper).astype(jnp.int32)
    target_one = ((near * half + owner_d) * x_count + (owner_x - x + x_count) % x_count) * rows_one
    target_one = (target_one + owner_rows % rows_one).astype(jnp.int32)
    middle = jnp.stack([(z == half - 1) | (z == half)]).astype(jnp.int32)

    way = (pair_two // rows_two // members - lax.axis_index("group") + groups) % groups
    target_two = (way * rows_two + pair_two % rows_two).astype(jnp.int32)

    outgoing = prepare(fine_blocks, slot_one, prolong_one, place, x_count, steps)
    across = [(at(0, 0, x_at), at(1, 0, x_at)) for x_at in range(x_count)]
    across = across + [(b, a) for a, b in across]
    before = [target_one]

    def in_turn(kernel, scalars, arrays, out_shapes, name, **more):
        arrays, before[0] = lax.optimization_barrier((list(arrays), before[0]))
        outs = whole(kernel, scalars, arrays, out_shapes, name, **more)
        before[0] = outs[0]
        return outs

    def rows_of(count, height):
        return jax.ShapeDtypeStruct((count, links, height, size), jnp.float32)

    coming, targets = [], [target_one]
    for chunk in range(len(steps)):
        own = outgoing[0][chunk]
        if chunk > 0:
            ahead = coming[-1]
            tied = (own, ahead[x_count], targets[0]) if chunk == 1 else (own, ahead[x_count])
            own, ahead[x_count], *seen = lax.optimization_barrier(tied)
            targets += seen
        coming.append(inward(along([own] + [ways[chunk] for ways in outgoing[1:]])))
    received = []

    smoothed = []

    def combine(chunk):
        held = coming[chunk]
        if chunk == min(1, len(steps) - 1):
            later, before[0] = lax.optimization_barrier((neighbours, before[0]))
            swept = sweep(fine_blocks, later, diag_inverse, right_side, initial_guess, window)
            held, swept = lax.optimization_barrier((held, swept))
            smoothed.append(swept)
        total = half * x_count * rows_one
        far, kept = in_turn(
            functools.partial(combine_kernel, len(held)),
            [targets[min(chunk, 1)]],
            held,
            [rows_of(total, steps[chunk]), rows_of(2 * total, steps[chunk])],
            "combine",
            work=beside,
        )
        return kept, lax.ppermute(far, "member", across)

    def finish(chunk, sums):
        finished = in_turn(
            finish_kernel,
            [middle],
            sums,
            [rows_of(x_count * rows_one, steps[chunk])] * (half - 1)
            + [rows_of(rows_one, steps[chunk])] * x_count,
            "finish",
        )
        return list(finished[half - 1 :]) + [hop(finished[d - 1], 0, d, 0) for d in range(1, half)]

    def settle(chunk, finished):
        return along(
            in_turn(
                functools.partial(settle_kernel, x_count),
                [],
                finished,
                [rows_of(rows_one, steps[chunk])] * x_count,
                "settle",
            )
        )

    def second(chunk, ours):
        received[-groups:], ours = lax.optimization_barrier((received[-groups:], ours))
        height = x_count * steps[chunk]
        shares = in_turn(
            functools.partial(second_kernel, x_count),
            [slot_two, target_two],
            ours,
            [rows_of(rows_two, height)] * groups,
            "second",
            scratch=[pltpu.VMEM((groups * rows_two, links, height, size), jnp.float32)],
        )
        for way, share in enumerate(shares):
            circle = [(g, (g + way) % groups) for g in range(groups)]
            received.append(lax.ppermute(share, "group", circle) if way > 0 else share)
        return ours

    stages, shares = (combine, finish, settle, second), (1.0, 0.5, 0.25)
    turns, rows_in, swapped = [], 0.0, 0.0
    for chunk, step in enumerate(steps):
        rows_in += step
        time = swapped = max(rows_in, swapped) + step + pause
        turns += [(rows_in, 0, chunk), (time, 1, chunk)]
        for stage, share in enumerate(shares[1:], 2):
            time += share * step + pause
            turns.append((time, stage, chunk))
    held = [[None] * len(steps) for _ in range(len(stages) + 1)]
    for _, stage, chunk in sorted(turns):
        given = [held[stage][chunk]] if stage > 0 else []
        held[stage + 1][chunk] = stages[stage](chunk, *given)
    parts = held[4]

    coarse_one = place_one(
        [parts[chunk][o] for o in range(x_count) for chunk in range(len(steps))], place, x_count
    )
    coarse_two = last(received, prolong_two, place, x_count, groups)
    return (coarse_one, coarse_two, smoothed[0])


def solution(mesh):
    rows = P(("group", "member"))
    return jax.shard_map(
        local,
        mesh=mesh,
        in_specs=(rows, rows, rows, rows, P(), rows, rows, P(), rows, rows, rows),
        out_specs=(rows, rows, rows),
        check_vma=False,
    )
```

```python
import functools

import jax
import jax.numpy as jnp
from jax import lax
from jax.experimental import pallas as pl
from jax.experimental.pallas import tpu as pltpu
from jax.sharding import PartitionSpec as P

damping = 0.7
rows_a_step = 4
prepare_limit = 20 * 1024 * 1024
vmem_limit = 20 * 1024 * 1024
pause = 3
beside = 6


def grid_of(member_count):
    x_count = max(d for d in range(1, member_count + 1) if member_count % d == 0 and d * d <= member_count)
    return member_count // x_count, x_count


def chunk_steps(part):
    tiles = part // 8
    step = max(tiles // 4, 1)
    ends = [max(step // 2, 1)] * min(2, tiles)
    inner = tiles - sum(ends)
    steps = ends[:1] + [step] * (inner // step) + [inner % step] * (inner % step > 0) + ends[1:]
    return [8 * step for step in steps]


def split(values):
    high = values.astype(jnp.bfloat16)
    low = (values - high.astype(jnp.float32)).astype(jnp.bfloat16)
    return high, low


def load_weights(prolong_ref, left_ref, right_ref):
    prolong = prolong_ref[...]
    size = prolong.shape[0]
    high, low = split(prolong)
    high_t, low_t = split(prolong.T)
    for half in range(2):
        at = pl.ds(half * size, size)
        left_ref[0:size, at] = high_t
        left_ref[size : 2 * size, at] = low_t
        right_ref[at, 0:size] = high
        right_ref[at, size : 2 * size] = low


def triple(blocks, left_ref, right_ref):
    size = blocks[0].shape[0]
    count = len(blocks)
    high, low = split(jnp.concatenate(blocks, axis=1))
    both = jnp.dot(
        left_ref[...], jnp.concatenate([high, low], axis=0), preferred_element_type=jnp.float32
    )
    left = both[:size] + both[size:]
    rows = jnp.concatenate([left[:, s * size : (s + 1) * size] for s in range(count)], axis=0)
    high, low = split(rows)
    both = jnp.dot(
        jnp.concatenate([high, low], axis=1), right_ref[...], preferred_element_type=jnp.float32
    )
    return (both[:, :size] + both[:, size:]).reshape(count, size, size)


def prepare_kernel(x_count, slot_ref, place_ref, prolong_ref, fine_ref, *rest):
    outs, (left_ref, right_ref, sums_ref, done_ref) = rest[:-4], rest[-4:]
    held, links, size, _ = fine_ref.shape
    chunks = len(outs) // x_count
    part = size // x_count

    @pl.when(pl.program_id(0) == 0)
    def _():
        load_weights(prolong_ref, left_ref, right_ref)

    sums_ref[...] = jnp.zeros_like(sums_ref)
    for row in range(held):
        for link in range(links):
            slot = slot_ref[pl.program_id(0) * held + row, link]
            sums_ref[row, slot] += fine_ref[row, link]
    sums = [sums_ref[row, slot] for row in range(held) for slot in range(links)]
    done_ref[...] = triple(sums, left_ref, right_ref).reshape(done_ref.shape)
    for offset in range(x_count):
        start = lax.rem(place_ref[0] + offset, x_count) * part
        for out in outs[offset * chunks : (offset + 1) * chunks]:
            step = out.shape[2]
            out[...] = done_ref[:, :, pl.ds(pl.multiple_of(start, 8), step), :]
            start = start + step


def prepare(fine_blocks, slot_one, prolong_one, place, x_count, steps):
    rows, links, size, _ = fine_blocks.shape
    chunks = len(steps)
    held = max(h for h in range(1, rows_a_step + 1) if rows % h == 0)
    outs = pl.pallas_call(
        functools.partial(prepare_kernel, x_count),
        out_shape=[
            jax.ShapeDtypeStruct((rows, links, step, size), jnp.float32)
            if chunk < 2
            else pltpu.HBM((rows, links, step, size), jnp.float32)
            for chunk, step in enumerate(steps)
        ]
        * x_count,
        grid_spec=pltpu.PrefetchScalarGridSpec(
            num_scalar_prefetch=2,
            grid=(rows // held,),
            in_specs=[
                pl.BlockSpec((size, size), lambda e, *_: (0, 0)),
                pl.BlockSpec((held, links, size, size), lambda e, *_: (e, 0, 0, 0)),
            ],
            out_specs=[
                pl.BlockSpec((held, links, step, size), lambda e, *_: (e, 0, 0, 0)) for step in steps
            ]
            * x_count,
            scratch_shapes=[
                pltpu.VMEM((2 * size, 2 * size), jnp.bfloat16),
                pltpu.VMEM((2 * size, 2 * size), jnp.bfloat16),
                pltpu.VMEM((held, links, size, size), jnp.float32),
                pltpu.VMEM((held, links, size, size), jnp.float32),
            ],
        ),
        compiler_params=pltpu.CompilerParams(vmem_limit_bytes=prepare_limit),
        cost_estimate=pl.CostEstimate(
            flops=16 * rows * links * size**3,
            bytes_accessed=8 * rows * links * size**2,
            transcendentals=0,
        ),
        name="prepare",
    )(slot_one, place, prolong_one, fine_blocks)
    return [list(outs[offset * chunks : (offset + 1) * chunks]) for offset in range(x_count)]


def whole(kernel, scalars, arrays, out_shapes, name, work=0, scratch=()):
    return pl.pallas_call(
        kernel,
        out_shape=out_shapes,
        in_specs=[pl.BlockSpec(memory_space=pltpu.SMEM)] * len(scalars)
        + [pl.BlockSpec(memory_space=pltpu.VMEM)] * len(arrays),
        out_specs=[pl.BlockSpec(memory_space=pltpu.VMEM)] * len(out_shapes),
        scratch_shapes=scratch,
        compiler_params=pltpu.CompilerParams(vmem_limit_bytes=vmem_limit),
        cost_estimate=pl.CostEstimate(flops=work * 10**9, bytes_accessed=0, transcendentals=0),
        name=name,
    )(*scalars, *arrays)


def combine_kernel(sources, target_ref, *refs):
    arrays, (far_ref, sums_ref) = refs[:sources], refs[sources:]
    rows = arrays[0].shape[0]
    sums_ref[...] = jnp.zeros_like(sums_ref)
    for source in range(sources):

        def one(row, carry, source=source):
            sums_ref[target_ref[source, row]] += arrays[source][row]
            return carry

        lax.fori_loop(0, rows, one, 0, unroll=True)
    far_ref[...] = sums_ref[0 : far_ref.shape[0]]


def finish_kernel(middle_ref, sums_ref, got_ref, *outs):
    half, rows = got_ref.shape[0], outs[-1].shape[0]
    own = len([out for out in outs if out.shape[0] == rows])
    far, near = outs[:-own], outs[-own:]
    width = own * rows
    for d, out in enumerate(far):
        at = (d + 1) * width
        out[...] = sums_ref[half + at : half + at + width] + got_ref[at : at + width]
    for offset, out in enumerate(near):
        at = offset * rows
        total = sums_ref[half + at : half + at + rows] + got_ref[at : at + rows]
        out[...] = jnp.where(middle_ref[0] > 0, total, 0.0)


def settle_kernel(count, *refs):
    near, far, outs = refs[:count], refs[count:-count], refs[-count:]
    rows = outs[0].shape[0]
    for offset, out in enumerate(outs):
        total = near[offset][...]
        for piece in far:
            total = total + piece[offset * rows : (offset + 1) * rows]
        out[...] = total


def second_kernel(x_count, slot_ref, target_ref, *refs):
    parts, outs, sums_ref = refs[:x_count], refs[x_count:-1], refs[-1]
    rows, links, step, _ = parts[0].shape
    share = outs[0].shape[0]
    sums_ref[...] = jnp.zeros_like(sums_ref)

    def one(row, carry):
        target = target_ref[row]
        for link in range(links):
            slot = slot_ref[row, link]
            for offset, part in enumerate(parts):
                sums_ref[target, slot, offset * step : (offset + 1) * step, :] += part[row, link]
        return carry

    lax.fori_loop(0, rows, one, 0, unroll=True)
    for way, out in enumerate(outs):
        out[...] = sums_ref[way * share : (way + 1) * share]


def place_kernel(x_count, place_ref, *refs):
    pieces, out = refs[:-1], refs[-1]
    part = out.shape[2] // x_count
    chunks = len(pieces) // x_count
    for offset in range(x_count):
        start = lax.rem(place_ref[0] + x_count - offset, x_count) * part
        for piece in pieces[offset * chunks : (offset + 1) * chunks]:
            step = piece.shape[2]
            out[:, :, pl.ds(pl.multiple_of(start, 8), step), :] = piece[...]
            start = start + step


def place_one(pieces, place, x_count):
    rows, links, _, size = pieces[0].shape
    return pl.pallas_call(
        functools.partial(place_kernel, x_count),
        out_shape=jax.ShapeDtypeStruct((rows, links, size, size), jnp.float32),
        grid_spec=pltpu.PrefetchScalarGridSpec(
            num_scalar_prefetch=1,
            grid=(rows,),
            in_specs=[
                pl.BlockSpec((1, links, piece.shape[2], size), lambda e, *_: (e, 0, 0, 0))
                for piece in pieces
            ],
            out_specs=pl.BlockSpec((1, links, size, size), lambda e, *_: (e, 0, 0, 0)),
        ),
        compiler_params=pltpu.CompilerParams(vmem_limit_bytes=vmem_limit),
        cost_estimate=pl.CostEstimate(
            flops=0, bytes_accessed=8 * rows * links * size**2, transcendentals=0
        ),
        name="place_one",
    )(place, *pieces)


def last_kernel(x_count, peers, place_ref, prolong_ref, *refs):
    pieces, (out, left_ref, right_ref, sums_ref) = refs[:-4], refs[-4:]
    links, size = out.shape[1], out.shape[2]
    part = size // x_count

    @pl.when(pl.program_id(0) == 0)
    def _():
        load_weights(prolong_ref, left_ref, right_ref)

    done = 0
    for first in range(0, len(pieces), peers):
        total = pieces[first][...]
        for piece in pieces[first + 1 : first + peers]:
            total = total + piece[...]
        step = total.shape[2] // x_count
        for offset in range(x_count):
            start = lax.rem(place_ref[0] + x_count - offset, x_count) * part
            at = pl.multiple_of(start + done, 8)
            sums_ref[:, :, pl.ds(at, step), :] = total[:, :, offset * step : (offset + 1) * step, :]
        done += step
    sums = [sums_ref[row, slot] for row in range(out.shape[0]) for slot in range(links)]
    out[...] = triple(sums, left_ref, right_ref).reshape(out.shape)


def last(pieces, prolong_two, place, x_count, peers):
    rows, links, _, size = pieces[0].shape
    held = max(h for h in range(1, rows_a_step // 2 + 1) if rows % h == 0)
    return pl.pallas_call(
        functools.partial(last_kernel, x_count, peers),
        out_shape=jax.ShapeDtypeStruct((rows, links, size, size), jnp.float32),
        grid_spec=pltpu.PrefetchScalarGridSpec(
            num_scalar_prefetch=1,
            grid=(rows // held,),
            in_specs=[pl.BlockSpec((size, size), lambda e, *_: (0, 0))]
            + [
                pl.BlockSpec((held, links, piece.shape[2], size), lambda e, *_: (e, 0, 0, 0))
                for piece in pieces
            ],
            out_specs=pl.BlockSpec((held, links, size, size), lambda e, *_: (e, 0, 0, 0)),
            scratch_shapes=[
                pltpu.VMEM((2 * size, 2 * size), jnp.bfloat16),
                pltpu.VMEM((2 * size, 2 * size), jnp.bfloat16),
                pltpu.VMEM((held, links, size, size), jnp.float32),
            ],
        ),
        compiler_params=pltpu.CompilerParams(vmem_limit_bytes=vmem_limit),
        cost_estimate=pl.CostEstimate(
            flops=16 * rows * links * size**3,
            bytes_accessed=4 * rows * links * size**2 * (peers + 1),
            transcendentals=0,
        ),
        name="last",
    )(place, prolong_two, *pieces)


def around(initial_guess):
    axes = ("group", "member")
    devices = lax.axis_size(axes)
    before = lax.ppermute(initial_guess, axes, [(i, (i + 1) % devices) for i in range(devices)])
    after = lax.ppermute(initial_guess, axes, [(i, (i - 1) % devices) for i in range(devices)])
    return [before, initial_guess, after]


def sweep(fine_blocks, neighbours, diag_inverse, right_side, initial_guess, window):
    rows = fine_blocks.shape[0]
    axes = ("group", "member")
    devices = lax.axis_size(axes)
    device = lax.axis_index(axes)
    window = jnp.concatenate(window, axis=0)
    position = (neighbours - device * rows + rows) % (rows * devices)
    nearby = window[position]
    product = jnp.sum(fine_blocks * nearby[:, :, None, :], axis=(1, 3))
    defect = right_side - product
    return initial_guess + damping * jnp.sum(diag_inverse * defect[:, None, :], axis=2)


def local(
    fine_blocks,
    neighbours,
    slot_one,
    pair_one,
    prolong_one,
    slot_two,
    pair_two,
    prolong_two,
    diag_inverse,
    right_side,
    initial_guess,
):
    rows, links, size, _ = fine_blocks.shape
    rows_one, rows_two = rows // 2, rows // 4
    members, groups = lax.axis_size("member"), lax.axis_size("group")
    z_count, x_count = grid_of(members)
    half = z_count // 2
    part = size // x_count
    steps = chunk_steps(part)

    member = lax.axis_index("member")
    z, x = member // x_count, member % x_count
    upper = (z >= half).astype(jnp.int32)
    place = jnp.stack([x]).astype(jnp.int32)

    def at(side, d, x_at):
        return (half + d if side else half - 1 - d) * x_count + x_at % x_count

    def hop(array, d_from, d_to, offset):
        pairs = [
            (at(side, d_from, x_at), at(side, d_to, x_at + offset))
            for side in range(2)
            for x_at in range(x_count)
        ]
        return lax.ppermute(array, "member", pairs)

    def hop_x(array, offset):
        pairs = [
            (z_at * x_count + x_at, z_at * x_count + (x_at + offset) % x_count)
            for z_at in range(z_count)
            for x_at in range(x_count)
        ]
        return lax.ppermute(array, "member", pairs)

    routes = [(d, o) for d in range(half) for o in range(x_count)]

    def along(arrays):
        return [array if o == 0 else hop_x(array, o) for o, array in enumerate(arrays)]

    def inward(arrays):
        return arrays + [hop(array, d, 0, 0) for d in range(1, half) for array in arrays]

    tags = jnp.stack(along([pair_one] * x_count))
    slot_one, tags, window = lax.optimization_barrier((slot_one, tags, around(initial_guess)))
    owner_rows = jnp.concatenate([tags] + [hop(tags, d, 0, 0) for d in range(1, half)])
    owner = owner_rows // rows_one % members
    owner_z, owner_x = owner // x_count, owner % x_count
    owner_upper = (owner_z >= half).astype(jnp.int32)
    owner_d = jnp.where(owner_upper > 0, owner_z - half, half - 1 - owner_z)
    near = (owner_upper == upper).astype(jnp.int32)
    target_one = ((near * half + owner_d) * x_count + (owner_x - x + x_count) % x_count) * rows_one
    target_one = (target_one + owner_rows % rows_one).astype(jnp.int32)
    middle = jnp.stack([(z == half - 1) | (z == half)]).astype(jnp.int32)

    way = (pair_two // rows_two // members - lax.axis_index("group") + groups) % groups
    target_two = (way * rows_two + pair_two % rows_two).astype(jnp.int32)

    outgoing = prepare(fine_blocks, slot_one, prolong_one, place, x_count, steps)
    across = [(at(0, 0, x_at), at(1, 0, x_at)) for x_at in range(x_count)]
    across = across + [(b, a) for a, b in across]
    before = [target_one]

    def in_turn(kernel, scalars, arrays, out_shapes, name, **more):
        arrays, before[0] = lax.optimization_barrier((list(arrays), before[0]))
        outs = whole(kernel, scalars, arrays, out_shapes, name, **more)
        before[0] = outs[0]
        return outs

    def rows_of(count, height):
        return jax.ShapeDtypeStruct((count, links, height, size), jnp.float32)

    coming, targets = [], [target_one]
    for chunk in range(len(steps)):
        own = outgoing[0][chunk]
        if chunk > 0:
            ahead = coming[-1]
            tied = (own, ahead[x_count], targets[0]) if chunk == 1 else (own, ahead[x_count])
            own, ahead[x_count], *seen = lax.optimization_barrier(tied)
            targets += seen
        coming.append(inward(along([own] + [ways[chunk] for ways in outgoing[1:]])))
    received = []

    smoothed = []

    def combine(chunk):
        held = coming[chunk]
        if chunk == min(1, len(steps) - 1):
            later, before[0] = lax.optimization_barrier((neighbours, before[0]))
            swept = sweep(fine_blocks, later, diag_inverse, right_side, initial_guess, window)
            held, swept = lax.optimization_barrier((held, swept))
            smoothed.append(swept)
        total = half * x_count * rows_one
        far, kept = in_turn(
            functools.partial(combine_kernel, len(held)),
            [targets[min(chunk, 1)]],
            held,
            [rows_of(total, steps[chunk]), rows_of(2 * total, steps[chunk])],
            "combine",
            work=beside,
        )
        return kept, lax.ppermute(far, "member", across)

    def finish(chunk, sums):
        finished = in_turn(
            finish_kernel,
            [middle],
            sums,
            [rows_of(x_count * rows_one, steps[chunk])] * (half - 1)
            + [rows_of(rows_one, steps[chunk])] * x_count,
            "finish",
        )
        return list(finished[half - 1 :]) + [hop(finished[d - 1], 0, d, 0) for d in range(1, half)]

    def settle(chunk, finished):
        if chunk == 0 and len(steps) > 2:
            ahead = coming[chunk + 2]
            ahead[x_count], finished = lax.optimization_barrier((ahead[x_count], finished))
        return along(
            in_turn(
                functools.partial(settle_kernel, x_count),
                [],
                finished,
                [rows_of(rows_one, steps[chunk])] * x_count,
                "settle",
            )
        )

    def second(chunk, ours):
        received[-groups:], ours = lax.optimization_barrier((received[-groups:], ours))
        height = x_count * steps[chunk]
        shares = in_turn(
            functools.partial(second_kernel, x_count),
            [slot_two, target_two],
            ours,
            [rows_of(rows_two, height)] * groups,
            "second",
            scratch=[pltpu.VMEM((groups * rows_two, links, height, size), jnp.float32)],
        )
        for way, share in enumerate(shares):
            circle = [(g, (g + way) % groups) for g in range(groups)]
            received.append(lax.ppermute(share, "group", circle) if way > 0 else share)
        return ours

    stages, shares = (combine, finish, settle, second), (1.0, 0.5, 0.25)
    turns, rows_in, swapped = [], 0.0, 0.0
    for chunk, step in enumerate(steps):
        rows_in += step
        time = swapped = max(rows_in, swapped) + step + pause
        turns += [(rows_in, 0, chunk), (time, 1, chunk)]
        for stage, share in enumerate(shares[1:], 2):
            time += share * step + pause
            turns.append((time, stage, chunk))
    held = [[None] * len(steps) for _ in range(len(stages) + 1)]
    for _, stage, chunk in sorted(turns):
        given = [held[stage][chunk]] if stage > 0 else []
        held[stage + 1][chunk] = stages[stage](chunk, *given)
    parts = held[4]

    coarse_one = place_one(
        [parts[chunk][o] for o in range(x_count) for chunk in range(len(steps))], place, x_count
    )
    coarse_two = last(received, prolong_two, place, x_count, groups)
    return (coarse_one, coarse_two, smoothed[0])


def solution(mesh):
    rows = P(("group", "member"))
    return jax.shard_map(
        local,
        mesh=mesh,
        in_specs=(rows, rows, rows, rows, P(), rows, rows, P(), rows, rows, rows),
        out_specs=(rows, rows, rows),
        check_vma=False,
    )
```

```python
import functools

import jax
import jax.numpy as jnp
from jax import lax
from jax.experimental import pallas as pl
from jax.experimental.pallas import tpu as pltpu
from jax.sharding import PartitionSpec as P

damping = 0.7
rows_a_step = 4
prepare_limit = 20 * 1024 * 1024
vmem_limit = 20 * 1024 * 1024
pause = 3
beside = 6


def grid_of(member_count):
    x_count = max(d for d in range(1, member_count + 1) if member_count % d == 0 and d * d <= member_count)
    return member_count // x_count, x_count


def chunk_steps(part):
    tiles = part // 8
    step = max(tiles // 4, 1)
    ends = [max(step // 2, 1)] * min(2, tiles)
    inner = tiles - sum(ends)
    steps = ends[:1] + [step] * (inner // step) + [inner % step] * (inner % step > 0) + ends[1:]
    return [8 * step for step in steps]


def split(values):
    high = values.astype(jnp.bfloat16)
    low = (values - high.astype(jnp.float32)).astype(jnp.bfloat16)
    return high, low


def load_weights(prolong_ref, left_ref, right_ref):
    prolong = prolong_ref[...]
    size = prolong.shape[0]
    high, low = split(prolong)
    high_t, low_t = split(prolong.T)
    for half in range(2):
        at = pl.ds(half * size, size)
        left_ref[0:size, at] = high_t
        left_ref[size : 2 * size, at] = low_t
        right_ref[at, 0:size] = high
        right_ref[at, size : 2 * size] = low


def triple(blocks, left_ref, right_ref):
    size = blocks[0].shape[0]
    count = len(blocks)
    high, low = split(jnp.concatenate(blocks, axis=1))
    both = jnp.dot(
        left_ref[...], jnp.concatenate([high, low], axis=0), preferred_element_type=jnp.float32
    )
    left = both[:size] + both[size:]
    rows = jnp.concatenate([left[:, s * size : (s + 1) * size] for s in range(count)], axis=0)
    high, low = split(rows)
    both = jnp.dot(
        jnp.concatenate([high, low], axis=1), right_ref[...], preferred_element_type=jnp.float32
    )
    return (both[:, :size] + both[:, size:]).reshape(count, size, size)


def prepare_kernel(x_count, slot_ref, place_ref, prolong_ref, fine_ref, *rest):
    outs, (left_ref, right_ref, sums_ref, done_ref) = rest[:-4], rest[-4:]
    held, links, size, _ = fine_ref.shape
    chunks = len(outs) // x_count
    part = size // x_count

    @pl.when(pl.program_id(0) == 0)
    def _():
        load_weights(prolong_ref, left_ref, right_ref)

    sums_ref[...] = jnp.zeros_like(sums_ref)
    for row in range(held):
        for link in range(links):
            slot = slot_ref[pl.program_id(0) * held + row, link]
            sums_ref[row, slot] += fine_ref[row, link]
    sums = [sums_ref[row, slot] for row in range(held) for slot in range(links)]
    done_ref[...] = triple(sums, left_ref, right_ref).reshape(done_ref.shape)
    for offset in range(x_count):
        start = lax.rem(place_ref[0] + offset, x_count) * part
        for out in outs[offset * chunks : (offset + 1) * chunks]:
            step = out.shape[2]
            out[...] = done_ref[:, :, pl.ds(pl.multiple_of(start, 8), step), :]
            start = start + step


def prepare(fine_blocks, slot_one, prolong_one, place, x_count, steps):
    rows, links, size, _ = fine_blocks.shape
    chunks = len(steps)
    held = max(h for h in range(1, rows_a_step + 1) if rows % h == 0)
    outs = pl.pallas_call(
        functools.partial(prepare_kernel, x_count),
        out_shape=[
            jax.ShapeDtypeStruct((rows, links, step, size), jnp.float32)
            if chunk < 2
            else pltpu.HBM((rows, links, step, size), jnp.float32)
            for chunk, step in enumerate(steps)
        ]
        * x_count,
        grid_spec=pltpu.PrefetchScalarGridSpec(
            num_scalar_prefetch=2,
            grid=(rows // held,),
            in_specs=[
                pl.BlockSpec((size, size), lambda e, *_: (0, 0)),
                pl.BlockSpec((held, links, size, size), lambda e, *_: (e, 0, 0, 0)),
            ],
            out_specs=[
                pl.BlockSpec((held, links, step, size), lambda e, *_: (e, 0, 0, 0)) for step in steps
            ]
            * x_count,
            scratch_shapes=[
                pltpu.VMEM((2 * size, 2 * size), jnp.bfloat16),
                pltpu.VMEM((2 * size, 2 * size), jnp.bfloat16),
                pltpu.VMEM((held, links, size, size), jnp.float32),
                pltpu.VMEM((held, links, size, size), jnp.float32),
            ],
        ),
        compiler_params=pltpu.CompilerParams(vmem_limit_bytes=prepare_limit),
        cost_estimate=pl.CostEstimate(
            flops=16 * rows * links * size**3,
            bytes_accessed=8 * rows * links * size**2,
            transcendentals=0,
        ),
        name="prepare",
    )(slot_one, place, prolong_one, fine_blocks)
    return [list(outs[offset * chunks : (offset + 1) * chunks]) for offset in range(x_count)]


def whole(kernel, scalars, arrays, out_shapes, name, work=0, scratch=()):
    return pl.pallas_call(
        kernel,
        out_shape=out_shapes,
        in_specs=[pl.BlockSpec(memory_space=pltpu.SMEM)] * len(scalars)
        + [pl.BlockSpec(memory_space=pltpu.VMEM)] * len(arrays),
        out_specs=[pl.BlockSpec(memory_space=pltpu.VMEM)] * len(out_shapes),
        scratch_shapes=scratch,
        compiler_params=pltpu.CompilerParams(vmem_limit_bytes=vmem_limit),
        cost_estimate=pl.CostEstimate(flops=work * 10**9, bytes_accessed=0, transcendentals=0),
        name=name,
    )(*scalars, *arrays)


def combine_kernel(sources, target_ref, *refs):
    arrays, (far_ref, sums_ref) = refs[:sources], refs[sources:]
    rows = arrays[0].shape[0]
    sums_ref[...] = jnp.zeros_like(sums_ref)
    for source in range(sources):

        def one(row, carry, source=source):
            sums_ref[target_ref[source, row]] += arrays[source][row]
            return carry

        lax.fori_loop(0, rows, one, 0, unroll=True)
    far_ref[...] = sums_ref[0 : far_ref.shape[0]]


def finish_kernel(middle_ref, sums_ref, got_ref, *outs):
    half, rows = got_ref.shape[0], outs[-1].shape[0]
    own = len([out for out in outs if out.shape[0] == rows])
    far, near = outs[:-own], outs[-own:]
    width = own * rows
    for d, out in enumerate(far):
        at = (d + 1) * width
        out[...] = sums_ref[half + at : half + at + width] + got_ref[at : at + width]
    for offset, out in enumerate(near):
        at = offset * rows
        total = sums_ref[half + at : half + at + rows] + got_ref[at : at + rows]
        out[...] = jnp.where(middle_ref[0] > 0, total, 0.0)


def settle_kernel(count, *refs):
    near, far, outs = refs[:count], refs[count:-count], refs[-count:]
    rows = outs[0].shape[0]
    for offset, out in enumerate(outs):
        total = near[offset][...]
        for piece in far:
            total = total + piece[offset * rows : (offset + 1) * rows]
        out[...] = total


def second_kernel(x_count, slot_ref, target_ref, *refs):
    parts, outs, sums_ref = refs[:x_count], refs[x_count:-1], refs[-1]
    rows, links, step, _ = parts[0].shape
    share = outs[0].shape[0]
    sums_ref[...] = jnp.zeros_like(sums_ref)

    def one(row, carry):
        target = target_ref[row]
        for link in range(links):
            slot = slot_ref[row, link]
            for offset, part in enumerate(parts):
                sums_ref[target, slot, offset * step : (offset + 1) * step, :] += part[row, link]
        return carry

    lax.fori_loop(0, rows, one, 0, unroll=True)
    for way, out in enumerate(outs):
        out[...] = sums_ref[way * share : (way + 1) * share]


def place_kernel(x_count, place_ref, *refs):
    pieces, out = refs[:-1], refs[-1]
    part = out.shape[2] // x_count
    chunks = len(pieces) // x_count
    for offset in range(x_count):
        start = lax.rem(place_ref[0] + x_count - offset, x_count) * part
        for piece in pieces[offset * chunks : (offset + 1) * chunks]:
            step = piece.shape[2]
            out[:, :, pl.ds(pl.multiple_of(start, 8), step), :] = piece[...]
            start = start + step


def place_one(pieces, place, x_count):
    rows, links, _, size = pieces[0].shape
    return pl.pallas_call(
        functools.partial(place_kernel, x_count),
        out_shape=jax.ShapeDtypeStruct((rows, links, size, size), jnp.float32),
        grid_spec=pltpu.PrefetchScalarGridSpec(
            num_scalar_prefetch=1,
            grid=(rows,),
            in_specs=[
                pl.BlockSpec((1, links, piece.shape[2], size), lambda e, *_: (e, 0, 0, 0))
                for piece in pieces
            ],
            out_specs=pl.BlockSpec((1, links, size, size), lambda e, *_: (e, 0, 0, 0)),
        ),
        compiler_params=pltpu.CompilerParams(vmem_limit_bytes=vmem_limit),
        cost_estimate=pl.CostEstimate(
            flops=0, bytes_accessed=8 * rows * links * size**2, transcendentals=0
        ),
        name="place_one",
    )(place, *pieces)


def last_kernel(x_count, peers, place_ref, prolong_ref, *refs):
    pieces, (out, left_ref, right_ref, sums_ref) = refs[:-4], refs[-4:]
    links, size = out.shape[1], out.shape[2]
    part = size // x_count

    @pl.when(pl.program_id(0) == 0)
    def _():
        load_weights(prolong_ref, left_ref, right_ref)

    done = 0
    for first in range(0, len(pieces), peers):
        total = pieces[first][...]
        for piece in pieces[first + 1 : first + peers]:
            total = total + piece[...]
        step = total.shape[2] // x_count
        for offset in range(x_count):
            start = lax.rem(place_ref[0] + x_count - offset, x_count) * part
            at = pl.multiple_of(start + done, 8)
            sums_ref[:, :, pl.ds(at, step), :] = total[:, :, offset * step : (offset + 1) * step, :]
        done += step
    sums = [sums_ref[row, slot] for row in range(out.shape[0]) for slot in range(links)]
    out[...] = triple(sums, left_ref, right_ref).reshape(out.shape)


def last(pieces, prolong_two, place, x_count, peers):
    rows, links, _, size = pieces[0].shape
    held = max(h for h in range(1, rows_a_step // 2 + 1) if rows % h == 0)
    return pl.pallas_call(
        functools.partial(last_kernel, x_count, peers),
        out_shape=jax.ShapeDtypeStruct((rows, links, size, size), jnp.float32),
        grid_spec=pltpu.PrefetchScalarGridSpec(
            num_scalar_prefetch=1,
            grid=(rows // held,),
            in_specs=[pl.BlockSpec((size, size), lambda e, *_: (0, 0))]
            + [
                pl.BlockSpec((held, links, piece.shape[2], size), lambda e, *_: (e, 0, 0, 0))
                for piece in pieces
            ],
            out_specs=pl.BlockSpec((held, links, size, size), lambda e, *_: (e, 0, 0, 0)),
            scratch_shapes=[
                pltpu.VMEM((2 * size, 2 * size), jnp.bfloat16),
                pltpu.VMEM((2 * size, 2 * size), jnp.bfloat16),
                pltpu.VMEM((held, links, size, size), jnp.float32),
            ],
        ),
        compiler_params=pltpu.CompilerParams(vmem_limit_bytes=vmem_limit),
        cost_estimate=pl.CostEstimate(
            flops=16 * rows * links * size**3,
            bytes_accessed=4 * rows * links * size**2 * (peers + 1),
            transcendentals=0,
        ),
        name="last",
    )(place, prolong_two, *pieces)


def around(initial_guess):
    axes = ("group", "member")
    devices = lax.axis_size(axes)
    before = lax.ppermute(initial_guess, axes, [(i, (i + 1) % devices) for i in range(devices)])
    after = lax.ppermute(initial_guess, axes, [(i, (i - 1) % devices) for i in range(devices)])
    return [before, initial_guess, after]


def sweep(fine_blocks, neighbours, diag_inverse, right_side, initial_guess, window):
    rows = fine_blocks.shape[0]
    axes = ("group", "member")
    devices = lax.axis_size(axes)
    device = lax.axis_index(axes)
    window = jnp.concatenate(window, axis=0)
    position = (neighbours - device * rows + rows) % (rows * devices)
    nearby = window[position]
    product = jnp.sum(fine_blocks * nearby[:, :, None, :], axis=(1, 3))
    defect = right_side - product
    return initial_guess + damping * jnp.sum(diag_inverse * defect[:, None, :], axis=2)


def local(
    fine_blocks,
    neighbours,
    slot_one,
    pair_one,
    prolong_one,
    slot_two,
    pair_two,
    prolong_two,
    diag_inverse,
    right_side,
    initial_guess,
):
    rows, links, size, _ = fine_blocks.shape
    rows_one, rows_two = rows // 2, rows // 4
    members, groups = lax.axis_size("member"), lax.axis_size("group")
    z_count, x_count = grid_of(members)
    half = z_count // 2
    part = size // x_count
    steps = chunk_steps(part)

    member = lax.axis_index("member")
    z, x = member // x_count, member % x_count
    upper = (z >= half).astype(jnp.int32)
    place = jnp.stack([x]).astype(jnp.int32)

    def at(side, d, x_at):
        return (half + d if side else half - 1 - d) * x_count + x_at % x_count

    def hop(array, d_from, d_to, offset):
        pairs = [
            (at(side, d_from, x_at), at(side, d_to, x_at + offset))
            for side in range(2)
            for x_at in range(x_count)
        ]
        return lax.ppermute(array, "member", pairs)

    def hop_x(array, offset):
        pairs = [
            (z_at * x_count + x_at, z_at * x_count + (x_at + offset) % x_count)
            for z_at in range(z_count)
            for x_at in range(x_count)
        ]
        return lax.ppermute(array, "member", pairs)

    routes = [(d, o) for d in range(half) for o in range(x_count)]

    def along(arrays):
        return [array if o == 0 else hop_x(array, o) for o, array in enumerate(arrays)]

    def inward(arrays):
        return arrays + [hop(array, d, 0, 0) for d in range(1, half) for array in arrays]

    tags = jnp.stack(along([pair_one] * x_count))
    slot_one, tags, window = lax.optimization_barrier((slot_one, tags, around(initial_guess)))
    owner_rows = jnp.concatenate([tags] + [hop(tags, d, 0, 0) for d in range(1, half)])
    owner = owner_rows // rows_one % members
    owner_z, owner_x = owner // x_count, owner % x_count
    owner_upper = (owner_z >= half).astype(jnp.int32)
    owner_d = jnp.where(owner_upper > 0, owner_z - half, half - 1 - owner_z)
    near = (owner_upper == upper).astype(jnp.int32)
    target_one = ((near * half + owner_d) * x_count + (owner_x - x + x_count) % x_count) * rows_one
    target_one = (target_one + owner_rows % rows_one).astype(jnp.int32)
    middle = jnp.stack([(z == half - 1) | (z == half)]).astype(jnp.int32)

    way = (pair_two // rows_two // members - lax.axis_index("group") + groups) % groups
    target_two = (way * rows_two + pair_two % rows_two).astype(jnp.int32)

    outgoing = prepare(fine_blocks, slot_one, prolong_one, place, x_count, steps)
    across = [(at(0, 0, x_at), at(1, 0, x_at)) for x_at in range(x_count)]
    across = across + [(b, a) for a, b in across]
    before = [target_one]

    def in_turn(kernel, scalars, arrays, out_shapes, name, **more):
        arrays, before[0] = lax.optimization_barrier((list(arrays), before[0]))
        outs = whole(kernel, scalars, arrays, out_shapes, name, **more)
        before[0] = outs[0]
        return outs

    def rows_of(count, height):
        return jax.ShapeDtypeStruct((count, links, height, size), jnp.float32)

    coming, targets = [], [target_one]
    for chunk in range(len(steps)):
        own = outgoing[0][chunk]
        if chunk > 0:
            ahead = coming[-1]
            tied = (own, ahead[x_count], targets[0]) if chunk == 1 else (own, ahead[x_count])
            own, ahead[x_count], *seen = lax.optimization_barrier(tied)
            targets += seen
        coming.append(inward(along([own] + [ways[chunk] for ways in outgoing[1:]])))
    received = []

    smoothed = []

    def combine(chunk):
        held = coming[chunk]
        if chunk == min(1, len(steps) - 1):
            later, before[0] = lax.optimization_barrier((neighbours, before[0]))
            swept = sweep(fine_blocks, later, diag_inverse, right_side, initial_guess, window)
            held, swept = lax.optimization_barrier((held, swept))
            smoothed.append(swept)
        total = half * x_count * rows_one
        far, kept = in_turn(
            functools.partial(combine_kernel, len(held)),
            [targets[min(chunk, 1)]],
            held,
            [rows_of(total, steps[chunk]), rows_of(2 * total, steps[chunk])],
            "combine",
            work=beside,
        )
        return kept, lax.ppermute(far, "member", across)

    def finish(chunk, sums):
        finished = in_turn(
            finish_kernel,
            [middle],
            sums,
            [rows_of(x_count * rows_one, steps[chunk])] * (half - 1)
            + [rows_of(rows_one, steps[chunk])] * x_count,
            "finish",
        )
        return list(finished[half - 1 :]) + [hop(finished[d - 1], 0, d, 0) for d in range(1, half)]

    def settle(chunk, finished):
        if chunk == 0 and len(steps) > 2:
            ahead = coming[chunk + 2]
            ahead[x_count], finished = lax.optimization_barrier((ahead[x_count], finished))
        return along(
            in_turn(
                functools.partial(settle_kernel, x_count),
                [],
                finished,
                [rows_of(rows_one, steps[chunk])] * x_count,
                "settle",
            )
        )

    def second(chunk, ours):
        received[-groups:], ours = lax.optimization_barrier((received[-groups:], ours))
        height = x_count * steps[chunk]
        shares = in_turn(
            functools.partial(second_kernel, x_count),
            [slot_two, target_two],
            ours,
            [rows_of(rows_two, height)] * groups,
            "second",
            scratch=[pltpu.VMEM((groups * rows_two, links, height, size), jnp.float32)],
        )
        for way, share in enumerate(shares):
            circle = [(g, (g + way) % groups) for g in range(groups)]
            received.append(lax.ppermute(share, "group", circle) if way > 0 else share)
        return ours

    stages, shares = (combine, finish, settle, second), (1.0, 0.5, 0.25)
    turns, rows_in, swapped = [], 0.0, 0.0
    for chunk, step in enumerate(steps):
        rows_in += step
        time = swapped = max(rows_in, swapped) + step + pause
        turns += [(rows_in, 0, chunk), (time, 1, chunk)]
        for stage, share in enumerate(shares[1:], 2):
            time += share * step + pause + (2 if stage == 3 and chunk == len(steps) - 3 else 0)
            turns.append((time, stage, chunk))
    held = [[None] * len(steps) for _ in range(len(stages) + 1)]
    for _, stage, chunk in sorted(turns):
        given = [held[stage][chunk]] if stage > 0 else []
        held[stage + 1][chunk] = stages[stage](chunk, *given)
    parts = held[4]

    coarse_one = place_one(
        [parts[chunk][o] for o in range(x_count) for chunk in range(len(steps))], place, x_count
    )
    coarse_two = last(received, prolong_two, place, x_count, groups)
    return (coarse_one, coarse_two, smoothed[0])


def solution(mesh):
    rows = P(("group", "member"))
    return jax.shard_map(
        local,
        mesh=mesh,
        in_specs=(rows, rows, rows, rows, P(), rows, rows, P(), rows, rows, rows),
        out_specs=(rows, rows, rows),
        check_vma=False,
    )
```

```python
import functools

import jax
import jax.numpy as jnp
from jax import lax
from jax.experimental import pallas as pl
from jax.experimental.pallas import tpu as pltpu
from jax.sharding import PartitionSpec as P

damping = 0.7
rows_a_step = 4
prepare_limit = 48 * 1024 * 1024
vmem_limit = 20 * 1024 * 1024
pause = 3
beside = 6


def grid_of(member_count):
    x_count = max(d for d in range(1, member_count + 1) if member_count % d == 0 and d * d <= member_count)
    return member_count // x_count, x_count


def chunk_steps(part):
    tiles = part // 8
    step = max(tiles // 4, 1)
    ends = [max(step // 2, 1)] * min(2, tiles)
    inner = tiles - sum(ends)
    steps = ends[:1] + [step] * (inner // step) + [inner % step] * (inner % step > 0) + ends[1:]
    return [8 * step for step in steps]


def split(values):
    high = values.astype(jnp.bfloat16)
    low = (values - high.astype(jnp.float32)).astype(jnp.bfloat16)
    return high, low


def load_weights(prolong_ref, left_ref, right_ref):
    prolong = prolong_ref[...]
    size = prolong.shape[0]
    high, low = split(prolong)
    high_t, low_t = split(prolong.T)
    for half in range(2):
        at = pl.ds(half * size, size)
        left_ref[0:size, at] = high_t
        left_ref[size : 2 * size, at] = low_t
        right_ref[at, 0:size] = high
        right_ref[at, size : 2 * size] = low


def triple(blocks, left_ref, right_ref):
    size = blocks[0].shape[0]
    count = len(blocks)
    high, low = split(jnp.concatenate(blocks, axis=1))
    both = jnp.dot(
        left_ref[...], jnp.concatenate([high, low], axis=0), preferred_element_type=jnp.float32
    )
    left = both[:size] + both[size:]
    rows = jnp.concatenate([left[:, s * size : (s + 1) * size] for s in range(count)], axis=0)
    high, low = split(rows)
    both = jnp.dot(
        jnp.concatenate([high, low], axis=1), right_ref[...], preferred_element_type=jnp.float32
    )
    return (both[:, :size] + both[:, size:]).reshape(count, size, size)


def prepare_kernel(x_count, slot_ref, place_ref, prolong_ref, fine_ref, *rest):
    outs, (left_ref, right_ref, sums_ref, done_ref) = rest[:-4], rest[-4:]
    held, links, size, _ = fine_ref.shape
    chunks = len(outs) // x_count
    part = size // x_count

    @pl.when(pl.program_id(0) == 0)
    def _():
        load_weights(prolong_ref, left_ref, right_ref)

    sums_ref[...] = jnp.zeros_like(sums_ref)
    for row in range(held):
        for link in range(links):
            slot = slot_ref[pl.program_id(0) * held + row, link]
            sums_ref[row, slot] += fine_ref[row, link]
    sums = [sums_ref[row, slot] for row in range(held) for slot in range(links)]
    done_ref[...] = triple(sums, left_ref, right_ref).reshape(done_ref.shape)
    for offset in range(x_count):
        start = lax.rem(place_ref[0] + offset, x_count) * part
        for out in outs[offset * chunks : (offset + 1) * chunks]:
            step = out.shape[2]
            out[...] = done_ref[:, :, pl.ds(pl.multiple_of(start, 8), step), :]
            start = start + step


def prepare(fine_blocks, slot_one, prolong_one, place, x_count, steps):
    rows, links, size, _ = fine_blocks.shape
    chunks = len(steps)
    held = max(h for h in range(1, rows_a_step + 1) if rows % h == 0)
    outs = pl.pallas_call(
        functools.partial(prepare_kernel, x_count),
        out_shape=[
            jax.ShapeDtypeStruct((rows, links, step, size), jnp.float32)
            if chunk < 2
            else pltpu.HBM((rows, links, step, size), jnp.float32)
            for chunk, step in enumerate(steps)
        ]
        * x_count,
        grid_spec=pltpu.PrefetchScalarGridSpec(
            num_scalar_prefetch=2,
            grid=(rows // held,),
            in_specs=[
                pl.BlockSpec((size, size), lambda e, *_: (0, 0)),
                pl.BlockSpec((held, links, size, size), lambda e, *_: (e, 0, 0, 0)),
            ],
            out_specs=[
                pl.BlockSpec((held, links, step, size), lambda e, *_: (e, 0, 0, 0)) for step in steps
            ]
            * x_count,
            scratch_shapes=[
                pltpu.VMEM((2 * size, 2 * size), jnp.bfloat16),
                pltpu.VMEM((2 * size, 2 * size), jnp.bfloat16),
                pltpu.VMEM((held, links, size, size), jnp.float32),
                pltpu.VMEM((held, links, size, size), jnp.float32),
            ],
        ),
        compiler_params=pltpu.CompilerParams(vmem_limit_bytes=prepare_limit),
        cost_estimate=pl.CostEstimate(
            flops=16 * rows * links * size**3,
            bytes_accessed=8 * rows * links * size**2,
            transcendentals=0,
        ),
        name="prepare",
    )(slot_one, place, prolong_one, fine_blocks)
    return [list(outs[offset * chunks : (offset + 1) * chunks]) for offset in range(x_count)]


def whole(kernel, scalars, arrays, out_shapes, name, work=0, scratch=()):
    return pl.pallas_call(
        kernel,
        out_shape=out_shapes,
        in_specs=[pl.BlockSpec(memory_space=pltpu.SMEM)] * len(scalars)
        + [pl.BlockSpec(memory_space=pltpu.VMEM)] * len(arrays),
        out_specs=[pl.BlockSpec(memory_space=pltpu.VMEM)] * len(out_shapes),
        scratch_shapes=scratch,
        compiler_params=pltpu.CompilerParams(vmem_limit_bytes=vmem_limit),
        cost_estimate=pl.CostEstimate(flops=work * 10**9, bytes_accessed=0, transcendentals=0),
        name=name,
    )(*scalars, *arrays)


def combine_kernel(sources, target_ref, *refs):
    arrays, (far_ref, sums_ref) = refs[:sources], refs[sources:]
    rows = arrays[0].shape[0]
    sums_ref[...] = jnp.zeros_like(sums_ref)
    for source in range(sources):

        def one(row, carry, source=source):
            sums_ref[target_ref[source, row]] += arrays[source][row]
            return carry

        lax.fori_loop(0, rows, one, 0, unroll=True)
    far_ref[...] = sums_ref[0 : far_ref.shape[0]]


def finish_kernel(middle_ref, sums_ref, got_ref, *outs):
    half, rows = got_ref.shape[0], outs[-1].shape[0]
    own = len([out for out in outs if out.shape[0] == rows])
    far, near = outs[:-own], outs[-own:]
    width = own * rows
    for d, out in enumerate(far):
        at = (d + 1) * width
        out[...] = sums_ref[half + at : half + at + width] + got_ref[at : at + width]
    for offset, out in enumerate(near):
        at = offset * rows
        total = sums_ref[half + at : half + at + rows] + got_ref[at : at + rows]
        out[...] = jnp.where(middle_ref[0] > 0, total, 0.0)


def settle_kernel(count, *refs):
    near, far, outs = refs[:count], refs[count:-count], refs[-count:]
    rows = outs[0].shape[0]
    for offset, out in enumerate(outs):
        total = near[offset][...]
        for piece in far:
            total = total + piece[offset * rows : (offset + 1) * rows]
        out[...] = total


def second_kernel(x_count, slot_ref, target_ref, *refs):
    parts, outs, sums_ref = refs[:x_count], refs[x_count:-1], refs[-1]
    rows, links, step, _ = parts[0].shape
    share = outs[0].shape[0]
    sums_ref[...] = jnp.zeros_like(sums_ref)

    def one(row, carry):
        target = target_ref[row]
        for link in range(links):
            slot = slot_ref[row, link]
            for offset, part in enumerate(parts):
                sums_ref[target, slot, offset * step : (offset + 1) * step, :] += part[row, link]
        return carry

    lax.fori_loop(0, rows, one, 0, unroll=True)
    for way, out in enumerate(outs):
        out[...] = sums_ref[way * share : (way + 1) * share]


def place_kernel(x_count, place_ref, *refs):
    pieces, out = refs[:-1], refs[-1]
    part = out.shape[2] // x_count
    chunks = len(pieces) // x_count
    for offset in range(x_count):
        start = lax.rem(place_ref[0] + x_count - offset, x_count) * part
        for piece in pieces[offset * chunks : (offset + 1) * chunks]:
            step = piece.shape[2]
            out[:, :, pl.ds(pl.multiple_of(start, 8), step), :] = piece[...]
            start = start + step


def place_one(pieces, place, x_count):
    rows, links, _, size = pieces[0].shape
    return pl.pallas_call(
        functools.partial(place_kernel, x_count),
        out_shape=jax.ShapeDtypeStruct((rows, links, size, size), jnp.float32),
        grid_spec=pltpu.PrefetchScalarGridSpec(
            num_scalar_prefetch=1,
            grid=(rows,),
            in_specs=[
                pl.BlockSpec((1, links, piece.shape[2], size), lambda e, *_: (e, 0, 0, 0))
                for piece in pieces
            ],
            out_specs=pl.BlockSpec((1, links, size, size), lambda e, *_: (e, 0, 0, 0)),
        ),
        compiler_params=pltpu.CompilerParams(vmem_limit_bytes=vmem_limit),
        cost_estimate=pl.CostEstimate(
            flops=0, bytes_accessed=8 * rows * links * size**2, transcendentals=0
        ),
        name="place_one",
    )(place, *pieces)


def last_kernel(x_count, peers, place_ref, prolong_ref, *refs):
    pieces, (out, left_ref, right_ref, sums_ref) = refs[:-4], refs[-4:]
    links, size = out.shape[1], out.shape[2]
    part = size // x_count

    @pl.when(pl.program_id(0) == 0)
    def _():
        load_weights(prolong_ref, left_ref, right_ref)

    done = 0
    for first in range(0, len(pieces), peers):
        total = pieces[first][...]
        for piece in pieces[first + 1 : first + peers]:
            total = total + piece[...]
        step = total.shape[2] // x_count
        for offset in range(x_count):
            start = lax.rem(place_ref[0] + x_count - offset, x_count) * part
            at = pl.multiple_of(start + done, 8)
            sums_ref[:, :, pl.ds(at, step), :] = total[:, :, offset * step : (offset + 1) * step, :]
        done += step
    sums = [sums_ref[row, slot] for row in range(out.shape[0]) for slot in range(links)]
    out[...] = triple(sums, left_ref, right_ref).reshape(out.shape)


def last(pieces, prolong_two, place, x_count, peers):
    rows, links, _, size = pieces[0].shape
    held = max(h for h in range(1, rows_a_step // 2 + 1) if rows % h == 0)
    return pl.pallas_call(
        functools.partial(last_kernel, x_count, peers),
        out_shape=jax.ShapeDtypeStruct((rows, links, size, size), jnp.float32),
        grid_spec=pltpu.PrefetchScalarGridSpec(
            num_scalar_prefetch=1,
            grid=(rows // held,),
            in_specs=[pl.BlockSpec((size, size), lambda e, *_: (0, 0))]
            + [
                pl.BlockSpec((held, links, piece.shape[2], size), lambda e, *_: (e, 0, 0, 0))
                for piece in pieces
            ],
            out_specs=pl.BlockSpec((held, links, size, size), lambda e, *_: (e, 0, 0, 0)),
            scratch_shapes=[
                pltpu.VMEM((2 * size, 2 * size), jnp.bfloat16),
                pltpu.VMEM((2 * size, 2 * size), jnp.bfloat16),
                pltpu.VMEM((held, links, size, size), jnp.float32),
            ],
        ),
        compiler_params=pltpu.CompilerParams(vmem_limit_bytes=vmem_limit),
        cost_estimate=pl.CostEstimate(
            flops=16 * rows * links * size**3,
            bytes_accessed=4 * rows * links * size**2 * (peers + 1),
            transcendentals=0,
        ),
        name="last",
    )(place, prolong_two, *pieces)


def around(initial_guess):
    axes = ("group", "member")
    devices = lax.axis_size(axes)
    before = lax.ppermute(initial_guess, axes, [(i, (i + 1) % devices) for i in range(devices)])
    after = lax.ppermute(initial_guess, axes, [(i, (i - 1) % devices) for i in range(devices)])
    return [before, initial_guess, after]


def sweep(fine_blocks, neighbours, diag_inverse, right_side, initial_guess, window):
    rows = fine_blocks.shape[0]
    axes = ("group", "member")
    devices = lax.axis_size(axes)
    device = lax.axis_index(axes)
    window = jnp.concatenate(window, axis=0)
    position = (neighbours - device * rows + rows) % (rows * devices)
    nearby = window[position]
    product = jnp.sum(fine_blocks * nearby[:, :, None, :], axis=(1, 3))
    defect = right_side - product
    return initial_guess + damping * jnp.sum(diag_inverse * defect[:, None, :], axis=2)


def local(
    fine_blocks,
    neighbours,
    slot_one,
    pair_one,
    prolong_one,
    slot_two,
    pair_two,
    prolong_two,
    diag_inverse,
    right_side,
    initial_guess,
):
    rows, links, size, _ = fine_blocks.shape
    rows_one, rows_two = rows // 2, rows // 4
    members, groups = lax.axis_size("member"), lax.axis_size("group")
    z_count, x_count = grid_of(members)
    half = z_count // 2
    part = size // x_count
    steps = chunk_steps(part)

    member = lax.axis_index("member")
    z, x = member // x_count, member % x_count
    upper = (z >= half).astype(jnp.int32)
    place = jnp.stack([x]).astype(jnp.int32)

    def at(side, d, x_at):
        return (half + d if side else half - 1 - d) * x_count + x_at % x_count

    def hop(array, d_from, d_to, offset):
        pairs = [
            (at(side, d_from, x_at), at(side, d_to, x_at + offset))
            for side in range(2)
            for x_at in range(x_count)
        ]
        return lax.ppermute(array, "member", pairs)

    def hop_x(array, offset):
        pairs = [
            (z_at * x_count + x_at, z_at * x_count + (x_at + offset) % x_count)
            for z_at in range(z_count)
            for x_at in range(x_count)
        ]
        return lax.ppermute(array, "member", pairs)

    routes = [(d, o) for d in range(half) for o in range(x_count)]

    def along(arrays):
        return [array if o == 0 else hop_x(array, o) for o, array in enumerate(arrays)]

    def inward(arrays):
        return arrays + [hop(array, d, 0, 0) for d in range(1, half) for array in arrays]

    tags = jnp.stack(along([pair_one] * x_count))
    slot_one, tags, window = lax.optimization_barrier((slot_one, tags, around(initial_guess)))
    owner_rows = jnp.concatenate([tags] + [hop(tags, d, 0, 0) for d in range(1, half)])
    owner = owner_rows // rows_one % members
    owner_z, owner_x = owner // x_count, owner % x_count
    owner_upper = (owner_z >= half).astype(jnp.int32)
    owner_d = jnp.where(owner_upper > 0, owner_z - half, half - 1 - owner_z)
    near = (owner_upper == upper).astype(jnp.int32)
    target_one = ((near * half + owner_d) * x_count + (owner_x - x + x_count) % x_count) * rows_one
    target_one = (target_one + owner_rows % rows_one).astype(jnp.int32)
    middle = jnp.stack([(z == half - 1) | (z == half)]).astype(jnp.int32)

    way = (pair_two // rows_two // members - lax.axis_index("group") + groups) % groups
    target_two = (way * rows_two + pair_two % rows_two).astype(jnp.int32)

    outgoing = prepare(fine_blocks, slot_one, prolong_one, place, x_count, steps)
    across = [(at(0, 0, x_at), at(1, 0, x_at)) for x_at in range(x_count)]
    across = across + [(b, a) for a, b in across]
    before = [target_one]

    def in_turn(kernel, scalars, arrays, out_shapes, name, **more):
        arrays, before[0] = lax.optimization_barrier((list(arrays), before[0]))
        outs = whole(kernel, scalars, arrays, out_shapes, name, **more)
        before[0] = outs[0]
        return outs

    def rows_of(count, height):
        return jax.ShapeDtypeStruct((count, links, height, size), jnp.float32)

    coming, targets = [], [target_one]
    for chunk in range(len(steps)):
        own = outgoing[0][chunk]
        if chunk > 0:
            ahead = coming[-1]
            tied = (own, ahead[x_count], targets[0]) if chunk == 1 else (own, ahead[x_count])
            own, ahead[x_count], *seen = lax.optimization_barrier(tied)
            targets += seen
        coming.append(inward(along([own] + [ways[chunk] for ways in outgoing[1:]])))
    received = []

    smoothed = []

    def combine(chunk):
        held = coming[chunk]
        if chunk == min(1, len(steps) - 1):
            later, before[0] = lax.optimization_barrier((neighbours, before[0]))
            swept = sweep(fine_blocks, later, diag_inverse, right_side, initial_guess, window)
            held, swept = lax.optimization_barrier((held, swept))
            smoothed.append(swept)
        total = half * x_count * rows_one
        far, kept = in_turn(
            functools.partial(combine_kernel, len(held)),
            [targets[min(chunk, 1)]],
            held,
            [rows_of(total, steps[chunk]), rows_of(2 * total, steps[chunk])],
            "combine",
            work=beside,
        )
        return kept, lax.ppermute(far, "member", across)

    def finish(chunk, sums):
        finished = in_turn(
            finish_kernel,
            [middle],
            sums,
            [rows_of(x_count * rows_one, steps[chunk])] * (half - 1)
            + [rows_of(rows_one, steps[chunk])] * x_count,
            "finish",
        )
        return list(finished[half - 1 :]) + [hop(finished[d - 1], 0, d, 0) for d in range(1, half)]

    def settle(chunk, finished):
        if chunk == 0 and len(steps) > 2:
            ahead = coming[chunk + 2]
            ahead[x_count], finished = lax.optimization_barrier((ahead[x_count], finished))
        return along(
            in_turn(
                functools.partial(settle_kernel, x_count),
                [],
                finished,
                [rows_of(rows_one, steps[chunk])] * x_count,
                "settle",
            )
        )

    def second(chunk, ours):
        received[-groups:], ours = lax.optimization_barrier((received[-groups:], ours))
        height = x_count * steps[chunk]
        shares = in_turn(
            functools.partial(second_kernel, x_count),
            [slot_two, target_two],
            ours,
            [rows_of(rows_two, height)] * groups,
            "second",
            scratch=[pltpu.VMEM((groups * rows_two, links, height, size), jnp.float32)],
        )
        for way, share in enumerate(shares):
            circle = [(g, (g + way) % groups) for g in range(groups)]
            received.append(lax.ppermute(share, "group", circle) if way > 0 else share)
        return ours

    stages, shares = (combine, finish, settle, second), (1.0, 0.5, 0.25)
    turns, rows_in, swapped = [], 0.0, 0.0
    for chunk, step in enumerate(steps):
        rows_in += step
        time = swapped = max(rows_in, swapped) + step + pause
        turns += [(rows_in, 0, chunk), (time, 1, chunk)]
        for stage, share in enumerate(shares[1:], 2):
            time += share * step + pause
            turns.append((time, stage, chunk))
    held = [[None] * len(steps) for _ in range(len(stages) + 1)]
    for _, stage, chunk in sorted(turns):
        given = [held[stage][chunk]] if stage > 0 else []
        held[stage + 1][chunk] = stages[stage](chunk, *given)
    parts = held[4]

    coarse_one = place_one(
        [parts[chunk][o] for o in range(x_count) for chunk in range(len(steps))], place, x_count
    )
    coarse_two = last(received, prolong_two, place, x_count, groups)
    return (coarse_one, coarse_two, smoothed[0])


def solution(mesh):
    rows = P(("group", "member"))
    return jax.shard_map(
        local,
        mesh=mesh,
        in_specs=(rows, rows, rows, rows, P(), rows, rows, P(), rows, rows, rows),
        out_specs=(rows, rows, rows),
        check_vma=False,
    )
```
